32 devices in a mesh: dp: 16 (over z, y, core), tensor: 2 (over x).
Axes of the slice: x: 2, y: 2, z: 4, core: 2. Of those that a mesh axis runs over, the one named last changes fastest.
Arguments:
- tokens: bfloat16 [4096, 2048], P(('dp', 'tensor')), may hold values from -6 to 6
- seq_lens: int32 [16, 4], P('dp'), may hold values from 1 to 253, as said below
- norm_gains: bfloat16 [2, 2048], replicated, may hold values from 0.099609375 to 1.8984375
- w_query: bfloat16 [2048, 2048], P('dp', 'tensor'), may hold values from -0.125 to 0.125
- key_weight: bfloat16 [2048, 512], P('dp', 'tensor'), may hold values from -0.125 to 0.125
- value_weight: bfloat16 [2048, 512], P('dp', 'tensor'), may hold values from -0.125 to 0.125
- w_out: bfloat16 [2048, 2048], P('dp', 'tensor'), may hold values from -0.75 to 0.75
- w_gate: bfloat16 [2048, 8192], P('dp', 'tensor'), may hold values from -0.125 to 0.125
- w_up: bfloat16 [2048, 8192], P('dp', 'tensor'), may hold values from -0.125 to 0.125
- w_down: bfloat16 [2048, 8192], P('dp', 'tensor'), may hold values from -0.0625 to 0.0625
- cotangent: bfloat16 [4096, 2048], P(('dp', 'tensor')), may hold values from -6 to 6
Outputs:
- mixed: bfloat16 [4096, 2048], P(('dp', 'tensor'))
- grad_tokens: bfloat16 [4096, 2048], P(('dp', 'tensor'))
- grad_gains: float32 [2, 2048], replicated
- grad_query: float32 [2048, 2048], P('dp', 'tensor')
- grad_key: float32 [2048, 512], P('dp', 'tensor')
- grad_value: float32 [2048, 512], P('dp', 'tensor')
- grad_out: float32 [2048, 2048], P('dp', 'tensor')
- grad_gate: float32 [2048, 8192], P('dp', 'tensor')
- grad_up: float32 [2048, 8192], P('dp', 'tensor')
- grad_down: float32 [2048, 8192], P('dp', 'tensor')
The draws below stay inside these ranges and needn't reach their ends.
Inputs may be any that keep to these rules, and one draw needn't show every extreme that they name: `seq_lens`: row b lists the lengths of 4 sequences packed from the first row of dp index b's 256 rows; the rows after them are unused. A row's lengths add up to 130 or more and to 256 at most; in every draw some row adds up to 256, and there its first sequence has the largest length. Rows 127 and 128 of a dp index always lie in one sequence.
All inputs are finite; a program needn't handle non-finite values.
Results may differ from the reference program's by a relative error of at most 0.014.
Values may be sent and summed in bfloat16 or wider, within the bound.
No kernel may reach another device: no remote copies, remote signals or barrier semaphores. Data moves between devices by JAX's collectives and lax.ppermute only.
A program may use at most 448 MiB of HBM per device.

```python
import math
import jax
import jax.numpy as jnp
from jax import lax

MODEL_WIDTH = 2048
QUERY_HEADS = 32
KEY_VALUE_HEADS = 8
HEAD_WIDTH = 64
FF = 8192
TOKEN_ROWS_PART = 256
SLOTS = 4
TOKENS = 4096
N_DP = 16


def draw_seq_lens(key, part):
    key = jax.random.fold_in(key, 7)
    key_total, key_full, key_cuts = jax.random.split(key, 3)
    halfway = TOKEN_ROWS_PART // 2
    totals = jax.random.randint(key_total, (N_DP,), halfway + 2, TOKEN_ROWS_PART + 1).astype(jnp.int32)
    full_row = jax.random.randint(key_full, (), 0, N_DP)
    row_ids = jnp.arange(N_DP, dtype=jnp.int32)
    totals = jnp.where(row_ids == full_row, TOKEN_ROWS_PART, totals).astype(jnp.int32)
    places = jnp.arange(1, TOKEN_ROWS_PART, dtype=jnp.int32)
    ranked = jax.random.randint(key_cuts, (N_DP, TOKEN_ROWS_PART - 1), 0, 4096).astype(jnp.int32) * TOKEN_ROWS_PART + places[None, :]
    allowed = (places[None, :] < totals[:, None]) & (places[None, :] != halfway)
    ranked = jnp.where(allowed, ranked, -1)
    picked = jnp.sort(lax.top_k(ranked, SLOTS - 1)[0] % TOKEN_ROWS_PART, 1)
    forced = TOKEN_ROWS_PART - SLOTS + 1 + jnp.arange(SLOTS - 1, dtype=jnp.int32)
    boundary = jnp.where((row_ids == full_row)[:, None], forced[None, :], picked)
    borders = jnp.concatenate([jnp.zeros((N_DP, 1), jnp.int32), boundary.astype(jnp.int32), totals[:, None]], 1)
    return (borders[:, 1:] - borders[:, :-1]).astype(jnp.int32)


def raised(entries, rng, source, target, parts, factor):
    owner, partner = [(jnp.arange(entries.shape[dim]) // (entries.shape[dim] // parts)).reshape([-1 if axis == dim else 1 for axis in range(entries.ndim)]) for dim in (source, target)]
    chosen = jax.random.permutation(rng, parts)[partner]
    strong = (owner == chosen) | (owner == (partner + parts // 2) % parts)
    return jnp.where(strong, factor * entries, entries)


def levels(rng, shape, cuts, least, top_value):
    factor_of, own = 1.0, jax.random.fold_in(rng, 6)
    for axis_at, shards_of in cuts:
        steps = jnp.exp(jax.random.uniform(jax.random.fold_in(own, axis_at), (shards_of,), jnp.float32, least / len(cuts), top_value / len(cuts)))
        factor_of = factor_of * jnp.repeat(steps, shape[axis_at] // shards_of).reshape([-1 if axis == axis_at else 1 for axis in range(len(shape))])
    return factor_of


def gaussian(rng, extent, width, most, cuts=(), held_as=jnp.bfloat16):
    values = jax.random.normal(rng, extent, jnp.float32) * width
    if len(cuts) > 0:
        values = levels(rng, extent, cuts, -0.22, 0.18) * values
    return jnp.clip(values, min=-most, max=most).astype(held_as)


def noise_with(key, extent, width, reach, cuts, heavy, kind=jnp.bfloat16):
    array = width * jax.random.normal(key, extent, jnp.float32)
    if cuts:
        array = array * levels(key, extent, cuts, -0.22, 0.18)
    return jnp.clip(raised(array, jax.random.fold_in(key, 3), *heavy), -reach, reach).astype(kind)


def setup_inputs(seed: int = 0) -> dict:
    keys = jax.random.split(jax.random.key(seed), 12)
    tokens = gaussian(keys[0], (TOKENS, MODEL_WIDTH), 1.0, 6.0, ((0, 32),))
    seq_lens = draw_seq_lens(jax.random.fold_in(keys[11], 71), 0)
    norm_gains = jnp.clip(1.0 + 0.18 * jax.random.normal(keys[2], (2, MODEL_WIDTH), jnp.float32), 0.099609375, 1.8984375).astype(jnp.bfloat16)
    w_query = gaussian(keys[3], (MODEL_WIDTH, QUERY_HEADS * HEAD_WIDTH), MODEL_WIDTH ** -0.5, 0.125, ((0, 16), (1, 2)))
    key_weight = gaussian(keys[4], (MODEL_WIDTH, KEY_VALUE_HEADS * HEAD_WIDTH), MODEL_WIDTH ** -0.5, 0.125, ((0, 16), (1, 2)))
    value_weight = gaussian(keys[5], (MODEL_WIDTH, KEY_VALUE_HEADS * HEAD_WIDTH), MODEL_WIDTH ** -0.5, 0.125, ((0, 16), (1, 2)))
    w_out = gaussian(keys[6], (MODEL_WIDTH, QUERY_HEADS * HEAD_WIDTH), HEAD_WIDTH ** -0.5, 0.75, ((0, 16), (1, 2)))
    w_gate = gaussian(keys[7], (MODEL_WIDTH, FF), MODEL_WIDTH ** -0.5, 0.125, ((0, 16), (1, 2)))
    w_up = gaussian(keys[8], (MODEL_WIDTH, FF), MODEL_WIDTH ** -0.5, 0.125, ((0, 16), (1, 2)))
    w_down = gaussian(keys[9], (MODEL_WIDTH, FF), FF ** -0.5, 0.0625, ((0, 16), (1, 2)))
    cotangent = noise_with(keys[10], (TOKENS, MODEL_WIDTH), 1.0, 6.0, ((0, 32),), (0, 1, 32, 2.75))
    return dict(tokens=tokens, seq_lens=seq_lens, norm_gains=norm_gains, w_query=w_query, key_weight=key_weight, value_weight=value_weight, w_out=w_out, w_gate=w_gate, w_up=w_up, w_down=w_down, cotangent=cotangent)


EPSILON = 1e-05
MASKED = -1e+30
PRECISE = lax.Precision.HIGHEST

@jax.custom_vjp
def lowered_state(v):
    return lax.optimization_barrier(v.astype(jnp.bfloat16)).astype(jnp.float32)

@jax.custom_vjp
def lowered_gradient(v):
    return v

def low_keep(v):
    return (lowered_state(v), None)

def low_pass(kept, grad):
    return (grad,)

def back_keep(v):
    return (v, None)

def back_low(kept, grad):
    return (lowered_state(grad),)
lowered_state.defvjp(low_keep, low_pass)
lowered_gradient.defvjp(back_keep, back_low)

def matrix_product(left_side, right_side):
    return jnp.dot(left_side, right_side, precision=PRECISE)

def layout(lengths, row_count):
    lengths = lengths.astype(jnp.int32)
    finish = jnp.cumsum(lengths).astype(jnp.int32)
    starts = jnp.concatenate([finish - lengths, finish[-1:]])
    row_ids = jnp.arange(row_count, dtype=jnp.int32)
    segment = lax.optimization_barrier(jnp.sum((row_ids[:, None] >= finish[None, :]).astype(jnp.int32), 1))
    chosen_slot = segment[:, None] == jnp.arange(starts.shape[0], dtype=jnp.int32)[None, :]
    first_row = lax.optimization_barrier(jnp.sum(jnp.where(chosen_slot, starts[None, :], 0), 1)).astype(jnp.int32)
    position = row_ids - first_row
    in_use = (segment < lengths.shape[0]).astype(jnp.float32)
    return (row_ids, segment, position, in_use)

def rope_tables(position, head_size):
    halfway = head_size // 2
    ladder = jnp.arange(halfway, dtype=jnp.float32)
    inverse = 1.0 / 500000.0 ** (ladder * 2.0 / head_size)
    wavelength = 2.0 * math.pi / inverse
    smooth = (8192.0 / wavelength - 1.0) / 3.0
    blended = (1.0 - smooth) * inverse / 32.0 + smooth * inverse
    scaled = jnp.where(wavelength > 8192.0, inverse / 32.0, jnp.where(wavelength < 2048.0, inverse, blended))
    angles = position.astype(jnp.float32)[:, None] * scaled[None, :]
    cosine_lookup = jnp.cos(angles)
    sine_lookup = jnp.sin(angles)
    return (jnp.concatenate([cosine_lookup, cosine_lookup], 1), jnp.concatenate([sine_lookup, sine_lookup], 1))

def apply_rotation(heads, cosine_lookup, sine_lookup):
    halfway = heads.shape[-1] // 2
    turned = jnp.concatenate([-heads[..., halfway:], heads[..., :halfway]], -1)
    return heads * cosine_lookup[:, None, :] + turned * sine_lookup[:, None, :]

def block(params, inputs, lengths):
    gain_rows, query_w, key_matrix, value_matrix, out_w, gate_w, up_w, down_w = params
    row_ids, segment, position, in_use = layout(lengths, TOKEN_ROWS_PART)
    cosine_lookup, sine_lookup = rope_tables(position, HEAD_WIDTH)
    allowed = (segment[:, None] == segment[None, :]) & (row_ids[None, :] <= row_ids[:, None])
    scale_one = lax.rsqrt(lax.optimization_barrier(jnp.mean(inputs * inputs, 1, keepdims=True)) + EPSILON)
    first_normalized = lowered_state(inputs * scale_one * gain_rows[0])
    query_rows = lowered_gradient(matrix_product(first_normalized, query_w)).reshape(TOKEN_ROWS_PART, QUERY_HEADS, HEAD_WIDTH)
    key_projected = lowered_gradient(matrix_product(first_normalized, key_matrix)).reshape(TOKEN_ROWS_PART, KEY_VALUE_HEADS, HEAD_WIDTH)
    value_rows = lowered_state(lowered_gradient(matrix_product(first_normalized, value_matrix))).reshape(TOKEN_ROWS_PART, KEY_VALUE_HEADS, HEAD_WIDTH)
    rotated_query = lowered_state(apply_rotation(query_rows, cosine_lookup, sine_lookup)).reshape(TOKEN_ROWS_PART, KEY_VALUE_HEADS, QUERY_HEADS // KEY_VALUE_HEADS, HEAD_WIDTH)
    key_rot = lowered_state(apply_rotation(key_projected, cosine_lookup, sine_lookup))
    scores = jnp.einsum('qgjd,kgd->gjqk', rotated_query, key_rot, precision=PRECISE) * HEAD_WIDTH ** (-0.5)
    scores = lowered_gradient(jnp.where(allowed[None, None], scores, MASKED))
    largest = lax.optimization_barrier(jnp.max(scores, 3, keepdims=True))
    exponent = jnp.exp(scores - largest)
    softmax_weights = exponent / lax.optimization_barrier(jnp.sum(exponent, 3, keepdims=True))
    attended = jnp.einsum('gjqk,kgd->qgjd', lowered_state(softmax_weights), value_rows, precision=PRECISE)
    attended = lowered_state(lowered_gradient(attended.reshape(TOKEN_ROWS_PART, QUERY_HEADS * HEAD_WIDTH)))
    state = inputs + lowered_gradient(matrix_product(attended, out_w.T))
    scale_two = lax.rsqrt(lax.optimization_barrier(jnp.mean(state * state, 1, keepdims=True)) + EPSILON)
    normed_two = lowered_state(state * scale_two * gain_rows[1])
    gate = lowered_gradient(matrix_product(normed_two, gate_w))
    up_proj = lowered_gradient(matrix_product(normed_two, up_w))
    hidden = lowered_state(jax.nn.silu(gate) * up_proj)
    result = state + lowered_gradient(matrix_product(hidden, down_w.T))
    return result * in_use[:, None]

def reference(tokens, seq_lens, norm_gains, w_query, key_weight, value_weight, w_out, w_gate, w_up, w_down, cotangent):
    params = tuple((weight.astype(jnp.float32) for weight in (norm_gains, w_query, key_weight, value_weight, w_out, w_gate, w_up, w_down)))
    inputs = tokens.astype(jnp.float32).reshape(N_DP, TOKEN_ROWS_PART, MODEL_WIDTH)

    def whole(params_in, inputs_in):

        def scan_step(carried, pieces):
            return (carried, jax.checkpoint(block)(params_in, pieces[0], pieces[1]))
        carried_out, outputs = lax.scan(scan_step, jnp.zeros((), jnp.float32), (inputs_in, seq_lens))
        return outputs
    outputs, pullback = jax.vjp(whole, params, inputs)
    param_grads, input_grads = pullback(cotangent.astype(jnp.float32).reshape(N_DP, TOKEN_ROWS_PART, MODEL_WIDTH))
    return (outputs.reshape(TOKENS, MODEL_WIDTH).astype(jnp.bfloat16), input_grads.reshape(TOKENS, MODEL_WIDTH).astype(jnp.bfloat16), param_grads[0], param_grads[1], param_grads[2], param_grads[3], param_grads[4], param_grads[5], param_grads[6], param_grads[7])
```

```python
import math

import jax
import jax.numpy as jnp
from jax import lax
from jax.sharding import PartitionSpec as P

HEAD_WIDTH = 64
EPSILON = 1e-05
MASKED = -1e30
CORES = 2
PLANES = 4


def matrix_product(left_side, right_side):
    return jnp.dot(left_side, right_side, preferred_element_type=jnp.float32)


def matmul_nt(left_side, right_side):
    return lax.dot_general(
        left_side, right_side, (((1,), (1,)), ((), ())), preferred_element_type=jnp.float32
    )


def matmul_tn(left_side, right_side):
    return lax.dot_general(
        left_side, right_side, (((0,), (0,)), ((), ())), preferred_element_type=jnp.float32
    )


def after(value, *earlier):
    return lax.optimization_barrier((value, *earlier))[0]


def layout(lengths, row_count):
    finish = jnp.cumsum(lengths)
    starts = jnp.concatenate([finish - lengths, finish[-1:]])
    row_ids = jnp.arange(row_count, dtype=jnp.int32)
    segment = jnp.sum((row_ids[:, None] >= finish[None, :]).astype(jnp.int32), 1)
    chosen_slot = segment[:, None] == jnp.arange(starts.shape[0], dtype=jnp.int32)[None, :]
    first_row = jnp.sum(jnp.where(chosen_slot, starts[None, :], 0), 1)
    position = row_ids - first_row
    in_use = (segment < lengths.shape[0]).astype(jnp.float32)
    return (row_ids, segment, position, in_use)


def rope_tables(position, head_size):
    halfway = head_size // 2
    ladder = jnp.arange(halfway, dtype=jnp.float32)
    inverse = 1.0 / 500000.0 ** (ladder * 2.0 / head_size)
    wavelength = 2.0 * math.pi / inverse
    smooth = (8192.0 / wavelength - 1.0) / 3.0
    blended = (1.0 - smooth) * inverse / 32.0 + smooth * inverse
    scaled = jnp.where(
        wavelength > 8192.0, inverse / 32.0, jnp.where(wavelength < 2048.0, inverse, blended)
    )
    angles = position.astype(jnp.float32)[:, None] * scaled[None, :]
    cosine_lookup = jnp.cos(angles)
    sine_lookup = jnp.sin(angles)
    return (
        jnp.concatenate([cosine_lookup, cosine_lookup], 1),
        jnp.concatenate([sine_lookup, sine_lookup], 1),
    )


def apply_rotation(heads, cosine_lookup, sine_lookup):
    halfway = heads.shape[-1] // 2
    turned = jnp.concatenate([-heads[..., halfway:], heads[..., :halfway]], -1)
    return heads * cosine_lookup[:, None, :] + turned * sine_lookup[:, None, :]


def unrotate(grads, cosine_lookup, sine_lookup):
    halfway = grads.shape[-1] // 2
    scaled = grads * sine_lookup[:, None, :]
    return grads * cosine_lookup[:, None, :] + jnp.concatenate(
        [scaled[..., halfway:], -scaled[..., :halfway]], -1
    )


def group_scores(rotated_query, key_rot, group_index, allowed, scaling):
    per_group = rotated_query.shape[1] // key_rot.shape[1]
    chosen = rotated_query[:, group_index * per_group : (group_index + 1) * per_group, :]
    scores = (
        jnp.einsum(
            "qhd,kd->hqk", chosen, key_rot[:, group_index, :], preferred_element_type=jnp.float32
        )
        * scaling
    )
    return (chosen, jnp.where(allowed[None], scores, MASKED))


def attend(rotated_query, key_rot, value_low, allowed, scaling):
    outputs = []
    logsums = []
    for group_index in range(key_rot.shape[1]):
        chosen, scores = group_scores(rotated_query, key_rot, group_index, allowed, scaling)
        largest = jnp.max(scores, 2, keepdims=True)
        logsum = largest + jnp.log(jnp.sum(jnp.exp(scores - largest), 2, keepdims=True))
        weights = jnp.exp(scores - logsum).astype(jnp.bfloat16)
        outputs.append(
            jnp.einsum(
                "hqk,kd->qhd",
                weights,
                value_low[:, group_index, :],
                preferred_element_type=jnp.float32,
            )
        )
        logsums.append(logsum)
    return (jnp.concatenate(outputs, 1), logsums)


def attend_back(rotated_query, key_rot, value_low, grad_heads, logsums, allowed, scaling):
    per_group = rotated_query.shape[1] // key_rot.shape[1]
    query_parts = []
    key_parts = []
    value_parts = []
    for group_index in range(key_rot.shape[1]):
        chosen, scores = group_scores(rotated_query, key_rot, group_index, allowed, scaling)
        softmax_weights = jnp.exp(scores - logsums[group_index])
        grad_group = grad_heads[:, group_index * per_group : (group_index + 1) * per_group, :]
        grad_probs = jnp.einsum(
            "qhd,kd->hqk",
            grad_group,
            value_low[:, group_index, :],
            preferred_element_type=jnp.float32,
        )
        centered = grad_probs - jnp.sum(softmax_weights * grad_probs, 2, keepdims=True)
        grad_scores = (softmax_weights * centered).astype(jnp.bfloat16)
        query_parts.append(
            jnp.einsum(
                "hqk,kd->qhd",
                grad_scores,
                key_rot[:, group_index, :],
                preferred_element_type=jnp.float32,
            )
            * scaling
        )
        key_parts.append(
            jnp.einsum("hqk,qhd->kd", grad_scores, chosen, preferred_element_type=jnp.float32)
            * scaling
        )
        value_parts.append(
            jnp.einsum(
                "hqk,qhd->kd",
                softmax_weights.astype(jnp.bfloat16),
                grad_group,
                preferred_element_type=jnp.float32,
            )
        )
    return (jnp.concatenate(query_parts, 1), jnp.stack(key_parts, 1), jnp.stack(value_parts, 1))


class Places:
    def __init__(self, dp):
        self.dp = dp
        self.planes = PLANES
        self.rows = dp // (PLANES * CORES)
        self.chips = dp // CORES
        index = lax.axis_index("dp")
        self.z = index // (self.rows * CORES)
        self.y = (index // CORES) % self.rows
        self.core = index % CORES
        self.x = lax.axis_index("tensor")
        chip = index // CORES
        self.ring_place = jnp.where(chip % 2 == 0, chip // 2, self.chips - 1 - chip // 2)

    def move(self, value, target):
        return lax.ppermute(value, "dp", [(d, target(d)) for d in range(self.dp)])

    def along_z(self, value, steps):
        stride = self.rows * CORES
        return self.move(value, lambda d: (d + steps * stride) % self.dp)

    def along_y(self, value, steps):
        def target(d):
            y = (d // CORES) % self.rows
            return d + ((y + steps) % self.rows - y) * CORES

        return self.move(value, target)

    def other_core(self, value):
        return self.move(value, lambda d: d ^ 1)

    def other_x(self, value):
        return lax.ppermute(value, "tensor", [(0, 1), (1, 0)])

    def ring_chip(self, place):
        place = place % self.chips
        half = self.chips // 2
        return jnp.where(place < half, 2 * place, 2 * (self.chips - 1 - place) + 1)

    def along_ring(self, value, steps):
        half = self.chips // 2
        cycle = [2 * p if p < half else 2 * (self.chips - 1 - p) + 1 for p in range(self.chips)]
        place_of = {chip: p for p, chip in enumerate(cycle)}

        def target(d):
            chip = cycle[(place_of[d // CORES] + steps) % self.chips]
            return chip * CORES + d % CORES

        return self.move(value, target)


def ring_gather(at, clockwise, counter):
    currents = [clockwise, counter]
    buffers = [
        jnp.zeros((at.chips, CORES) + part.shape, part.dtype) for part in (clockwise, counter)
    ]
    for step in range(at.chips):
        for way, sign in ((0, 1), (1, -1)):
            block = currents[way]
            chip = at.ring_chip(at.ring_place - sign * step)
            if step < at.chips - 1:
                currents[way] = at.along_ring(block, sign)
            twin = at.other_core(block)
            buffers[way] = lax.dynamic_update_slice(
                buffers[way], block[None, None], (chip, at.core, 0, 0)
            )
            buffers[way] = lax.dynamic_update_slice(
                buffers[way], twin[None, None], (chip, 1 - at.core, 0, 0)
            )
    return [buffer.reshape(-1, buffer.shape[-1]) for buffer in buffers]


def ring_scatter(at, clockwise, counter):
    locals_ = []
    for part in (clockwise, counter):
        blocks = part.reshape(at.chips, CORES, -1, part.shape[-1])
        away = lax.dynamic_index_in_dim(blocks, 1 - at.core, 1, keepdims=False)
        mine = lax.dynamic_index_in_dim(blocks, at.core, 1, keepdims=False)
        locals_.append((mine.astype(jnp.float32) + at.other_core(away)).astype(jnp.bfloat16))

    def local(way, place):
        return lax.dynamic_index_in_dim(locals_[way], at.ring_chip(place), 0, keepdims=False)

    totals = [local(way, at.ring_place - sign) for way, sign in ((0, 1), (1, -1))]
    for step in range(1, at.chips):
        for way, sign in ((0, 1), (1, -1)):
            arrived = at.along_ring(totals[way], sign).astype(jnp.float32)
            total = arrived + local(way, at.ring_place - sign * (step + 1)).astype(jnp.float32)
            totals[way] = total if step == at.chips - 1 else total.astype(jnp.bfloat16)
    return totals


def quarter_gather(at, parts, quarter):
    count, own_rows, _ = parts.shape
    buffer = jnp.zeros((count, at.planes, at.rows, CORES, own_rows, quarter), parts.dtype)
    for k in (2, 1, 3, 0):
        wanted = ((at.z + k) % at.planes) * quarter
        block = lax.dynamic_slice(parts, (0, 0, wanted), (count, own_rows, quarter))
        if k:
            block = at.along_z(block, k)
        plane = (at.z - k) % at.planes
        for j in range(at.rows):
            other = at.along_y(block, j) if j else block
            row = (at.y - j) % at.rows
            for core, piece in ((at.core, other), (1 - at.core, at.other_core(other))):
                buffer = lax.dynamic_update_slice(
                    buffer, piece[:, None, None, None], (0, plane, row, core, 0, 0)
                )
    return buffer.reshape(count, -1, quarter)


def quarter_scatter(at, grads):
    columns = grads.shape[-1]
    blocks = grads.reshape(at.planes, at.rows, CORES, -1, columns)
    away = lax.dynamic_index_in_dim(blocks, 1 - at.core, 2, keepdims=False)
    mine = lax.dynamic_index_in_dim(blocks, at.core, 2, keepdims=False)
    blocks = (mine.astype(jnp.float32) + at.other_core(away)).astype(jnp.bfloat16)
    total = lax.dynamic_index_in_dim(blocks, at.y, 1, keepdims=False).astype(jnp.float32)
    for j in range(1, at.rows):
        away = lax.dynamic_index_in_dim(blocks, (at.y + j) % at.rows, 1, keepdims=False)
        total = total + at.along_y(away, j)
    result = jnp.zeros((total.shape[1], at.planes * columns), jnp.float32)
    low = total.astype(jnp.bfloat16)
    for k in (2, 1, 3, 0):
        if k:
            piece = at.along_z(
                lax.dynamic_index_in_dim(low, (at.z + k) % at.planes, 0, keepdims=False), k
            )
        else:
            piece = lax.dynamic_index_in_dim(total, at.z, 0, keepdims=False)
        result = lax.dynamic_update_slice(
            result, piece.astype(jnp.float32), (0, ((at.z - k) % at.planes) * columns)
        )
    return result


def token_gather(at, own):
    blocks = []
    for k in range(at.planes):
        block = at.along_z(own, k) if k else own
        blocks += [block, at.other_x(block)]
    return jnp.concatenate(blocks, 0)


def token_scatter(at, part_of, rows_own):
    total = None
    for k in (2, 1, 3, 0):
        part = part_of(k)
        mine = part[:rows_own] + at.other_x(part[rows_own:].astype(jnp.bfloat16))
        if k:
            mine = at.along_z(mine.astype(jnp.bfloat16), -k)
        total = mine.astype(jnp.float32) if total is None else total + mine
    return total


def on_device(
    tokens,
    seq_lens,
    norm_gains,
    w_query,
    key_weight,
    value_weight,
    w_out,
    w_gate,
    w_up,
    w_down,
    cotangent,
):
    at = Places(lax.axis_size("dp"))
    rows_own = tokens.shape[0]
    row_count = rows_own * lax.axis_size("tensor")
    width_query = w_query.shape[1]
    width_kv = key_weight.shape[1]
    heads_query = width_query // HEAD_WIDTH
    heads_kv = width_kv // HEAD_WIDTH
    width_quarter = w_gate.shape[1] // at.planes
    scaling = HEAD_WIDTH ** (-0.5)

    def both_x(own, other):
        first = jnp.where(at.x == 0, own, other)
        second = jnp.where(at.x == 0, other, own)
        return jnp.concatenate([first, second], 0)

    def sum_x(part):
        other = lax.dynamic_slice_in_dim(part, (1 - at.x) * rows_own, rows_own, 0)
        mine = lax.dynamic_slice_in_dim(part, at.x * rows_own, rows_own, 0)
        return mine + at.other_x(other.astype(jnp.bfloat16))

    row_ids, segment, position, in_use = layout(seq_lens[0], row_count)
    in_use_own = lax.dynamic_slice_in_dim(in_use, at.x * rows_own, rows_own, 0)
    cosine_lookup, sine_lookup = rope_tables(position, HEAD_WIDTH)
    allowed = (segment[:, None] == segment[None, :]) & (row_ids[None, :] <= row_ids[:, None])
    gain_rows = norm_gains.astype(jnp.float32)
    inputs = tokens.astype(jnp.float32)
    scale_one = lax.rsqrt(jnp.mean(inputs * inputs, 1, keepdims=True) + EPSILON)
    normed_own = (inputs * scale_one * gain_rows[0]).astype(jnp.bfloat16)
    first_normalized = both_x(normed_own, at.other_x(normed_own))
    grad_mixed = cotangent.astype(jnp.float32) * in_use_own[:, None]
    grad_low_own = grad_mixed.astype(jnp.bfloat16)

    qk_all, vo_all = ring_gather(
        at,
        jnp.concatenate([w_query, key_weight], 1),
        jnp.concatenate([value_weight, w_out], 1),
    )
    value_all, out_all = vo_all[:, :width_kv], vo_all[:, width_kv:]
    ffn_own = after(jnp.stack([w_gate, w_up, w_down]), qk_all, vo_all)
    gate_all, up_all, down_all = quarter_gather(at, ffn_own, width_quarter)

    qk_rows = matrix_product(first_normalized, qk_all)
    query_rows = qk_rows[:, :width_query].reshape(row_count, heads_query, HEAD_WIDTH)
    key_projected = qk_rows[:, width_query:].reshape(row_count, heads_kv, HEAD_WIDTH)
    value_low = (
        matrix_product(first_normalized, value_all)
        .astype(jnp.bfloat16)
        .reshape(row_count, heads_kv, HEAD_WIDTH)
    )
    rotated_query = apply_rotation(query_rows, cosine_lookup, sine_lookup).astype(jnp.bfloat16)
    key_rot = apply_rotation(key_projected, cosine_lookup, sine_lookup).astype(jnp.bfloat16)
    attended, logsums = attend(rotated_query, key_rot, value_low, allowed, scaling)
    attended = attended.reshape(row_count, heads_query * HEAD_WIDTH).astype(jnp.bfloat16)
    state = inputs + sum_x(matmul_nt(attended, out_all))
    scale_two = lax.rsqrt(jnp.mean(state * state, 1, keepdims=True) + EPSILON)
    normed_two = token_gather(at, (state * scale_two * gain_rows[1]).astype(jnp.bfloat16))
    grad_low = token_gather(at, after(grad_low_own, normed_two))

    gate = matrix_product(normed_two, gate_all)
    up_proj = matrix_product(normed_two, up_all)
    sigmoid_gate = jax.nn.sigmoid(gate)
    silu_gate = gate * sigmoid_gate
    hidden = (silu_gate * up_proj).astype(jnp.bfloat16)
    grad_hidden = matrix_product(grad_low, down_all)
    grad_gate_in = (
        grad_hidden * up_proj * sigmoid_gate * (1.0 + gate * (1.0 - sigmoid_gate))
    ).astype(jnp.bfloat16)
    grad_up_in = (grad_hidden * silu_gate).astype(jnp.bfloat16)

    def rows_of(value, k):
        return value[k * row_count : (k + 1) * row_count]

    grad_normed_two = token_scatter(
        at,
        lambda k: matmul_nt(rows_of(grad_gate_in, k), gate_all)
        + matmul_nt(rows_of(grad_up_in, k), up_all),
        rows_own,
    )
    hidden_late = after(hidden, grad_normed_two)
    ffn_out = token_scatter(at, lambda k: matmul_nt(rows_of(hidden_late, k), down_all), rows_own)
    mixed = ((state + ffn_out) * in_use_own[:, None]).astype(jnp.bfloat16)
    hat_two = state * scale_two
    inner_two = grad_normed_two * gain_rows[1]
    grad_state = grad_mixed + scale_two * (
        inner_two - hat_two * jnp.mean(inner_two * hat_two, 1, keepdims=True)
    )
    gain_two = jnp.sum(grad_normed_two * hat_two, 0)
    grad_state_own = grad_state.astype(jnp.bfloat16)
    grad_state_low = both_x(grad_state_own, at.other_x(grad_state_own))

    grad_gate = quarter_scatter(at, matmul_tn(normed_two, grad_gate_in).astype(jnp.bfloat16))
    grad_up = quarter_scatter(at, matmul_tn(normed_two, grad_up_in).astype(jnp.bfloat16))
    grad_down = quarter_scatter(at, matmul_tn(grad_low, hidden).astype(jnp.bfloat16))

    grad_attended = (
        matrix_product(grad_state_low, out_all)
        .astype(jnp.bfloat16)
        .reshape(row_count, heads_query, HEAD_WIDTH)
    )
    grad_query_rot, grad_key_rot, grad_values = attend_back(
        rotated_query, key_rot, value_low, grad_attended, logsums, allowed, scaling
    )
    grad_q = (
        unrotate(grad_query_rot, cosine_lookup, sine_lookup)
        .reshape(row_count, heads_query * HEAD_WIDTH)
        .astype(jnp.bfloat16)
    )
    grad_k = (
        unrotate(grad_key_rot, cosine_lookup, sine_lookup)
        .reshape(row_count, heads_kv * HEAD_WIDTH)
        .astype(jnp.bfloat16)
    )
    grad_v = grad_values.reshape(row_count, heads_kv * HEAD_WIDTH).astype(jnp.bfloat16)
    grad_qk = jnp.concatenate([grad_q, grad_k], 1)
    grad_vo = jnp.concatenate(
        [
            matmul_tn(first_normalized, grad_v).astype(jnp.bfloat16),
            matmul_tn(grad_state_low, attended).astype(jnp.bfloat16),
        ],
        1,
    )
    sum_qk, sum_vo = ring_scatter(
        at, matmul_tn(first_normalized, grad_qk).astype(jnp.bfloat16), grad_vo
    )
    grad_normed_one = sum_x(matmul_nt(grad_qk, qk_all) + matmul_nt(grad_v, value_all))
    hat_one = inputs * scale_one
    inner_one = grad_normed_one * gain_rows[0]
    grad_tokens = (
        grad_state
        + scale_one * (inner_one - hat_one * jnp.mean(inner_one * hat_one, 1, keepdims=True))
    ).astype(jnp.bfloat16)
    gain_one = jnp.sum(grad_normed_one * hat_one, 0)
    grad_gains = jnp.stack([gain_one, gain_two])
    grad_gains = grad_gains + at.other_x(grad_gains)
    bit = 1
    while bit < at.dp:
        grad_gains = grad_gains + at.move(grad_gains, lambda d: d ^ bit)
        bit *= 2
    return (
        mixed,
        grad_tokens,
        grad_gains,
        sum_qk[:, :width_query],
        sum_qk[:, width_query:],
        sum_vo[:, :width_kv],
        sum_vo[:, width_kv:],
        grad_gate,
        grad_up,
        grad_down,
    )


def solution(mesh):
    in_specs = (
        P(("dp", "tensor"), None),
        P("dp", None),
        P(),
        P("dp", "tensor"),
        P("dp", "tensor"),
        P("dp", "tensor"),
        P("dp", "tensor"),
        P("dp", "tensor"),
        P("dp", "tensor"),
        P("dp", "tensor"),
        P(("dp", "tensor"), None),
    )
    out_specs = (
        P(("dp", "tensor"), None),
        P(("dp", "tensor"), None),
        P(),
        P("dp", "tensor"),
        P("dp", "tensor"),
        P("dp", "tensor"),
        P("dp", "tensor"),
        P("dp", "tensor"),
        P("dp", "tensor"),
        P("dp", "tensor"),
    )
    return jax.shard_map(
        on_device, mesh=mesh, in_specs=in_specs, out_specs=out_specs, check_vma=False
    )
```

```python
import functools
import math

import jax
import jax.numpy as jnp
from jax import lax
from jax.experimental import pallas as pl
from jax.experimental.layout import Layout, with_layout_constraint
from jax.experimental.pallas import tpu as pltpu
from jax.sharding import PartitionSpec as P

HEAD_WIDTH = 64
EPSILON = 1e-05
MASKED = -1e30
CORES = 2
PLANES = 4


def matrix_product(left_side, right_side):
    return jnp.dot(left_side, right_side, preferred_element_type=jnp.float32)


def matmul_nt(left_side, right_side):
    return lax.dot_general(
        left_side, right_side, (((1,), (1,)), ((), ())), preferred_element_type=jnp.float32
    )


def matmul_tn(left_side, right_side):
    return lax.dot_general(
        left_side, right_side, (((0,), (0,)), ((), ())), preferred_element_type=jnp.float32
    )


def after(value, *earlier):
    return lax.optimization_barrier((value, *earlier))[0]


def row_major(value):
    return with_layout_constraint(value, Layout(major_to_minor=(0, 1)))


def layout(lengths, row_count):
    finish = jnp.cumsum(lengths)
    starts = jnp.concatenate([finish - lengths, finish[-1:]])
    row_ids = jnp.arange(row_count, dtype=jnp.int32)
    segment = jnp.sum((row_ids[:, None] >= finish[None, :]).astype(jnp.int32), 1)
    chosen_slot = segment[:, None] == jnp.arange(starts.shape[0], dtype=jnp.int32)[None, :]
    first_row = jnp.sum(jnp.where(chosen_slot, starts[None, :], 0), 1)
    position = row_ids - first_row
    in_use = (segment < lengths.shape[0]).astype(jnp.float32)
    return (row_ids, segment, position, in_use)


def rope_tables(position, head_size):
    halfway = head_size // 2
    ladder = jnp.arange(halfway, dtype=jnp.float32)
    inverse = 1.0 / 500000.0 ** (ladder * 2.0 / head_size)
    wavelength = 2.0 * math.pi / inverse
    smooth = (8192.0 / wavelength - 1.0) / 3.0
    blended = (1.0 - smooth) * inverse / 32.0 + smooth * inverse
    scaled = jnp.where(
        wavelength > 8192.0, inverse / 32.0, jnp.where(wavelength < 2048.0, inverse, blended)
    )
    angles = position.astype(jnp.float32)[:, None] * scaled[None, :]
    cosine_lookup = jnp.cos(angles)
    sine_lookup = jnp.sin(angles)
    return (
        jnp.concatenate([cosine_lookup, cosine_lookup], 1),
        jnp.concatenate([sine_lookup, sine_lookup], 1),
    )


def apply_rotation(heads, cosine_lookup, sine_lookup):
    halfway = heads.shape[-1] // 2
    turned = jnp.concatenate([-heads[..., halfway:], heads[..., :halfway]], -1)
    return heads * cosine_lookup[:, None, :] + turned * sine_lookup[:, None, :]


def unrotate(grads, cosine_lookup, sine_lookup):
    halfway = grads.shape[-1] // 2
    scaled = grads * sine_lookup[:, None, :]
    return grads * cosine_lookup[:, None, :] + jnp.concatenate(
        [scaled[..., halfway:], -scaled[..., :halfway]], -1
    )


def group_scores(rotated_query, key_rot, group_index, allowed, scaling):
    per_group = rotated_query.shape[1] // key_rot.shape[1]
    chosen = rotated_query[:, group_index * per_group : (group_index + 1) * per_group, :]
    scores = (
        jnp.einsum(
            "qhd,kd->hqk", chosen, key_rot[:, group_index, :], preferred_element_type=jnp.float32
        )
        * scaling
    )
    return (chosen, jnp.where(allowed[None], scores, MASKED))


def attend(rotated_query, key_rot, value_low, allowed, scaling):
    outputs = []
    logsums = []
    for group_index in range(key_rot.shape[1]):
        chosen, scores = group_scores(rotated_query, key_rot, group_index, allowed, scaling)
        largest = jnp.max(scores, 2, keepdims=True)
        logsum = largest + jnp.log(jnp.sum(jnp.exp(scores - largest), 2, keepdims=True))
        weights = jnp.exp(scores - logsum).astype(jnp.bfloat16)
        outputs.append(
            jnp.einsum(
                "hqk,kd->qhd",
                weights,
                value_low[:, group_index, :],
                preferred_element_type=jnp.float32,
            )
        )
        logsums.append(logsum)
    return (jnp.concatenate(outputs, 1), logsums)


def attend_back(rotated_query, key_rot, value_low, grad_heads, logsums, allowed, scaling):
    per_group = rotated_query.shape[1] // key_rot.shape[1]
    query_parts = []
    key_parts = []
    value_parts = []
    for group_index in range(key_rot.shape[1]):
        chosen, scores = group_scores(rotated_query, key_rot, group_index, allowed, scaling)
        softmax_weights = jnp.exp(scores - logsums[group_index])
        grad_group = grad_heads[:, group_index * per_group : (group_index + 1) * per_group, :]
        grad_probs = jnp.einsum(
            "qhd,kd->hqk",
            grad_group,
            value_low[:, group_index, :],
            preferred_element_type=jnp.float32,
        )
        centered = grad_probs - jnp.sum(softmax_weights * grad_probs, 2, keepdims=True)
        grad_scores = (softmax_weights * centered).astype(jnp.bfloat16)
        query_parts.append(
            jnp.einsum(
                "hqk,kd->qhd",
                grad_scores,
                key_rot[:, group_index, :],
                preferred_element_type=jnp.float32,
            )
            * scaling
        )
        key_parts.append(
            jnp.einsum("hqk,qhd->kd", grad_scores, chosen, preferred_element_type=jnp.float32)
            * scaling
        )
        value_parts.append(
            jnp.einsum(
                "hqk,qhd->kd",
                softmax_weights.astype(jnp.bfloat16),
                grad_group,
                preferred_element_type=jnp.float32,
            )
        )
    return (jnp.concatenate(query_parts, 1), jnp.stack(key_parts, 1), jnp.stack(value_parts, 1))


class Places:
    def __init__(self, dp):
        self.dp = dp
        self.planes = PLANES
        self.rows = dp // (PLANES * CORES)
        self.chips = dp // CORES
        index = lax.axis_index("dp")
        self.z = index // (self.rows * CORES)
        self.y = (index // CORES) % self.rows
        self.core = index % CORES
        self.x = lax.axis_index("tensor")
        chip = index // CORES
        self.ring_place = jnp.where(chip % 2 == 0, chip // 2, self.chips - 1 - chip // 2)
        stride = self.rows * CORES
        self.columns = [[z * stride + i for z in range(PLANES)] for i in range(stride)]

    def move(self, value, target):
        return lax.ppermute(value, "dp", [(d, target(d)) for d in range(self.dp)])

    def across_z(self, value, mask):
        stride = self.rows * CORES
        return self.move(value, lambda d: d ^ (mask * stride))

    def along_y(self, value, steps):
        def target(d):
            y = (d // CORES) % self.rows
            return d + ((y + steps) % self.rows - y) * CORES

        return self.move(value, target)

    def other_core(self, value):
        return self.move(value, lambda d: d ^ 1)

    def other_x(self, value):
        return lax.ppermute(value, "tensor", [(0, 1), (1, 0)])

    def by_core(self, own, other, axis):
        first = jnp.where(self.core == 0, own, other)
        second = jnp.where(self.core == 0, other, own)
        return jnp.stack([first, second], axis)

    def ring_chip(self, place):
        place = place % self.chips
        half = self.chips // 2
        return jnp.where(place < half, 2 * place, 2 * (self.chips - 1 - place) + 1)

    def along_ring(self, value, steps):
        half = self.chips // 2
        cycle = [2 * p if p < half else 2 * (self.chips - 1 - p) + 1 for p in range(self.chips)]
        place_of = {chip: p for p, chip in enumerate(cycle)}

        def target(d):
            chip = cycle[(place_of[d // CORES] + steps) % self.chips]
            return chip * CORES + d % CORES

        return self.move(value, target)


def ring_gather(at, clockwise, counter, beside):
    currents = [clockwise, counter]
    buffers = [jnp.zeros((at.chips,) + part.shape, part.dtype) for part in currents]
    steps = []
    for step in range(at.chips):
        if step == at.chips // 2:
            extra = beside(tuple(currents))
        if step == at.chips - 2:
            currents = list(after(tuple(currents), *extra))
        else:
            currents = list(lax.optimization_barrier(tuple(currents)))
        for way, sign in ((0, 1), (1, -1)):
            block = currents[way]
            if step < at.chips - 1:
                currents[way] = at.along_ring(block, sign)
            chip = at.ring_chip(at.ring_place - sign * step)
            buffers[way] = lax.dynamic_update_slice(buffers[way], block[None], (chip, 0, 0))
        steps.append(tuple(currents))
    return buffers, steps, extra


def ring_scatter(at, clockwise, counter):
    locals_ = []
    for part in (clockwise, counter):
        blocks = part.reshape(at.chips, CORES, -1, part.shape[-1])
        away = lax.dynamic_index_in_dim(blocks, 1 - at.core, 1, keepdims=False)
        mine = lax.dynamic_index_in_dim(blocks, at.core, 1, keepdims=False)
        locals_.append((mine.astype(jnp.float32) + at.other_core(away)).astype(jnp.bfloat16))

    def local(way, place):
        return lax.dynamic_index_in_dim(locals_[way], at.ring_chip(place), 0, keepdims=False)

    totals = [local(way, at.ring_place - sign) for way, sign in ((0, 1), (1, -1))]
    steps = []
    for step in range(1, at.chips):
        totals = list(lax.optimization_barrier(tuple(totals)))
        for way, sign in ((0, 1), (1, -1)):
            arrived = at.along_ring(totals[way], sign).astype(jnp.float32)
            total = arrived + local(way, at.ring_place - sign * (step + 1)).astype(jnp.float32)
            totals[way] = total if step == at.chips - 1 else total.astype(jnp.bfloat16)
        if step < at.chips - 1:
            steps.append(totals[0])
    return (*totals, steps)


def product(left_side, right_side, contract):
    return lax.dot_general(
        left_side, right_side, (contract, ((), ())), preferred_element_type=jnp.float32
    )


NN = ((1,), (0,))
NT = ((1,), (1,))
TN = ((0,), (0,))


class Held:
    def __init__(self, place, blocks, weights, which, held, sems):
        self.z, self.y, self.core, self.rows = (place[i] for i in range(4))
        self.blocks, self.weights, self.which = blocks, weights, which
        self.held, self.sems = held, sems
        for i in range(len(which)):
            for n in range(len(blocks)):
                self.copy(i, n).start()

    def copy(self, i, n):
        mask, back, other = self.blocks[n]
        size = self.weights[n].shape[1]
        chip = (self.z ^ mask) * self.rows + lax.rem(self.y + self.rows - back, self.rows)
        start = pl.multiple_of((chip * CORES + (self.core ^ other)) * size, size)
        return pltpu.make_async_copy(
            self.weights[n].at[self.which[i]],
            self.held.at[i, pl.ds(start, size)],
            self.sems.at[i, n],
        )

    def wait(self, i):
        for n in range(len(self.blocks)):
            self.copy(i, n).wait()


def held_call(at, kernel, weights, which, arrays, out_shapes):
    blocks = list(weights)
    sources = [weights[key] for key in blocks]
    _, size, quarter = sources[0].shape
    place = jnp.stack([at.z, at.y, at.core, jnp.int32(at.rows)]).astype(jnp.int32)
    vmem = pl.BlockSpec(memory_space=pltpu.VMEM)
    low = jnp.bfloat16

    def body(place, *refs):
        ins, refs = refs[: len(arrays)], refs[len(arrays) :]
        sources, refs = refs[: len(blocks)], refs[len(blocks) :]
        outs, (held, sems) = refs[: len(out_shapes)], refs[len(out_shapes) :]
        kernel(Held(place, blocks, sources, which, held, sems), ins, outs)

    return pl.pallas_call(
        body,
        in_specs=[pl.BlockSpec(memory_space=pltpu.SMEM)]
        + [vmem] * len(arrays)
        + [pl.BlockSpec(memory_space=pl.ANY)] * len(sources),
        out_specs=[vmem] * len(out_shapes),
        out_shape=[jax.ShapeDtypeStruct(shape, low) for shape in out_shapes],
        scratch_shapes=[
            pltpu.VMEM((len(which), len(blocks) * size, quarter), low),
            pltpu.SemaphoreType.DMA((len(which), len(blocks))),
        ],
        compiler_params=pltpu.CompilerParams(vmem_limit_bytes=56 * 2**20),
        cost_estimate=pl.CostEstimate(flops=1, bytes_accessed=1, transcendentals=0),
    )(place, *arrays, *sources)


def forward(at, weights, normed):
    rows_own, width = normed[0].shape
    quarter = next(iter(weights.values())).shape[-1]
    count = len(normed) // 2
    half = width // 2

    def kernel(held, normed, outs):
        hidden_ref, silu_ref, slope_ref, *out_refs = outs
        for k in range(count):
            here = slice(2 * k * rows_own, 2 * (k + 1) * rows_own)
            own = slice(k * rows_own, (k + 1) * rows_own)
            rows = jnp.concatenate([normed[2 * k][...], normed[2 * k + 1][...]], 0)
            if k == 0:
                held.wait(0)
            gate = product(rows, held.held[0], NN)
            if k == 0:
                held.wait(1)
            up = product(rows, held.held[1], NN)
            sigmoid_gate = jax.nn.sigmoid(gate)
            silu_gate = gate * sigmoid_gate
            hidden = (silu_gate * up).astype(jnp.bfloat16)
            hidden_ref[here] = hidden
            silu_ref[here] = silu_gate.astype(jnp.bfloat16)
            slope = up * sigmoid_gate * (1.0 + gate * (1.0 - sigmoid_gate))
            slope_ref[here] = slope.astype(jnp.bfloat16)
            if k == 0:
                held.wait(2)
            out = product(hidden, held.held[2], NT).astype(jnp.bfloat16)
            for i in range(2):
                columns = slice(i * half, (i + 1) * half)
                out_refs[2 * i][own] = out[:rows_own, columns]
                out_refs[2 * i + 1][own] = out[rows_own:, columns]

    shapes = [(2 * count * rows_own, quarter)] * 3 + [(count * rows_own, half)] * 4
    return held_call(at, kernel, weights, (0, 1, 2), normed, shapes)


def backward(at, weights, masks, grads, silu, slope):
    rows_own, width = grads[0].shape[1:]

    def kernel(held, ins, outs):
        mine, other, silu, slope = ins
        gate_ref, up_ref, *back = outs
        for k, mask in enumerate(masks):
            here = slice(2 * k * rows_own, 2 * (k + 1) * rows_own)
            rows = jnp.concatenate([mine[held.z ^ mask], other[held.z ^ mask]], 0)
            if k == 0:
                held.wait(0)
            grad_hidden = product(rows, held.held[0], NN)
            grad_gate = (grad_hidden * slope[here]).astype(jnp.bfloat16)
            grad_up = (grad_hidden * silu[here]).astype(jnp.bfloat16)
            gate_ref[here] = grad_gate
            up_ref[here] = grad_up
            if k == 0:
                held.wait(1)
            total = product(grad_gate, held.held[1], NT)
            if k == 0:
                held.wait(2)
            total = (total + product(grad_up, held.held[2], NT)).astype(jnp.bfloat16)
            back[2 * k][...] = total[:rows_own]
            back[2 * k + 1][...] = total[rows_own:]

    shapes = [silu.shape] * 2 + [(rows_own, width)] * (2 * len(masks))
    return held_call(at, kernel, weights, (2, 0, 1), [*grads, silu, slope], shapes)


def weight_grad_kernel(masks, by_plane, place, *refs):
    z, core = place[0], place[1]
    *left, right, own_ref, other_ref = refs
    if by_plane:
        pieces = [ref[z ^ mask] for mask in masks for ref in left]
    else:
        pieces = [ref[...] for ref in left]
    total = product(jnp.concatenate(pieces, 0), right[...], TN).astype(jnp.bfloat16)
    rows, _, own_features, quarter = own_ref.shape
    total = total.reshape(rows, CORES, own_features, quarter)
    own_ref[:, 0] = jnp.where(core == 0, total[:, 0], total[:, 1])
    other_ref[:, 0] = jnp.where(core == 0, total[:, 1], total[:, 0])


def weight_grad(at, masks, left, right, own_features):
    by_plane = left[0].ndim == 3
    width = left[0].shape[-1]
    quarter = right.shape[-1]
    share = width // at.planes
    place = jnp.stack([at.z, at.core]).astype(jnp.int32)
    shape = (at.rows, at.planes, own_features, quarter)
    block = (at.rows, 1, own_features, quarter)
    if by_plane:
        left_spec = pl.BlockSpec(left[0].shape[:2] + (share,), lambda i, place: (0, 0, i))
    else:
        left_spec = pl.BlockSpec((left[0].shape[0], share), lambda i, place: (0, i))
    return pl.pallas_call(
        functools.partial(weight_grad_kernel, masks, by_plane),
        grid_spec=pltpu.PrefetchScalarGridSpec(
            num_scalar_prefetch=1,
            grid=(at.planes,),
            in_specs=[left_spec] * len(left) + [pl.BlockSpec(right.shape, lambda i, place: (0, 0))],
            out_specs=[pl.BlockSpec(block, lambda i, place: (0, i, 0, 0))] * 2,
        ),
        out_shape=[jax.ShapeDtypeStruct(shape, jnp.bfloat16)] * 2,
        compiler_params=pltpu.CompilerParams(vmem_limit_bytes=56 * 2**20),
        cost_estimate=pl.CostEstimate(flops=1, bytes_accessed=1, transcendentals=0),
    )(place, *left, right)


def on_device(
    tokens,
    seq_lens,
    norm_gains,
    w_query,
    key_weight,
    value_weight,
    w_out,
    w_gate,
    w_up,
    w_down,
    cotangent,
):
    at = Places(lax.axis_size("dp"))
    rows_own = tokens.shape[0]
    row_count = rows_own * lax.axis_size("tensor")
    width_query = w_query.shape[1]
    width_kv = key_weight.shape[1]
    heads_query = width_query // HEAD_WIDTH
    heads_kv = width_kv // HEAD_WIDTH
    quarter = w_gate.shape[1] // at.planes
    own_features = w_gate.shape[0]
    scaling = HEAD_WIDTH ** (-0.5)

    def both_x(own, other):
        first = jnp.where(at.x == 0, own, other)
        second = jnp.where(at.x == 0, other, own)
        return jnp.concatenate([first, second], 0)

    def sum_x(part):
        other = lax.dynamic_slice_in_dim(part, (1 - at.x) * rows_own, rows_own, 0)
        mine = lax.dynamic_slice_in_dim(part, at.x * rows_own, rows_own, 0)
        return mine + at.other_x(other.astype(jnp.bfloat16))

    row_ids, segment, position, in_use = layout(seq_lens[0], row_count)
    in_use_own = lax.dynamic_slice_in_dim(in_use, at.x * rows_own, rows_own, 0)
    gain_rows = norm_gains.astype(jnp.float32)
    inputs = tokens.astype(jnp.float32)
    scale_one = lax.rsqrt(jnp.mean(inputs * inputs, 1, keepdims=True) + EPSILON)
    normed_own = (inputs * scale_one * gain_rows[0]).astype(jnp.bfloat16)
    first_normalized = both_x(normed_own, at.other_x(normed_own))
    grad_mixed = cotangent.astype(jnp.float32) * in_use_own[:, None]
    grad_low_own = grad_mixed.astype(jnp.bfloat16)
    grad_low_mine = lax.all_gather(grad_low_own, "dp", axis_index_groups=at.columns)

    weights = {}
    shares = {}

    def beside(halfway):
        for mask in range(at.planes):
            start = (at.z ^ mask) * quarter
            parts = after((w_gate, w_up, w_down), *halfway)
            shares[mask] = jnp.stack(
                [lax.dynamic_slice_in_dim(part, start, quarter, 1) for part in parts]
            )
        grad_rows = at.other_x(after(grad_low_mine, *halfway))
        return (grad_rows, at.across_z(shares[2], 2), *to_chips(0, shares[0]))

    def to_chips(mask, block, *earlier):
        weights[mask, 0, 0] = block
        for j in range(1, at.rows):
            weights[mask, j, 0] = at.along_y(after(block, *earlier), j)
            earlier = (weights[mask, j, 0],)
        return earlier

    (qk_mine, vo_mine), steps, (grad_low_other, plane_two, *last) = ring_gather(
        at,
        jnp.concatenate([w_query, key_weight], 1),
        jnp.concatenate([value_weight, w_out], 1),
        beside,
    )
    qk_all = at.by_core(qk_mine, at.other_core(qk_mine), 1).reshape(-1, qk_mine.shape[-1])
    vo_all = at.by_core(vo_mine, at.other_core(vo_mine), 1).reshape(-1, vo_mine.shape[-1])
    value_all, out_all = vo_all[:, :width_kv], vo_all[:, width_kv:]
    position, segment = after((position, segment), *steps[1])
    cosine_lookup, sine_lookup = rope_tables(position, HEAD_WIDTH)
    allowed = (segment[:, None] == segment[None, :]) & (row_ids[None, :] <= row_ids[:, None])

    ring_end = steps[-1]
    plane_three = at.across_z(after(shares[3], *ring_end), 3)
    plane_one = at.across_z(after(shares[1], *ring_end), 1)
    last = to_chips(2, plane_two, *last, *ring_end)

    qk_rows = matrix_product(first_normalized, qk_all)
    query_rows = qk_rows[:, :width_query].reshape(row_count, heads_query, HEAD_WIDTH)
    key_projected = qk_rows[:, width_query:].reshape(row_count, heads_kv, HEAD_WIDTH)
    value_low = (
        matrix_product(first_normalized, value_all)
        .astype(jnp.bfloat16)
        .reshape(row_count, heads_kv, HEAD_WIDTH)
    )
    rotated_query = apply_rotation(query_rows, cosine_lookup, sine_lookup).astype(jnp.bfloat16)
    key_rot = apply_rotation(key_projected, cosine_lookup, sine_lookup).astype(jnp.bfloat16)
    attended, logsums = attend(rotated_query, key_rot, value_low, allowed, scaling)
    attended = attended.reshape(row_count, heads_query * HEAD_WIDTH).astype(jnp.bfloat16)
    branch = matmul_nt(after(attended, grad_low_other, plane_one, plane_three, *last), out_all)
    state = inputs + sum_x(branch)
    scale_two = lax.rsqrt(jnp.mean(state * state, 1, keepdims=True) + EPSILON)
    normed_two = (state * scale_two * gain_rows[1]).astype(jnp.bfloat16)

    last = to_chips(1, plane_one, *last, branch)

    def to_cores(*keys, earlier):
        for mask, back in keys:
            weights[mask, back, 1] = at.other_core(after(weights[mask, back, 0], *earlier))

    every_row = range(at.rows)
    to_cores(*((0, j) for j in every_row), earlier=[branch])
    normed = {(0, 0): normed_two, (0, 1): at.other_x(normed_two)}
    normed[2, 0] = at.across_z(normed_two, 2)
    normed[1, 0] = at.across_z(normed_two, 1)
    to_cores(*((2, j) for j in every_row), earlier=[normed_two])

    stage = list(normed.values()) + list(last)
    normed[3, 0] = at.across_z(after(normed[2, 0], *stage), 1)
    normed[2, 1] = at.other_x(after(normed[2, 0], *stage))
    last = to_chips(3, plane_three, *stage)
    to_cores(*((1, j) for j in every_row), earlier=stage)

    stage = [normed[3, 0], normed[2, 1], *last]
    normed[3, 1] = at.other_x(after(normed[3, 0], *stage))
    normed[1, 1] = at.across_z(after(normed[0, 1], *stage), 1)
    to_cores(*((3, j) for j in every_row), earlier=stage)

    masks = (3, 2, 1, 0)
    normed_rows = [normed[mask, x] for mask in masks for x in range(2)]
    grad_rows = [grad_low_mine, grad_low_other]
    hidden, silu, slope, *outs = forward(at, weights, normed_rows)
    def out_sums(mine, arrived):
        total = (mine.astype(jnp.float32) + arrived).astype(jnp.bfloat16)
        total = total.reshape(len(masks), rows_own, -1)
        order = []
        for z in range(at.planes):
            slot = sum(jnp.where((at.z ^ z) == mask, i, 0) for i, mask in enumerate(masks))
            order.append(lax.dynamic_index_in_dim(total, slot, 0))
        return lax.psum_scatter(
            jnp.concatenate(order, 0), "dp", scatter_dimension=0, axis_index_groups=at.columns
        )

    def of_chip(own, arrived, j):
        y = (at.y + j) % at.rows
        mine = lax.dynamic_index_in_dim(own, y, 0, keepdims=False)
        theirs = lax.dynamic_index_in_dim(arrived, y, 0, keepdims=False)
        return mine.astype(jnp.float32) + theirs

    def over_cores(own, arrived):
        half = at.planes // 2
        away = [of_chip(own, arrived, j).astype(jnp.bfloat16) for j in range(1, at.rows)]
        return of_chip(own, arrived, 0), [[a[:half] for a in away], [a[half:] for a in away]]

    def send_chips(away, earlier):
        return [at.along_y(after(a, *earlier), j + 1) for j, a in enumerate(away)]

    def over_chips(total, lower, upper):
        for first, second in zip(lower, upper, strict=True):
            total = total + jnp.concatenate([first, second], 0)
        return total

    def send_planes(total, wanted, earlier):
        low = total.astype(jnp.bfloat16)
        sent = {}
        for mask in wanted:
            piece = lax.dynamic_index_in_dim(low, at.z ^ mask, 0, keepdims=False)
            sent[mask] = at.across_z(after(piece, *earlier), mask)
        return sent

    def all_columns(total, pieces, *earlier):
        result = jnp.zeros((own_features, at.planes * quarter), jnp.float32)
        own = {0: lax.dynamic_index_in_dim(total, at.z, 0, keepdims=False)}
        for mask, piece in after({**own, **pieces}, *earlier).items():
            result = lax.dynamic_update_slice(
                result, piece.astype(jnp.float32), (0, (at.z ^ mask) * quarter)
            )
        return result

    grad_gate_in, grad_up_in, *back = backward(at, weights, masks, grad_rows, silu, slope)
    out_first = at.other_x(outs[1])

    def sum_of(i, arrived):
        return back[2 * i].astype(jnp.float32) + arrived

    stage = [out_first, back[0]]
    three = at.other_x(after(back[1], *stage))
    one = at.across_z(after(back[5], *stage), 1)
    gate_own, gate_other = weight_grad(
        at, masks, normed_rows, after(grad_gate_in, *stage), own_features
    )
    out_sums_first = out_sums(outs[0], out_first)

    stage = [three, one, gate_own]
    to_two = at.across_z(after(sum_of(0, three).astype(jnp.bfloat16), *stage), 1)
    two = at.other_x(after(back[3], *stage))
    gate_arrived = at.other_core(after(gate_other, *stage))
    up_own, up_other = weight_grad(at, masks, normed_rows, after(grad_up_in, *stage), own_features)

    stage = [to_two, two, gate_arrived, up_own]
    to_zero = at.across_z(after((sum_of(1, two) + to_two).astype(jnp.bfloat16), *stage), 2)
    other_zero = (back[7].astype(jnp.float32) + one).astype(jnp.bfloat16)
    zero = at.other_x(after(other_zero, *stage))
    gate_total, gate_away = over_cores(gate_own, gate_arrived)
    gate_lower = send_chips(gate_away[0], stage)
    up_arrived = at.other_core(after(up_other, *stage))
    down_own, down_other = weight_grad(at, masks, grad_rows, after(hidden, *stage), own_features)

    stage = [zero, *gate_lower, up_arrived, down_own]
    from_one = at.across_z(after(back[4], *stage), 1)
    gate_upper = send_chips(gate_away[1], stage)
    down_arrived = at.other_core(after(down_other, *stage))
    up_total, up_away = over_cores(up_own, up_arrived)

    grad_normed_two = sum_of(3, zero) + from_one + to_zero
    hat_two = state * scale_two
    inner_two = grad_normed_two * gain_rows[1]
    grad_state = grad_mixed + scale_two * (
        inner_two - hat_two * jnp.mean(inner_two * hat_two, 1, keepdims=True)
    )
    gain_two = jnp.sum(grad_normed_two * hat_two, 0)
    grad_state_own = grad_state.astype(jnp.bfloat16)

    stage = [grad_state_own, *gate_upper, down_arrived]
    grad_state_other = at.other_x(after(grad_state_own, *stage))
    up_lower = send_chips(up_away[0], stage)
    gate_total = over_chips(gate_total, gate_lower, gate_upper)
    gate_pieces = send_planes(gate_total, (2, 1), stage)
    down_total, down_away = over_cores(down_own, down_arrived)

    stage = [grad_state_other, *up_lower, *gate_pieces.values()]
    grad_state_low = after(both_x(grad_state_own, grad_state_other), *stage)
    up_upper = send_chips(up_away[1], stage)
    gate_pieces.update(send_planes(gate_total, (3,), stage))
    out_second = at.other_x(after(outs[3], *stage))

    grad_attended = (
        matrix_product(grad_state_low, out_all)
        .astype(jnp.bfloat16)
        .reshape(row_count, heads_query, HEAD_WIDTH)
    )
    stage = [grad_attended, *up_upper, gate_pieces[3]]
    grad_attended = after(grad_attended, *stage)
    up_total = over_chips(up_total, up_lower, up_upper)
    up_pieces = send_planes(up_total, (2, 1), stage)
    down_lower = send_chips(down_away[0], stage)
    grad_query_rot, grad_key_rot, grad_values = attend_back(
        rotated_query, key_rot, value_low, grad_attended, logsums, allowed, scaling
    )
    grad_q = (
        unrotate(grad_query_rot, cosine_lookup, sine_lookup)
        .reshape(row_count, heads_query * HEAD_WIDTH)
        .astype(jnp.bfloat16)
    )
    grad_k = (
        unrotate(grad_key_rot, cosine_lookup, sine_lookup)
        .reshape(row_count, heads_kv * HEAD_WIDTH)
        .astype(jnp.bfloat16)
    )
    grad_v = grad_values.reshape(row_count, heads_kv * HEAD_WIDTH).astype(jnp.bfloat16)
    grad_qk = jnp.concatenate([grad_q, grad_k], 1)
    stage = [grad_qk, *up_pieces.values(), *down_lower, out_second]
    grad_qk = after(grad_qk, *stage)
    up_pieces.update(send_planes(up_total, (3,), stage))
    down_upper = send_chips(down_away[1], stage)
    out_sums_second = out_sums(after(outs[2], *stage), out_second)
    grad_vo = row_major(
        jnp.concatenate(
            [
                row_major(matmul_tn(first_normalized, grad_v).astype(jnp.bfloat16)),
                row_major(matmul_tn(grad_state_low, attended).astype(jnp.bfloat16)),
            ],
            1,
        )
    )
    sum_qk, sum_vo, steps = ring_scatter(
        at, row_major(matmul_tn(first_normalized, grad_qk).astype(jnp.bfloat16)), grad_vo
    )
    down_total = over_chips(down_total, down_lower, down_upper)
    down_pieces = send_planes(down_total, (2, 1), [steps[0]])
    down_pieces.update(send_planes(down_total, (3,), [steps[2], down_pieces[2]]))
    grad_gate = all_columns(gate_total, gate_pieces, steps[1])
    grad_up = all_columns(up_total, up_pieces, steps[2])
    grad_down = all_columns(down_total, down_pieces, steps[-1])
    out_sums_first, out_sums_second = after((out_sums_first, out_sums_second), sum_qk, sum_vo)
    ffn_out = jnp.concatenate([out_sums_first, out_sums_second], 1).astype(jnp.float32)
    mixed = ((state + ffn_out) * in_use_own[:, None]).astype(jnp.bfloat16)
    grad_qk, grad_v = after((grad_qk, grad_v), steps[0])
    grad_normed_one = sum_x(matmul_nt(grad_qk, qk_all) + matmul_nt(grad_v, value_all))
    hat_one = inputs * scale_one
    inner_one = grad_normed_one * gain_rows[0]
    grad_tokens = (
        grad_state
        + scale_one * (inner_one - hat_one * jnp.mean(inner_one * hat_one, 1, keepdims=True))
    ).astype(jnp.bfloat16)
    gain_one = jnp.sum(grad_normed_one * hat_one, 0)
    grad_gains = jnp.stack([gain_one, gain_two])
    grad_gains = grad_gains + at.other_x(grad_gains)
    bit = 1
    while bit < at.dp:
        if steps:
            grad_gains = after(grad_gains, steps.pop(0))
        grad_gains = grad_gains + at.move(grad_gains, lambda d: d ^ bit)
        bit *= 2
    return (
        mixed,
        grad_tokens,
        grad_gains,
        sum_qk[:, :width_query],
        sum_qk[:, width_query:],
        sum_vo[:, :width_kv],
        sum_vo[:, width_kv:],
        grad_gate,
        grad_up,
        grad_down,
    )


def solution(mesh):
    in_specs = (
        P(("dp", "tensor"), None),
        P("dp", None),
        P(),
        P("dp", "tensor"),
        P("dp", "tensor"),
        P("dp", "tensor"),
        P("dp", "tensor"),
        P("dp", "tensor"),
        P("dp", "tensor"),
        P("dp", "tensor"),
        P(("dp", "tensor"), None),
    )
    out_specs = (
        P(("dp", "tensor"), None),
        P(("dp", "tensor"), None),
        P(),
        P("dp", "tensor"),
        P("dp", "tensor"),
        P("dp", "tensor"),
        P("dp", "tensor"),
        P("dp", "tensor"),
        P("dp", "tensor"),
        P("dp", "tensor"),
    )
    return jax.shard_map(
        on_device, mesh=mesh, in_specs=in_specs, out_specs=out_specs, check_vma=False
    )
```

```python
import functools
import math

import jax
import jax.numpy as jnp
from jax import lax
from jax.experimental import pallas as pl
from jax.experimental.pallas import tpu as pltpu
from jax.sharding import PartitionSpec as P

HEAD_WIDTH = 64
EPSILON = 1e-05
MASKED = -1e30
CORES = 2
PLANES = 4


def after(value, *earlier):
    return lax.optimization_barrier((value, *earlier))[0]


def layout(lengths, row_count):
    finish = jnp.cumsum(lengths)
    starts = jnp.concatenate([finish - lengths, finish[-1:]])
    row_ids = jnp.arange(row_count, dtype=jnp.int32)
    segment = jnp.sum((row_ids[:, None] >= finish[None, :]).astype(jnp.int32), 1)
    chosen_slot = segment[:, None] == jnp.arange(starts.shape[0], dtype=jnp.int32)[None, :]
    first_row = jnp.sum(jnp.where(chosen_slot, starts[None, :], 0), 1)
    position = row_ids - first_row
    in_use = (segment < lengths.shape[0]).astype(jnp.float32)
    return (row_ids, segment, position, in_use)


def rope_tables(position, head_size):
    halfway = head_size // 2
    ladder = jnp.arange(halfway, dtype=jnp.float32)
    inverse = 1.0 / 500000.0 ** (ladder * 2.0 / head_size)
    wavelength = 2.0 * math.pi / inverse
    smooth = (8192.0 / wavelength - 1.0) / 3.0
    blended = (1.0 - smooth) * inverse / 32.0 + smooth * inverse
    scaled = jnp.where(
        wavelength > 8192.0, inverse / 32.0, jnp.where(wavelength < 2048.0, inverse, blended)
    )
    angles = position.astype(jnp.float32)[:, None] * scaled[None, :]
    cosine_lookup = jnp.cos(angles)
    sine_lookup = jnp.sin(angles)
    return (
        jnp.concatenate([cosine_lookup, cosine_lookup], 1),
        jnp.concatenate([sine_lookup, sine_lookup], 1),
    )


class Places:
    def __init__(self, dp):
        self.dp = dp
        self.planes = PLANES
        self.rows = dp // (PLANES * CORES)
        self.chips = dp // CORES
        index = lax.axis_index("dp")
        self.z = index // (self.rows * CORES)
        self.y = (index // CORES) % self.rows
        self.core = index % CORES
        self.x = lax.axis_index("tensor")
        stride = self.rows * CORES
        self.columns = [[z * stride + i for z in range(PLANES)] for i in range(stride)]

    def move(self, value, target):
        return lax.ppermute(value, "dp", [(d, target(d)) for d in range(self.dp)])

    def across_z(self, value, mask):
        stride = self.rows * CORES
        return self.move(value, lambda d: d ^ (mask * stride))

    def along_y(self, value, steps):
        def target(d):
            y = (d // CORES) % self.rows
            return d + ((y + steps) % self.rows - y) * CORES

        return self.move(value, target)

    def other_core(self, value):
        return self.move(value, lambda d: d ^ 1)

    def other_x(self, value):
        return lax.ppermute(value, "tensor", [(0, 1), (1, 0)])


def product(left_side, right_side, contract):
    return lax.dot_general(
        left_side, right_side, (contract, ((), ())), preferred_element_type=jnp.float32
    )


NN = ((1,), (0,))
NT = ((1,), (1,))
TN = ((0,), (0,))


class Held:
    def __init__(self, place, blocks, sources, which, held, sems):
        self.z, self.y, self.core, self.rows = (place[i] for i in range(4))
        self.blocks, self.sources, self.which = blocks, sources, which
        self.held, self.sems = held, sems
        for i in range(len(which)):
            for n in range(len(blocks)):
                self.copy(i, n).start()

    def copy(self, i, n):
        (mask, back, other), first, counts = self.blocks[n]
        source, within = first, self.which[i]
        for count in counts:
            if within < count:
                break
            source, within = source + 1, within - count
        size = self.sources[source].shape[1]
        chip = (self.z ^ mask) * self.rows + lax.rem(self.y + self.rows - back, self.rows)
        start = pl.multiple_of((chip * CORES + (self.core ^ other)) * size, size)
        return pltpu.make_async_copy(
            self.sources[source].at[within], self.held.at[i, pl.ds(start, size)], self.sems.at[i, n]
        )

    def wait(self, i):
        for n in range(len(self.blocks)):
            self.copy(i, n).wait()


def cost_of(flops, arrays, out_shapes):
    moved = [math.prod(array.shape) * array.dtype.itemsize for array in arrays]
    moved += [math.prod(shape) * jnp.dtype(kind).itemsize for shape, kind in out_shapes]
    return pl.CostEstimate(flops=flops, bytes_accessed=sum(moved), transcendentals=0)


def held_call(at, kernel, weights, which, arrays, out_shapes):
    blocks, sources = [], []
    for key, parts in weights.items():
        blocks.append((key, len(sources), [part.shape[0] for part in parts]))
        sources += parts
    _, size, quarter = sources[0].shape
    place = jnp.stack([at.z, at.y, at.core, jnp.int32(at.rows)]).astype(jnp.int32)
    vmem = pl.BlockSpec(memory_space=pltpu.VMEM)
    low = jnp.bfloat16

    def body(place, *refs):
        ins, refs = refs[: len(arrays)], refs[len(arrays) :]
        given, refs = refs[: len(sources)], refs[len(sources) :]
        outs, (held, sems) = refs[: len(out_shapes)], refs[len(out_shapes) :]
        kernel(Held(place, blocks, given, which, held, sems), ins, outs)

    return pl.pallas_call(
        body,
        in_specs=[pl.BlockSpec(memory_space=pltpu.SMEM)]
        + [vmem] * len(arrays)
        + [pl.BlockSpec(memory_space=pl.ANY)] * len(sources),
        out_specs=[vmem] * len(out_shapes),
        out_shape=[jax.ShapeDtypeStruct(shape, low) for shape in out_shapes],
        scratch_shapes=[
            pltpu.VMEM((len(which), len(blocks) * size, quarter), low),
            pltpu.SemaphoreType.DMA((len(which), len(blocks))),
        ],
        compiler_params=pltpu.CompilerParams(vmem_limit_bytes=56 * 2**20),
        cost_estimate=cost_of(
            6 * out_shapes[0][0] * size * len(blocks) * quarter,
            [*arrays, *sources],
            [(shape, low) for shape in out_shapes],
        ),
    )(place, *arrays, *sources)


def forward(at, weights, normed):
    rows_own, width = normed[0].shape
    quarter = next(iter(weights.values()))[0].shape[-1]
    count = len(normed) // 2
    half = width // 2

    def kernel(held, normed, outs):
        hidden_ref, silu_ref, slope_ref, *out_refs = outs
        for k in range(count):
            here = slice(2 * k * rows_own, 2 * (k + 1) * rows_own)
            own = slice(k * rows_own, (k + 1) * rows_own)
            rows = jnp.concatenate([normed[2 * k][...], normed[2 * k + 1][...]], 0)
            if k == 0:
                held.wait(0)
            gate = product(rows, held.held[0], NN)
            if k == 0:
                held.wait(1)
            up = product(rows, held.held[1], NN)
            sigmoid_gate = jax.nn.sigmoid(gate)
            silu_gate = gate * sigmoid_gate
            hidden = (silu_gate * up).astype(jnp.bfloat16)
            hidden_ref[here] = hidden
            silu_ref[here] = silu_gate.astype(jnp.bfloat16)
            slope = up * sigmoid_gate * (1.0 + gate * (1.0 - sigmoid_gate))
            slope_ref[here] = slope.astype(jnp.bfloat16)
            if k == 0:
                held.wait(2)
            out = product(hidden, held.held[2], NT).astype(jnp.bfloat16)
            for i in range(2):
                columns = slice(i * half, (i + 1) * half)
                out_refs[2 * i][own] = out[:rows_own, columns]
                out_refs[2 * i + 1][own] = out[rows_own:, columns]

    shapes = [(2 * count * rows_own, quarter)] * 3 + [(count * rows_own, half)] * 4
    return held_call(at, kernel, weights, (0, 1, 2), normed, shapes)


def backward(at, weights, grads, silu, slope):
    rows_own, width = grads[0].shape
    count = len(grads) // 2

    def kernel(held, ins, outs):
        *grads, silu, slope = ins
        gate_ref, up_ref, *back = outs
        for k in range(count):
            here = slice(2 * k * rows_own, 2 * (k + 1) * rows_own)
            rows = jnp.concatenate([grads[2 * k][...], grads[2 * k + 1][...]], 0)
            if k == 0:
                held.wait(0)
            grad_hidden = product(rows, held.held[0], NN)
            grad_gate = (grad_hidden * slope[here]).astype(jnp.bfloat16)
            grad_up = (grad_hidden * silu[here]).astype(jnp.bfloat16)
            gate_ref[here] = grad_gate
            up_ref[here] = grad_up
            if k == 0:
                held.wait(1)
            total = product(grad_gate, held.held[1], NT)
            if k == 0:
                held.wait(2)
            total = (total + product(grad_up, held.held[2], NT)).astype(jnp.bfloat16)
            back[2 * k][...] = total[:rows_own]
            back[2 * k + 1][...] = total[rows_own:]

    shapes = [silu.shape] * 2 + [(rows_own, width)] * (2 * count)
    return held_call(at, kernel, weights, (2, 0, 1), [*grads, silu, slope], shapes)


def weight_grad_kernel(place, *refs):
    core = place[0]
    *left, right, own_ref, other_ref = refs
    rows = jnp.concatenate([ref[...] for ref in left], 0)
    total = product(rows, right[...], TN).astype(jnp.bfloat16)
    chips, _, own_features, quarter = own_ref.shape
    total = total.reshape(chips, CORES, own_features, quarter)
    own_ref[:, 0] = jnp.where(core == 0, total[:, 0], total[:, 1])
    other_ref[:, 0] = jnp.where(core == 0, total[:, 1], total[:, 0])


def weight_grad(at, left, right, own_features):
    rows, width = left[0].shape
    quarter = right.shape[-1]
    place = jnp.stack([at.core]).astype(jnp.int32)
    shape = (at.rows, at.planes, own_features, quarter)
    block = (at.rows, 1, own_features, quarter)
    left_spec = pl.BlockSpec((rows, width // at.planes), lambda i, place: (0, i))
    return pl.pallas_call(
        weight_grad_kernel,
        grid_spec=pltpu.PrefetchScalarGridSpec(
            num_scalar_prefetch=1,
            grid=(at.planes,),
            in_specs=[left_spec] * len(left) + [pl.BlockSpec(right.shape, lambda i, place: (0, 0))],
            out_specs=[pl.BlockSpec(block, lambda i, place: (0, i, 0, 0))] * 2,
        ),
        out_shape=[jax.ShapeDtypeStruct(shape, jnp.bfloat16)] * 2,
        compiler_params=pltpu.CompilerParams(vmem_limit_bytes=56 * 2**20),
        cost_estimate=cost_of(
            2 * len(left) * rows * width * quarter,
            [*left, right],
            [(shape, right.dtype)] * 2,
        ),
    )(place, *left, right)


class Rotation:
    def __init__(self, cosine, sine):
        self.cosine, self.sine = cosine[...], sine[...]
        lanes = lax.broadcasted_iota(jnp.int32, self.cosine.shape, 1)
        self.first_half = lax.rem(lanes, HEAD_WIDTH) < HEAD_WIDTH // 2

    def turned(self, pair):
        quarter = HEAD_WIDTH // 2
        return pltpu.roll(pair, 2 * HEAD_WIDTH - quarter, 1), pltpu.roll(pair, quarter, 1)

    def forward(self, pair):
        ahead, behind = self.turned(pair)
        return pair * self.cosine + jnp.where(self.first_half, -ahead, behind) * self.sine

    def backward(self, pair):
        ahead, behind = self.turned(pair * self.sine)
        return pair * self.cosine + jnp.where(self.first_half, ahead, -behind)


class Whole:
    def __init__(self, place, keys, sources, held, sems):
        core, z, y, rows = (place[i] for i in range(1, 5))
        self.held = held
        self.copies = []
        for n, (mask, back, other) in enumerate(keys):
            chip = lax.rem(y + rows - back, rows)
            here = held.at[z ^ mask, chip, core ^ other]
            self.copies.append(pltpu.make_async_copy(sources[n], here, sems.at[n]))
        for copy in self.copies:
            copy.start()

    def wait(self):
        for copy in self.copies:
            copy.wait()

    def columns(self, at_columns):
        part = self.held[:, :, :, :, at_columns]
        return part.reshape(-1, part.shape[-1])


def by_x(x, own, other):
    first = jnp.where(x == 0, own[...], other[...])
    second = jnp.where(x == 0, other[...], own[...])
    return jnp.concatenate([first, second], 0)


def allowed_keys(segment, segment_row, per_group):
    rows = segment.shape[0]
    stacked = (per_group * rows, rows)
    row_ids = lax.rem(lax.broadcasted_iota(jnp.int32, stacked, 0), rows)
    columns = lax.broadcasted_iota(jnp.int32, stacked, 1)
    segments = jnp.concatenate([segment[...]] * per_group, 0)
    return (segments == segment_row[...]) & (columns <= row_ids)


def heads_of(values, group, per_group):
    start = group * per_group
    return jnp.concatenate(
        [
            values[:, (start + i) * HEAD_WIDTH : (start + i + 1) * HEAD_WIDTH]
            for i in range(per_group)
        ],
        0,
    )


def softmax_weights(query, key, allowed):
    scores = jnp.where(allowed, product(query, key, NT) * HEAD_WIDTH ** (-0.5), MASKED)
    exponent = jnp.exp(scores - jnp.max(scores, 1, keepdims=True))
    return exponent / jnp.sum(exponent, 1, keepdims=True)


def attention_kernel(width_kv, keys, place, *refs):
    normed_own, normed_other, segment, segment_row, cosine, sine = refs[:6]
    sources, refs = refs[6 : 6 + len(keys)], refs[6 + len(keys) :]
    query_key, value, attended, branch_own, branch_other, held, sems = refs
    x = place[0]
    low = jnp.bfloat16
    weights_of = Whole(place, keys, sources, held, sems)
    normed = by_x(x, normed_own, normed_other)
    rows_own = normed_own.shape[0]
    rotation = Rotation(cosine, sine)
    width_query = attended.shape[1]
    per_group = width_query // width_kv
    allowed = allowed_keys(segment, segment_row, per_group)
    to_value = slice(width_query + width_kv, width_query + 2 * width_kv)
    to_out = slice(width_query + 2 * width_kv, None)
    weights_of.wait()
    projected = product(normed, weights_of.columns(slice(0, width_query + width_kv)), NN)
    pairs = []
    for start in range(0, projected.shape[1], 2 * HEAD_WIDTH):
        pairs.append(rotation.forward(projected[:, start : start + 2 * HEAD_WIDTH]).astype(low))
    rotated = jnp.concatenate(pairs, 1)
    query_key[...] = rotated
    values = product(normed, weights_of.columns(to_value), NN).astype(low)
    value[...] = values
    heads = []
    for group in range(width_kv // HEAD_WIDTH):
        here = slice(group * HEAD_WIDTH, (group + 1) * HEAD_WIDTH)
        key = rotated[:, width_query:][:, here]
        weights = softmax_weights(heads_of(rotated, group, per_group), key, allowed).astype(low)
        out = product(weights, values[:, here], NN).astype(low)
        rows = rotated.shape[0]
        heads += [out[i * rows : (i + 1) * rows] for i in range(per_group)]
    all_heads = jnp.concatenate(heads, 1)
    attended[...] = all_heads
    branch = product(all_heads, weights_of.columns(to_out), NT)
    first, second = branch[:rows_own], branch[rows_own:]
    branch_own[...] = jnp.where(x == 0, first, second)
    branch_other[...] = jnp.where(x == 0, second, first).astype(low)


def attention_back_kernel(width_kv, keys, place, *refs):
    state_own, state_other, normed_own, normed_other, segment, segment_row, cosine, sine = refs[:8]
    query_key, value, attended = refs[8:11]
    sources, refs = refs[11 : 11 + len(keys)], refs[11 + len(keys) :]
    back_own, back_other, qk_own, qk_other, vo_own, vo_other, held, sems = refs
    x, core = place[0], place[1]
    low = jnp.bfloat16
    weights_of = Whole(place, keys, sources, held, sems)
    scaling = HEAD_WIDTH ** (-0.5)
    state = by_x(x, state_own, state_other)
    normed = by_x(x, normed_own, normed_other)
    rows_own, rows = state_own.shape[0], state.shape[0]
    rotation = Rotation(cosine, sine)
    width_query = attended.shape[1]
    per_group = width_query // width_kv
    allowed = allowed_keys(segment, segment_row, per_group)
    to_value = slice(width_query + width_kv, width_query + 2 * width_kv)
    to_out = slice(width_query + 2 * width_kv, None)
    weights_of.wait()
    grad_attended = product(state, weights_of.columns(to_out), NN).astype(low)

    grad_query, grad_key, grad_value = [], [], []
    for group in range(width_kv // HEAD_WIDTH):
        here = slice(group * HEAD_WIDTH, (group + 1) * HEAD_WIDTH)
        key = query_key[:, width_query:][:, here]
        query, grads = heads_of(query_key, group, per_group), heads_of(grad_attended, group, per_group)
        weights = softmax_weights(query, key, allowed)
        grad_probs = product(grads, value[:, here], NT)
        centered = grad_probs - jnp.sum(weights * grad_probs, 1, keepdims=True)
        grad_scores = (weights * centered).astype(low)
        grad_heads = product(grad_scores, key, NN) * scaling
        grad_query += [grad_heads[i * rows : (i + 1) * rows] for i in range(per_group)]
        grad_key.append(product(grad_scores, query, TN) * scaling)
        grad_value.append(product(weights.astype(low), grads, TN))

    grads = grad_query + grad_key
    grad_qk = jnp.concatenate(
        [
            rotation.backward(jnp.concatenate(grads[n : n + 2], 1)).astype(low)
            for n in range(0, len(grads), 2)
        ],
        1,
    )
    grad_v = jnp.concatenate(grad_value, 1).astype(low)

    own_features = qk_own.shape[1]
    block = max(256, CORES * own_features)
    count = block // (CORES * own_features)
    for start in range(0, normed.shape[1], block):
        features = slice(start, start + block)
        chip = slice(start // (CORES * own_features), start // (CORES * own_features) + count)
        left = normed[:, features]
        for total, own_ref, other_ref, at_columns in (
            (product(left, grad_qk, TN), qk_own, qk_other, slice(None)),
            (product(left, grad_v, TN), vo_own, vo_other, slice(0, width_kv)),
            (product(state[:, features], attended[...], TN), vo_own, vo_other, slice(width_kv, None)),
        ):
            total = total.astype(low).reshape(count, CORES, own_features, total.shape[-1])
            own_ref[chip, :, at_columns] = jnp.where(core == 0, total[:, 0], total[:, 1])
            other_ref[chip, :, at_columns] = jnp.where(core == 0, total[:, 1], total[:, 0])
    back = product(grad_qk, weights_of.columns(slice(0, width_query + width_kv)), NT)
    back = back + product(grad_v, weights_of.columns(to_value), NT)
    first, second = back[:rows_own], back[rows_own:]
    back_own[...] = jnp.where(x == 0, first, second)
    back_other[...] = jnp.where(x == 0, second, first).astype(low)


def attention_call(at, kernel, width_kv, arrays, weights, out_shapes):
    place = jnp.stack([at.x, at.core, at.z, at.y, jnp.int32(at.rows)]).astype(jnp.int32)
    vmem = pl.BlockSpec(memory_space=pltpu.VMEM)
    keys, sources = list(weights), list(weights.values())
    held = pltpu.VMEM((at.planes, at.rows, CORES) + sources[0].shape, sources[0].dtype)
    return pl.pallas_call(
        functools.partial(kernel, width_kv, keys),
        in_specs=[pl.BlockSpec(memory_space=pltpu.SMEM)]
        + [vmem] * len(arrays)
        + [pl.BlockSpec(memory_space=pl.ANY)] * len(sources),
        out_specs=[vmem] * len(out_shapes),
        out_shape=[jax.ShapeDtypeStruct(*shape) for shape in out_shapes],
        scratch_shapes=[held, pltpu.SemaphoreType.DMA((len(keys),))],
        compiler_params=pltpu.CompilerParams(vmem_limit_bytes=56 * 2**20),
        cost_estimate=cost_of(
            2 * len(arrays) * arrays[0].shape[0] * sources[0].size * len(sources) // 2,
            [*arrays, *sources],
            out_shapes,
        ),
    )(place, *arrays, *sources)


def on_device(
    tokens,
    seq_lens,
    norm_gains,
    w_query,
    key_weight,
    value_weight,
    w_out,
    w_gate,
    w_up,
    w_down,
    cotangent,
):
    at = Places(lax.axis_size("dp"))
    rows_own = tokens.shape[0]
    row_count = rows_own * lax.axis_size("tensor")
    width_query = w_query.shape[1]
    width_kv = key_weight.shape[1]
    quarter = w_gate.shape[1] // at.planes
    own_features = w_gate.shape[0]

    row_ids, segment, position, in_use = layout(seq_lens[0], row_count)
    in_use_own = lax.dynamic_slice_in_dim(in_use, at.x * rows_own, rows_own, 0)
    gain_rows = norm_gains.astype(jnp.float32)
    inputs = tokens.astype(jnp.float32)
    scale_one = lax.rsqrt(jnp.mean(inputs * inputs, 1, keepdims=True) + EPSILON)
    normed_own = (inputs * scale_one * gain_rows[0]).astype(jnp.bfloat16)
    normed_other = at.other_x(normed_own)
    grad_mixed = cotangent.astype(jnp.float32) * in_use_own[:, None]
    grad_low_own = grad_mixed.astype(jnp.bfloat16)
    grad_low_mine = lax.all_gather(grad_low_own, "dp", axis_index_groups=at.columns)
    packed = jnp.concatenate([w_query, key_weight, value_weight, w_out], 1)
    others = range(1, at.rows)
    projections = {(0, 0, 0): packed}
    projections[2, 0, 0] = at.across_z(packed, 2)
    projections[1, 0, 0] = at.across_z(packed, 1)
    for j in others:
        projections[0, j, 0] = at.along_y(packed, j)

    stage = [*list(projections.values())[1:], normed_other]
    projections[3, 0, 0] = at.across_z(after(projections[2, 0, 0], *stage), 1)
    for j in others:
        projections[1, j, 0] = at.along_y(after(projections[1, 0, 0], *stage), j)
    grads_low = {(0, 0): grad_low_own, (0, 1): at.other_x(after(grad_low_own, *stage))}
    shares = {}
    for mask in range(at.planes):
        start = (at.z ^ mask) * quarter
        shares[mask] = jnp.stack(
            [lax.dynamic_slice_in_dim(w, start, quarter, 1) for w in (w_gate, w_up, w_down)]
        )
    plane_two = [at.across_z(after(shares[2][:1], *stage), 2)]
    second = [plane_two[0], *(projections[1, j, 0] for j in others)]
    for j in others:
        projections[2, j, 0] = at.along_y(after(projections[2, 0, 0], *second), j)
    plane_two.append(at.across_z(after(shares[2][1:2], *second), 2))
    for mask in (0, 1):
        for j in range(at.rows):
            key = (mask, j, 0)
            if key in projections:
                projections[mask, j, 1] = at.other_core(after(projections[key], *stage))

    stage = [projections[3, 0, 0], grads_low[0, 1], plane_two[1]]
    stage += [projections[2, j, 0] for j in others]
    plane_two.append(at.across_z(after(shares[2][2:], *stage), 2))
    for j in others:
        projections[3, j, 0] = at.along_y(after(projections[3, 0, 0], *stage), j)
    for mask, j in ((1, 1), (2, 0), (2, 1), (3, 0)):
        for back in others if j else (0,):
            if (mask, back, 1) not in projections:
                block = after(projections[mask, back, 0], *stage)
                projections[mask, back, 1] = at.other_core(block)

    stage = [projections[3, j, 0] for j in others] + [plane_two[2]]
    plane_two = jnp.concatenate(plane_two, 0)
    for j in others:
        projections[3, j, 1] = at.other_core(projections[3, j, 0])
    tables = [jnp.concatenate([table, table], 1) for table in rope_tables(position, HEAD_WIDTH)]
    keys_of = [segment[:, None], segment[None, :], *tables]

    weights = {}

    def to_chips(mask, parts, *earlier):
        weights.setdefault((mask, 0, 0), []).extend(parts)
        for j in range(1, at.rows):
            sent = [at.along_y(after(part, *earlier), j) for part in parts]
            weights.setdefault((mask, j, 0), []).extend(sent)
            earlier = tuple(sent)
        return earlier

    plane_three = at.across_z(after(shares[3][:2], plane_two, *stage), 3)
    plane_one = at.across_z(after(shares[1][:2], plane_two, *stage), 1)
    last = to_chips(0, [shares[0]], *stage)

    low = jnp.bfloat16
    query_key, value, attended, branch_own, branch_other = attention_call(
        at,
        attention_kernel,
        width_kv,
        [normed_own, normed_other, *keys_of],
        projections,
        [
            ((row_count, width_query + width_kv), low),
            ((row_count, width_kv), low),
            ((row_count, width_query), low),
            ((rows_own, inputs.shape[1]), jnp.float32),
            ((rows_own, inputs.shape[1]), low),
        ],
    )
    branch_other = after(branch_other, plane_one, plane_three, *last)
    branch = branch_other
    state = inputs + branch_own + at.other_x(branch_other)
    scale_two = lax.rsqrt(jnp.mean(state * state, 1, keepdims=True) + EPSILON)
    normed_two = (state * scale_two * gain_rows[1]).astype(jnp.bfloat16)

    plane_three_last = at.across_z(after(shares[3][2:], branch), 3)
    plane_one_last = at.across_z(after(shares[1][2:], branch), 1)
    last = to_chips(2, [plane_two], *last, branch)

    def to_cores(*keys, earlier):
        for mask, back in keys:
            parts = weights[mask, back, 0]
            weights[mask, back, 1] = [at.other_core(after(part, *earlier)) for part in parts]

    every_row = range(at.rows)
    to_cores(*((0, j) for j in every_row), earlier=[branch])
    stage = [normed_two, plane_three_last, plane_one_last]
    normed = {(0, 0): normed_two, (0, 1): at.other_x(after(normed_two, *stage))}
    normed[2, 0] = at.across_z(after(normed_two, *stage), 2)
    normed[1, 0] = at.across_z(after(normed_two, *stage), 1)
    last = to_chips(1, [plane_one], *last, *stage)
    last = to_chips(3, [plane_three], *last)

    for mask in (1, 2, 3):
        grads_low[mask, 0] = lax.dynamic_index_in_dim(
            grad_low_mine, at.z ^ mask, 0, keepdims=False
        )
    grads_low[1, 1] = at.other_x(after(grads_low[1, 0], *stage))

    stage = [*normed.values(), *last, grads_low[1, 1]]
    normed[3, 0] = at.across_z(after(normed[2, 0], *stage), 1)
    normed[2, 1] = at.other_x(after(normed[2, 0], *stage))
    last = to_chips(1, [plane_one_last], *stage)
    last = to_chips(3, [plane_three_last], *last)
    to_cores(*((2, j) for j in every_row), earlier=stage)

    stage = [normed[3, 0], normed[2, 1], *last]
    normed[3, 1] = at.other_x(after(normed[3, 0], *stage))
    normed[1, 1] = at.across_z(after(normed[0, 1], *stage), 1)
    to_cores(*((1, j) for j in every_row), earlier=stage)
    to_cores(*((3, j) for j in every_row), earlier=stage)
    grads_far = at.other_x(
        after(jnp.stack([grads_low[mask, 0] for mask in (2, 3)]), normed[3, 1])
    )
    grads_low[2, 1], grads_low[3, 1] = grads_far[0], grads_far[1]

    masks = (3, 2, 1, 0)
    normed_rows = [normed[mask, x] for mask in masks for x in range(2)]
    grad_rows = [grads_low[mask, x] for mask in masks for x in range(2)]
    hidden, silu, slope, *outs = forward(at, weights, normed_rows)
    def block_of(value, i):
        return value[i * rows_own : (i + 1) * rows_own]

    def out_block(mine, arrived, i):
        return block_of(mine, i).astype(jnp.float32) + arrived

    def of_chip(own, arrived, j):
        y = (at.y + j) % at.rows
        mine = lax.dynamic_index_in_dim(own, y, 0, keepdims=False)
        theirs = lax.dynamic_index_in_dim(arrived, y, 0, keepdims=False)
        return mine.astype(jnp.float32) + theirs

    def for_chips(own, arrived):
        return [of_chip(own, arrived, j).astype(jnp.bfloat16) for j in range(1, at.rows)]

    def send_chips(away, earlier):
        return [at.along_y(after(a, *earlier), j + 1) for j, a in enumerate(away)]

    def of_plane(terms, mask):
        own, arrived, chips = terms
        size = (1, 1) + own.shape[2:]
        at_plane = (at.y, at.z ^ mask, 0, 0)
        total = lax.dynamic_slice(own, at_plane, size)[0, 0].astype(jnp.float32)
        total = total + lax.dynamic_slice(arrived, at_plane, size)[0, 0]
        for part in chips:
            total = total + lax.dynamic_index_in_dim(part, at.z ^ mask, 0, keepdims=False)
        return total

    def send_planes(terms, wanted, earlier):
        sent = {}
        for mask in wanted:
            piece = of_plane(terms, mask).astype(jnp.bfloat16)
            sent[mask] = at.across_z(after(piece, *earlier), mask)
        return sent

    def all_columns(terms, pieces, *earlier):
        result = jnp.zeros((own_features, at.planes * quarter), jnp.float32)
        own = {0: of_plane(terms, 0)}
        for mask, piece in after({**own, **pieces}, *earlier).items():
            result = lax.dynamic_update_slice(
                result, piece.astype(jnp.float32), (0, (at.z ^ mask) * quarter)
            )
        return result

    grad_gate_in, grad_up_in, *back = backward(at, weights, grad_rows, silu, slope)
    out_first = at.other_x(outs[1])

    def sum_of(i, arrived):
        return back[2 * i].astype(jnp.float32) + arrived

    stage = [out_first, back[0]]
    three = at.other_x(after(back[1], *stage))
    one = at.across_z(after(back[5], *stage), 1)
    gate_own, gate_other = weight_grad(
        at, normed_rows, after(grad_gate_in, *stage), own_features
    )
    first_blocks = [out_block(outs[0], block_of(out_first, i), i) for i in range(4)]
    first_two = at.across_z(after(first_blocks[0].astype(jnp.bfloat16), *stage), 1)

    stage = [three, one, gate_own, first_two]
    to_two = at.across_z(after(sum_of(0, three).astype(jnp.bfloat16), *stage), 1)
    two = at.other_x(after(back[3], *stage))
    gate_arrived = at.other_core(after(gate_other, *stage))
    up_own, up_other = weight_grad(at, normed_rows, after(grad_up_in, *stage), own_features)
    first_zero = (first_blocks[1] + first_two).astype(jnp.bfloat16)
    first_zero = at.across_z(after(first_zero, *stage), 2)

    stage = [to_two, two, gate_arrived, up_own, first_zero]
    for_zero = (sum_of(1, two) + to_two).astype(jnp.bfloat16)
    middle = for_zero.shape[1] // 2
    to_zero_first = at.across_z(after(for_zero[:, :middle], *stage), 2)
    other_zero = (back[7].astype(jnp.float32) + one).astype(jnp.bfloat16)
    zero = at.other_x(after(other_zero, *stage))
    gate_chips = send_chips(for_chips(gate_own, gate_arrived), stage)
    up_arrived = at.other_core(after(up_other, *stage))
    down_own, down_other = weight_grad(at, grad_rows, after(hidden, *stage), own_features)
    first_one = at.across_z(after(first_blocks[2].astype(jnp.bfloat16), *stage), 1)

    stage = [zero, to_zero_first, *gate_chips, up_arrived, down_own, first_one]
    to_zero_second = at.across_z(after(for_zero[:, middle:], *stage), 2)
    from_one = at.across_z(after(back[4], *stage), 1)
    down_arrived = at.other_core(after(down_other, *stage))
    gate_terms = (gate_own, gate_arrived, gate_chips)
    gate_pieces = send_planes(gate_terms, (2,), stage)
    up_chips = send_chips(for_chips(up_own, up_arrived), stage)

    to_zero = jnp.concatenate([to_zero_first, to_zero_second], 1)
    grad_normed_two = sum_of(3, zero) + from_one + to_zero
    hat_two = state * scale_two
    inner_two = grad_normed_two * gain_rows[1]
    grad_state = grad_mixed + scale_two * (
        inner_two - hat_two * jnp.mean(inner_two * hat_two, 1, keepdims=True)
    )
    gain_two = jnp.sum(grad_normed_two * hat_two, 0)
    grad_state_own = grad_state.astype(jnp.bfloat16)

    stage = [grad_state_own, *up_chips, down_arrived, gate_pieces[2]]
    grad_state_other = at.other_x(grad_state_own)
    up_terms = (up_own, up_arrived, up_chips)
    down_chips = send_chips(for_chips(down_own, down_arrived), stage)

    def both(mask):
        return jnp.stack([of_plane(terms, mask).astype(jnp.bfloat16) for terms in (gate_terms, up_terms)])

    up_pieces = send_planes(up_terms, (2,), stage)
    pair_pieces = {mask: at.across_z(after(both(mask), *stage), mask) for mask in (3, 1)}
    out_second = at.other_x(after(outs[3], grad_state_other))
    shape = (at.chips, own_features, width_query + width_kv)
    back_own, back_other, qk_own, qk_other, vo_own, vo_other = attention_call(
        at,
        attention_back_kernel,
        width_kv,
        [
            grad_state_own,
            grad_state_other,
            normed_own,
            normed_other,
            *keys_of,
            query_key,
            value,
            attended,
        ],
        projections,
        [
            ((rows_own, inputs.shape[1]), jnp.float32),
            ((rows_own, inputs.shape[1]), low),
            *[(shape, low)] * 4,
        ],
    )
    stage = [qk_other, out_second, *down_chips, *up_pieces.values(), *pair_pieces.values()]
    for mask, piece in pair_pieces.items():
        gate_pieces[mask], up_pieces[mask] = piece[0], piece[1]

    owns = {"qk": qk_own, "vo": vo_own}
    cores = {
        "qk": at.other_core(after(qk_other, *stage)),
        "vo": at.other_core(after(vo_other, *stage)),
    }
    normed_arrived = at.other_x(after(back_other, *stage))

    def by_place(value):
        return value.reshape(at.planes, at.rows, own_features, -1)

    def for_chip(name, j):
        y = (at.y + j) % at.rows
        parts = [
            lax.dynamic_index_in_dim(by_place(value), y, 1, keepdims=False)
            for value in (owns[name], cores[name])
        ]
        return (parts[0].astype(jnp.float32) + parts[1]).astype(jnp.bfloat16)

    chips = {"qk": [], "vo": []}

    def to_chips_of(name, earlier):
        for j in others:
            chips[name].append(at.along_y(after(for_chip(name, j), *earlier), j))

    def for_plane(name, mask):
        z = at.z ^ mask
        total = 0.0
        for value in (owns[name], cores[name]):
            part = lax.dynamic_slice(by_place(value), (z, at.y, 0, 0), (1, 1) + by_place(value).shape[2:])
            total = total + part[0, 0].astype(jnp.float32)
        for part in chips[name]:
            total = total + lax.dynamic_index_in_dim(part, z, 0, keepdims=False)
        return total

    pairs, quarters = {}, {}

    def to_pair(name, earlier):
        both_planes = jnp.stack([for_plane(name, 1), for_plane(name, 3)]).astype(jnp.bfloat16)
        pairs[name] = at.across_z(after(both_planes, *earlier), 1)

    def to_quarter(name, earlier):
        far = (for_plane(name, 2) + pairs[name][1]).astype(jnp.bfloat16)
        quarters[name] = at.across_z(after(far, *earlier), 2)

    def total_of(name):
        return for_plane(name, 0) + pairs[name][0] + quarters[name]

    down_terms = (down_own, down_arrived, down_chips)
    down_pieces = send_planes(down_terms, (2,), stage)
    second_two = out_block(outs[2], block_of(out_second, 0), 0).astype(jnp.bfloat16)
    second_two = at.across_z(after(second_two, *stage), 1)

    to_chips_of("qk", stage)

    stage = [*chips["qk"], *down_pieces.values(), second_two, normed_arrived]
    to_chips_of("vo", stage)
    to_pair("qk", stage)
    down_pieces.update(send_planes(down_terms, (3,), stage))
    second_zero = out_block(outs[2], block_of(out_second, 1), 1) + second_two
    second_zero = at.across_z(after(second_zero.astype(jnp.bfloat16), *stage), 2)
    grad_normed_one = back_own + normed_arrived
    hat_one = inputs * scale_one
    inner_one = grad_normed_one * gain_rows[0]
    grad_tokens = (
        grad_state
        + scale_one * (inner_one - hat_one * jnp.mean(inner_one * hat_one, 1, keepdims=True))
    ).astype(jnp.bfloat16)
    gain_one = jnp.sum(grad_normed_one * hat_one, 0)
    grad_gains = jnp.stack([gain_one, gain_two])
    grad_gains = grad_gains + at.other_x(grad_gains)
    bits = [1 << i for i in range(at.dp.bit_length() - 1)]
    chip_bits = [bit for bit in bits if CORES <= bit < CORES * at.rows]
    for bit in bits:
        if bit not in chip_bits:
            grad_gains = grad_gains + at.move(grad_gains, lambda d: d ^ bit)

    stage = [*chips["vo"], pairs["qk"], second_zero, grad_gains, *down_pieces.values()]
    down_pieces.update(send_planes(down_terms, (1,), stage))
    to_pair("vo", stage)
    to_quarter("qk", stage)
    second_one = out_block(outs[2], block_of(out_second, 2), 2).astype(jnp.bfloat16)
    second_one = at.across_z(after(second_one, *stage), 1)
    for bit in chip_bits:
        grad_gains = grad_gains + at.move(after(grad_gains, *stage), lambda d: d ^ bit)

    stage = [pairs["vo"], quarters["qk"], second_one]
    to_quarter("vo", stage)
    sum_qk, sum_vo = total_of("qk"), total_of("vo")
    grad_gate = all_columns(gate_terms, gate_pieces, *stage)
    grad_up = all_columns(up_terms, up_pieces, *stage)
    grad_down = all_columns(down_terms, down_pieces, *stage)
    first_sum = first_blocks[3] + first_zero + first_one
    second_sum = out_block(outs[2], block_of(out_second, 3), 3) + second_zero + second_one
    ffn_out = jnp.concatenate([first_sum, second_sum], 1)
    mixed = ((state + ffn_out) * in_use_own[:, None]).astype(jnp.bfloat16)
    return (
        mixed,
        grad_tokens,
        grad_gains,
        sum_qk[:, :width_query],
        sum_qk[:, width_query:],
        sum_vo[:, :width_kv],
        sum_vo[:, width_kv:],
        grad_gate,
        grad_up,
        grad_down,
    )


def solution(mesh):
    in_specs = (
        P(("dp", "tensor"), None),
        P("dp", None),
        P(),
        P("dp", "tensor"),
        P("dp", "tensor"),
        P("dp", "tensor"),
        P("dp", "tensor"),
        P("dp", "tensor"),
        P("dp", "tensor"),
        P("dp", "tensor"),
        P(("dp", "tensor"), None),
    )
    out_specs = (
        P(("dp", "tensor"), None),
        P(("dp", "tensor"), None),
        P(),
        P("dp", "tensor"),
        P("dp", "tensor"),
        P("dp", "tensor"),
        P("dp", "tensor"),
        P("dp", "tensor"),
        P("dp", "tensor"),
        P("dp", "tensor"),
    )
    return jax.shard_map(
        on_device, mesh=mesh, in_specs=in_specs, out_specs=out_specs, check_vma=False
    )
```

```python
import functools
import math

import jax
import jax.numpy as jnp
from jax import lax
from jax.experimental import pallas as pl
from jax.experimental.pallas import tpu as pltpu
from jax.sharding import PartitionSpec as P

HEAD_WIDTH = 64
EPSILON = 1e-05
MASKED = -1e30
CORES = 2
PLANES = 4


def after(value, *earlier):
    return lax.optimization_barrier((value, *earlier))[0]


def layout(lengths, row_count):
    finish = jnp.cumsum(lengths)
    starts = jnp.concatenate([finish - lengths, finish[-1:]])
    row_ids = jnp.arange(row_count, dtype=jnp.int32)
    segment = jnp.sum((row_ids[:, None] >= finish[None, :]).astype(jnp.int32), 1)
    chosen_slot = segment[:, None] == jnp.arange(starts.shape[0], dtype=jnp.int32)[None, :]
    first_row = jnp.sum(jnp.where(chosen_slot, starts[None, :], 0), 1)
    position = row_ids - first_row
    in_use = (segment < lengths.shape[0]).astype(jnp.float32)
    return (row_ids, segment, position, in_use)


def rope_tables(position, head_size):
    halfway = head_size // 2
    ladder = jnp.arange(halfway, dtype=jnp.float32)
    inverse = 1.0 / 500000.0 ** (ladder * 2.0 / head_size)
    wavelength = 2.0 * math.pi / inverse
    smooth = (8192.0 / wavelength - 1.0) / 3.0
    blended = (1.0 - smooth) * inverse / 32.0 + smooth * inverse
    scaled = jnp.where(
        wavelength > 8192.0, inverse / 32.0, jnp.where(wavelength < 2048.0, inverse, blended)
    )
    angles = position.astype(jnp.float32)[:, None] * scaled[None, :]
    cosine_lookup = jnp.cos(angles)
    sine_lookup = jnp.sin(angles)
    return (
        jnp.concatenate([cosine_lookup, cosine_lookup], 1),
        jnp.concatenate([sine_lookup, sine_lookup], 1),
    )


class Places:
    def __init__(self, dp):
        self.dp = dp
        self.planes = PLANES
        self.rows = dp // (PLANES * CORES)
        self.chips = dp // CORES
        index = lax.axis_index("dp")
        self.z = index // (self.rows * CORES)
        self.y = (index // CORES) % self.rows
        self.core = index % CORES
        self.x = lax.axis_index("tensor")

    def move(self, value, target):
        return lax.ppermute(value, "dp", [(d, target(d)) for d in range(self.dp)])

    def across_z(self, value, mask):
        stride = self.rows * CORES
        return self.move(value, lambda d: d ^ (mask * stride))

    def along_y(self, value, steps):
        def target(d):
            y = (d // CORES) % self.rows
            return d + ((y + steps) % self.rows - y) * CORES

        return self.move(value, target)

    def other_core(self, value):
        return self.move(value, lambda d: d ^ 1)

    def other_x(self, value):
        return lax.ppermute(value, "tensor", [(0, 1), (1, 0)])


def product(left_side, right_side, contract):
    return lax.dot_general(
        left_side, right_side, (contract, ((), ())), preferred_element_type=jnp.float32
    )


NN = ((1,), (0,))
NT = ((1,), (1,))
TN = ((0,), (0,))


class Held:
    def __init__(self, place, blocks, sources, which, held, sems):
        self.z, self.y, self.core, self.rows = (place[i] for i in range(4))
        self.blocks, self.sources, self.which = blocks, sources, which
        self.held, self.sems = held, sems
        for i in range(len(which)):
            for n in range(len(blocks)):
                self.copy(i, n).start()

    def copy(self, i, n):
        (mask, back, other), first, counts = self.blocks[n]
        source, within = first, self.which[i]
        for count in counts:
            if within < count:
                break
            source, within = source + 1, within - count
        size = self.sources[source].shape[1]
        chip = (self.z ^ mask) * self.rows + lax.rem(self.y + self.rows - back, self.rows)
        start = pl.multiple_of((chip * CORES + (self.core ^ other)) * size, size)
        return pltpu.make_async_copy(
            self.sources[source].at[within], self.held.at[i, pl.ds(start, size)], self.sems.at[i, n]
        )

    def wait(self, i):
        for n in range(len(self.blocks)):
            self.copy(i, n).wait()


def cost_of(flops, arrays, out_shapes):
    moved = [math.prod(array.shape) * array.dtype.itemsize for array in arrays]
    moved += [math.prod(shape) * jnp.dtype(kind).itemsize for shape, kind in out_shapes]
    return pl.CostEstimate(flops=flops, bytes_accessed=sum(moved), transcendentals=0)


def held_call(at, kernel, weights, which, arrays, out_shapes):
    blocks, sources = [], []
    for key, parts in weights.items():
        blocks.append((key, len(sources), [part.shape[0] for part in parts]))
        sources += parts
    _, size, quarter = sources[0].shape
    place = jnp.stack([at.z, at.y, at.core, jnp.int32(at.rows)]).astype(jnp.int32)
    vmem = pl.BlockSpec(memory_space=pltpu.VMEM)
    low = jnp.bfloat16

    def body(place, *refs):
        ins, refs = refs[: len(arrays)], refs[len(arrays) :]
        given, refs = refs[: len(sources)], refs[len(sources) :]
        outs, (held, sems) = refs[: len(out_shapes)], refs[len(out_shapes) :]
        kernel(Held(place, blocks, given, which, held, sems), ins, outs)

    return pl.pallas_call(
        body,
        in_specs=[pl.BlockSpec(memory_space=pltpu.SMEM)]
        + [vmem] * len(arrays)
        + [pl.BlockSpec(memory_space=pl.ANY)] * len(sources),
        out_specs=[vmem] * len(out_shapes),
        out_shape=[jax.ShapeDtypeStruct(shape, low) for shape in out_shapes],
        scratch_shapes=[
            pltpu.VMEM((len(which), len(blocks) * size, quarter), low),
            pltpu.SemaphoreType.DMA((len(which), len(blocks))),
        ],
        compiler_params=pltpu.CompilerParams(vmem_limit_bytes=56 * 2**20),
        cost_estimate=cost_of(
            6 * out_shapes[0][0] * size * len(blocks) * quarter,
            [*arrays, *sources],
            [(shape, low) for shape in out_shapes],
        ),
    )(place, *arrays, *sources)


def forward(at, weights, normed):
    rows_own, width = normed[0].shape
    quarter = next(iter(weights.values()))[0].shape[-1]
    count = len(normed) // 2
    half = width // 2

    def kernel(held, normed, outs):
        hidden_ref, silu_ref, slope_ref, *out_refs = outs
        held.wait(0)
        held.wait(1)

        def block(k, rows):
            here = pl.ds(pl.multiple_of(2 * k * rows_own, rows_own), 2 * rows_own)
            own = pl.ds(pl.multiple_of(k * rows_own, rows_own), rows_own)
            gate = product(rows, held.held[0], NN)
            up = product(rows, held.held[1], NN)
            sigmoid_gate = jax.nn.sigmoid(gate)
            silu_gate = gate * sigmoid_gate
            hidden = (silu_gate * up).astype(jnp.bfloat16)
            hidden_ref[here] = hidden
            silu_ref[here] = silu_gate.astype(jnp.bfloat16)
            slope = up * sigmoid_gate * (1.0 + gate * (1.0 - sigmoid_gate))
            slope_ref[here] = slope.astype(jnp.bfloat16)

            @pl.when(k == 0)
            def _():
                held.wait(2)

            out = product(hidden, held.held[2], NT).astype(jnp.bfloat16)
            for i in range(2):
                columns = slice(i * half, (i + 1) * half)
                out_refs[2 * i][own] = out[:rows_own, columns]
                out_refs[2 * i + 1][own] = out[rows_own:, columns]

        @pl.loop(0, count)
        def _(k):
            rows = jnp.concatenate([normed[0][...], normed[1][...]], 0)
            for i in range(1, count):
                other = jnp.concatenate([normed[2 * i][...], normed[2 * i + 1][...]], 0)
                rows = jnp.where(k == i, other, rows)
            block(k, rows)

    shapes = [(2 * count * rows_own, quarter)] * 3 + [(count * rows_own, half)] * 4
    return held_call(at, kernel, weights, (0, 1, 2), normed, shapes)


def backward(at, weights, grads, silu, slope):
    rows_own, width = grads[0].shape
    count = len(grads) // 2

    def kernel(held, ins, outs):
        *grads, silu, slope = ins
        gate_ref, up_ref, *back = outs
        for k in range(count):
            here = slice(2 * k * rows_own, 2 * (k + 1) * rows_own)
            rows = jnp.concatenate([grads[2 * k][...], grads[2 * k + 1][...]], 0)
            if k == 0:
                held.wait(0)
            grad_hidden = product(rows, held.held[0], NN)
            grad_gate = (grad_hidden * slope[here]).astype(jnp.bfloat16)
            grad_up = (grad_hidden * silu[here]).astype(jnp.bfloat16)
            gate_ref[here] = grad_gate
            up_ref[here] = grad_up
            if k == 0:
                held.wait(1)
            total = product(grad_gate, held.held[1], NT)
            if k == 0:
                held.wait(2)
            total = (total + product(grad_up, held.held[2], NT)).astype(jnp.bfloat16)
            back[2 * k][...] = total[:rows_own]
            back[2 * k + 1][...] = total[rows_own:]

    shapes = [silu.shape] * 2 + [(rows_own, width)] * (2 * count)
    return held_call(at, kernel, weights, (2, 0, 1), [*grads, silu, slope], shapes)


def weight_grad_kernel(place, *refs):
    core = place[0]
    *left, right, own_ref, other_ref = refs
    rows = jnp.concatenate([ref[...] for ref in left], 0)
    total = product(rows, right[...], TN).astype(jnp.bfloat16)
    chips, _, own_features, quarter = own_ref.shape
    total = total.reshape(chips, CORES, own_features, quarter)
    own_ref[:, 0] = jnp.where(core == 0, total[:, 0], total[:, 1])
    other_ref[:, 0] = jnp.where(core == 0, total[:, 1], total[:, 0])


def weight_grad(at, left, right, own_features):
    rows, width = left[0].shape
    quarter = right.shape[-1]
    place = jnp.stack([at.core]).astype(jnp.int32)
    shape = (at.rows, at.planes, own_features, quarter)
    block = (at.rows, 1, own_features, quarter)
    left_spec = pl.BlockSpec((rows, width // at.planes), lambda i, place: (0, i))
    return pl.pallas_call(
        weight_grad_kernel,
        grid_spec=pltpu.PrefetchScalarGridSpec(
            num_scalar_prefetch=1,
            grid=(at.planes,),
            in_specs=[left_spec] * len(left) + [pl.BlockSpec(right.shape, lambda i, place: (0, 0))],
            out_specs=[pl.BlockSpec(block, lambda i, place: (0, i, 0, 0))] * 2,
        ),
        out_shape=[jax.ShapeDtypeStruct(shape, jnp.bfloat16)] * 2,
        compiler_params=pltpu.CompilerParams(vmem_limit_bytes=56 * 2**20),
        cost_estimate=cost_of(
            2 * len(left) * rows * width * quarter,
            [*left, right],
            [(shape, right.dtype)] * 2,
        ),
    )(place, *left, right)


class Rotation:
    def __init__(self, cosine, sine):
        self.cosine, self.sine = cosine[...], sine[...]
        lanes = lax.broadcasted_iota(jnp.int32, self.cosine.shape, 1)
        self.first_half = lax.rem(lanes, HEAD_WIDTH) < HEAD_WIDTH // 2

    def turned(self, pair):
        quarter = HEAD_WIDTH // 2
        return pltpu.roll(pair, 2 * HEAD_WIDTH - quarter, 1), pltpu.roll(pair, quarter, 1)

    def forward(self, pair):
        ahead, behind = self.turned(pair)
        return pair * self.cosine + jnp.where(self.first_half, -ahead, behind) * self.sine

    def backward(self, pair):
        ahead, behind = self.turned(pair * self.sine)
        return pair * self.cosine + jnp.where(self.first_half, ahead, -behind)


class Whole:
    def __init__(self, place, keys, sources, held, sems):
        core, z, y, rows = (place[i] for i in range(1, 5))
        self.held = held
        self.copies = []
        for n, (mask, back, other) in enumerate(keys):
            chip = lax.rem(y + rows - back, rows)
            here = held.at[z ^ mask, chip, core ^ other]
            self.copies.append(pltpu.make_async_copy(sources[n], here, sems.at[n]))
        for copy in self.copies:
            copy.start()

    def wait(self):
        for copy in self.copies:
            copy.wait()

    def columns(self, at_columns):
        part = self.held[:, :, :, :, at_columns]
        return part.reshape(-1, part.shape[-1])


def by_x(x, own, other):
    first = jnp.where(x == 0, own[...], other[...])
    second = jnp.where(x == 0, other[...], own[...])
    return jnp.concatenate([first, second], 0)


def allowed_keys(segment, segment_row, per_group):
    rows = segment.shape[0]
    stacked = (per_group * rows, rows)
    row_ids = lax.rem(lax.broadcasted_iota(jnp.int32, stacked, 0), rows)
    columns = lax.broadcasted_iota(jnp.int32, stacked, 1)
    segments = jnp.concatenate([segment[...]] * per_group, 0)
    return (segments == segment_row[...]) & (columns <= row_ids)


def heads_of(values, group, per_group):
    start = group * per_group
    return jnp.concatenate(
        [
            values[:, (start + i) * HEAD_WIDTH : (start + i + 1) * HEAD_WIDTH]
            for i in range(per_group)
        ],
        0,
    )


def softmax_weights(query, key, allowed):
    scores = jnp.where(allowed, product(query, key, NT) * HEAD_WIDTH ** (-0.5), MASKED)
    exponent = jnp.exp(scores - jnp.max(scores, 1, keepdims=True))
    return exponent / jnp.sum(exponent, 1, keepdims=True)


def attention_kernel(width_kv, keys, place, *refs):
    normed_own, normed_other, segment, segment_row, cosine, sine = refs[:6]
    sources, refs = refs[6 : 6 + len(keys)], refs[6 + len(keys) :]
    query_key, value, attended, branch_own, branch_other, held, sems = refs
    x = place[0]
    low = jnp.bfloat16
    weights_of = Whole(place, keys, sources, held, sems)
    normed = by_x(x, normed_own, normed_other)
    rows_own = normed_own.shape[0]
    rotation = Rotation(cosine, sine)
    width_query = attended.shape[1]
    per_group = width_query // width_kv
    allowed = allowed_keys(segment, segment_row, per_group)
    to_value = slice(width_query + width_kv, width_query + 2 * width_kv)
    to_out = slice(width_query + 2 * width_kv, None)
    weights_of.wait()
    projected = product(normed, weights_of.columns(slice(0, width_query + width_kv)), NN)
    pairs = []
    for start in range(0, projected.shape[1], 2 * HEAD_WIDTH):
        pairs.append(rotation.forward(projected[:, start : start + 2 * HEAD_WIDTH]).astype(low))
    rotated = jnp.concatenate(pairs, 1)
    query_key[...] = rotated
    values = product(normed, weights_of.columns(to_value), NN).astype(low)
    value[...] = values
    heads = []
    for group in range(width_kv // HEAD_WIDTH):
        here = slice(group * HEAD_WIDTH, (group + 1) * HEAD_WIDTH)
        key = rotated[:, width_query:][:, here]
        weights = softmax_weights(heads_of(rotated, group, per_group), key, allowed).astype(low)
        out = product(weights, values[:, here], NN).astype(low)
        rows = rotated.shape[0]
        heads += [out[i * rows : (i + 1) * rows] for i in range(per_group)]
    all_heads = jnp.concatenate(heads, 1)
    attended[...] = all_heads
    branch = product(all_heads, weights_of.columns(to_out), NT)
    first, second = branch[:rows_own], branch[rows_own:]
    branch_own[...] = jnp.where(x == 0, first, second)
    branch_other[...] = jnp.where(x == 0, second, first).astype(low)


def attention_back_kernel(width_kv, keys, place, *refs):
    state_own, state_other, normed_own, normed_other, segment, segment_row, cosine, sine = refs[:8]
    query_key, value, attended = refs[8:11]
    sources, refs = refs[11 : 11 + len(keys)], refs[11 + len(keys) :]
    back_own, back_other, qk_own, qk_other, vo_own, vo_other, held, sems = refs
    x, core = place[0], place[1]
    low = jnp.bfloat16
    weights_of = Whole(place, keys, sources, held, sems)
    scaling = HEAD_WIDTH ** (-0.5)
    state = by_x(x, state_own, state_other)
    normed = by_x(x, normed_own, normed_other)
    rows_own, rows = state_own.shape[0], state.shape[0]
    rotation = Rotation(cosine, sine)
    width_query = attended.shape[1]
    per_group = width_query // width_kv
    allowed = allowed_keys(segment, segment_row, per_group)
    to_value = slice(width_query + width_kv, width_query + 2 * width_kv)
    to_out = slice(width_query + 2 * width_kv, None)
    weights_of.wait()
    grad_attended = product(state, weights_of.columns(to_out), NN).astype(low)

    grad_query, grad_key, grad_value = [], [], []
    for group in range(width_kv // HEAD_WIDTH):
        here = slice(group * HEAD_WIDTH, (group + 1) * HEAD_WIDTH)
        key = query_key[:, width_query:][:, here]
        query, grads = heads_of(query_key, group, per_group), heads_of(grad_attended, group, per_group)
        weights = softmax_weights(query, key, allowed)
        grad_probs = product(grads, value[:, here], NT)
        centered = grad_probs - jnp.sum(weights * grad_probs, 1, keepdims=True)
        grad_scores = (weights * centered).astype(low)
        grad_heads = product(grad_scores, key, NN) * scaling
        grad_query += [grad_heads[i * rows : (i + 1) * rows] for i in range(per_group)]
        grad_key.append(product(grad_scores, query, TN) * scaling)
        grad_value.append(product(weights.astype(low), grads, TN))

    grads = grad_query + grad_key
    grad_qk = jnp.concatenate(
        [
            rotation.backward(jnp.concatenate(grads[n : n + 2], 1)).astype(low)
            for n in range(0, len(grads), 2)
        ],
        1,
    )
    grad_v = jnp.concatenate(grad_value, 1).astype(low)

    own_features = qk_own.shape[1]
    block = max(256, CORES * own_features)
    count = block // (CORES * own_features)
    for start in range(0, normed.shape[1], block):
        features = slice(start, start + block)
        chip = slice(start // (CORES * own_features), start // (CORES * own_features) + count)
        left = normed[:, features]
        for total, own_ref, other_ref, at_columns in (
            (product(left, grad_qk, TN), qk_own, qk_other, slice(None)),
            (product(left, grad_v, TN), vo_own, vo_other, slice(0, width_kv)),
            (product(state[:, features], attended[...], TN), vo_own, vo_other, slice(width_kv, None)),
        ):
            total = total.astype(low).reshape(count, CORES, own_features, total.shape[-1])
            own_ref[chip, :, at_columns] = jnp.where(core == 0, total[:, 0], total[:, 1])
            other_ref[chip, :, at_columns] = jnp.where(core == 0, total[:, 1], total[:, 0])
    back = product(grad_qk, weights_of.columns(slice(0, width_query + width_kv)), NT)
    back = back + product(grad_v, weights_of.columns(to_value), NT)
    first, second = back[:rows_own], back[rows_own:]
    back_own[...] = jnp.where(x == 0, first, second)
    back_other[...] = jnp.where(x == 0, second, first).astype(low)


def attention_call(at, kernel, width_kv, arrays, weights, out_shapes):
    place = jnp.stack([at.x, at.core, at.z, at.y, jnp.int32(at.rows)]).astype(jnp.int32)
    vmem = pl.BlockSpec(memory_space=pltpu.VMEM)
    keys, sources = list(weights), list(weights.values())
    held = pltpu.VMEM((at.planes, at.rows, CORES) + sources[0].shape, sources[0].dtype)
    return pl.pallas_call(
        functools.partial(kernel, width_kv, keys),
        in_specs=[pl.BlockSpec(memory_space=pltpu.SMEM)]
        + [vmem] * len(arrays)
        + [pl.BlockSpec(memory_space=pl.ANY)] * len(sources),
        out_specs=[vmem] * len(out_shapes),
        out_shape=[jax.ShapeDtypeStruct(*shape) for shape in out_shapes],
        scratch_shapes=[held, pltpu.SemaphoreType.DMA((len(keys),))],
        compiler_params=pltpu.CompilerParams(vmem_limit_bytes=56 * 2**20),
        cost_estimate=cost_of(
            2 * len(arrays) * arrays[0].shape[0] * sources[0].size * len(sources) // 2,
            [*arrays, *sources],
            out_shapes,
        ),
    )(place, *arrays, *sources)


def side_by_side(*arrays):
    def kernel(*refs):
        start = 0
        for ref in refs[:-1]:
            refs[-1][:, start : start + ref.shape[1]] = ref[...]
            start += ref.shape[1]

    vmem = pl.BlockSpec(memory_space=pltpu.VMEM)
    shape = (arrays[0].shape[0], sum(array.shape[1] for array in arrays))
    return pl.pallas_call(
        kernel,
        in_specs=[vmem] * len(arrays),
        out_specs=vmem,
        out_shape=jax.ShapeDtypeStruct(shape, arrays[0].dtype),
        cost_estimate=cost_of(0, arrays, [(shape, arrays[0].dtype)]),
    )(*arrays)


def on_device(
    tokens,
    seq_lens,
    norm_gains,
    w_query,
    key_weight,
    value_weight,
    w_out,
    w_gate,
    w_up,
    w_down,
    cotangent,
):
    at = Places(lax.axis_size("dp"))
    rows_own = tokens.shape[0]
    row_count = rows_own * lax.axis_size("tensor")
    width_query = w_query.shape[1]
    width_kv = key_weight.shape[1]
    quarter = w_gate.shape[1] // at.planes
    own_features = w_gate.shape[0]

    row_ids, segment, position, in_use = layout(seq_lens[0], row_count)
    in_use_own = lax.dynamic_slice_in_dim(in_use, at.x * rows_own, rows_own, 0)
    gain_rows = norm_gains.astype(jnp.float32)
    inputs = tokens.astype(jnp.float32)
    scale_one = lax.rsqrt(jnp.mean(inputs * inputs, 1, keepdims=True) + EPSILON)
    normed_own = (inputs * scale_one * gain_rows[0]).astype(jnp.bfloat16)
    normed_other = at.other_x(normed_own)
    grad_mixed = cotangent.astype(jnp.float32) * in_use_own[:, None]
    grad_low_own = grad_mixed.astype(jnp.bfloat16)
    packed = side_by_side(w_query, key_weight, value_weight, w_out)
    others = range(1, at.rows)
    projections = {(0, 0, 0): packed}
    projections[2, 0, 0] = at.across_z(packed, 2)
    projections[1, 0, 0] = at.across_z(packed, 1)
    for j in others:
        projections[0, j, 0] = at.along_y(packed, j)

    stage = [*list(projections.values())[1:], normed_other]
    projections[3, 0, 0] = at.across_z(after(projections[2, 0, 0], *stage), 1)
    for j in others:
        projections[1, j, 0] = at.along_y(after(projections[1, 0, 0], *stage), j)
    grads_low = {(0, 0): grad_low_own, (0, 1): at.other_x(after(grad_low_own, *stage))}
    shares = {}
    for mask in range(at.planes):
        start = (at.z ^ mask) * quarter
        shares[mask] = jnp.stack(
            [lax.dynamic_slice_in_dim(w, start, quarter, 1) for w in (w_gate, w_up, w_down)]
        )
    plane_two = [at.across_z(after(shares[2][:1], *stage), 2)]
    second = [plane_two[0], *(projections[1, j, 0] for j in others)]
    for j in others:
        projections[2, j, 0] = at.along_y(after(projections[2, 0, 0], *second), j)
    plane_two.append(at.across_z(after(shares[2][1:2], *second), 2))
    for mask in (0, 1):
        for j in range(at.rows):
            key = (mask, j, 0)
            if key in projections:
                projections[mask, j, 1] = at.other_core(after(projections[key], *stage))

    middle = grad_low_own.shape[1] // 2
    stage = [projections[3, 0, 0], grads_low[0, 1], plane_two[1]]
    stage += [projections[2, j, 0] for j in others]
    plane_two.append(at.across_z(after(shares[2][2:], *stage), 2))
    grads_low[1, 0] = at.across_z(after(grad_low_own, *stage), 1)
    for j in others:
        projections[3, j, 0] = at.along_y(after(projections[3, 0, 0], *stage), j)
    for mask, j in ((1, 1), (2, 0), (2, 1), (3, 0)):
        for back in others if j else (0,):
            if (mask, back, 1) not in projections:
                block = after(projections[mask, back, 0], *stage)
                projections[mask, back, 1] = at.other_core(block)

    stage = [projections[3, j, 0] for j in others] + [plane_two[2], grads_low[1, 0]]
    plane_two = jnp.concatenate(plane_two, 0)
    low_first = at.across_z(after(grad_low_own[:, :middle], *stage), 2)
    for j in others:
        projections[3, j, 1] = at.other_core(projections[3, j, 0])
    tables = [jnp.concatenate([table, table], 1) for table in rope_tables(position, HEAD_WIDTH)]
    keys_of = [segment[:, None], segment[None, :], *tables]

    weights = {}

    def to_chips(mask, parts, *earlier):
        weights.setdefault((mask, 0, 0), []).extend(parts)
        for j in range(1, at.rows):
            sent = [at.along_y(after(part, *earlier), j) for part in parts]
            weights.setdefault((mask, j, 0), []).extend(sent)
            earlier = tuple(sent)
        return earlier

    plane_three = at.across_z(after(shares[3][:2], low_first, *stage), 3)
    plane_one = at.across_z(after(shares[1][:2], low_first, *stage), 1)
    grads_low[1, 1] = at.other_x(after(grads_low[1, 0], *stage))
    last = to_chips(0, [shares[0]], *stage)

    low = jnp.bfloat16
    query_key, value, attended, branch_own, branch_other = attention_call(
        at,
        attention_kernel,
        width_kv,
        [normed_own, normed_other, *keys_of],
        projections,
        [
            ((row_count, width_query + width_kv), low),
            ((row_count, width_kv), low),
            ((row_count, width_query), low),
            ((rows_own, inputs.shape[1]), jnp.float32),
            ((rows_own, inputs.shape[1]), low),
        ],
    )
    branch_other = after(branch_other, plane_one, plane_three, grads_low[1, 1], *last)
    branch = branch_other
    state = inputs + branch_own + at.other_x(branch_other)
    scale_two = lax.rsqrt(jnp.mean(state * state, 1, keepdims=True) + EPSILON)
    normed_two = (state * scale_two * gain_rows[1]).astype(jnp.bfloat16)

    plane_three_last = at.across_z(after(shares[3][2:], branch), 3)
    plane_one_last = at.across_z(after(shares[1][2:], branch), 1)
    low_second = at.across_z(after(grad_low_own[:, middle:], branch), 2)
    last = to_chips(2, [plane_two], *last, branch)

    def to_cores(mask, backs, part, *earlier):
        for back in backs:
            block = after(weights[mask, back, 0][part], *earlier)
            weights.setdefault((mask, back, 1), []).append(at.other_core(block))

    to_cores(0, range(at.rows), 0, branch)
    stage = [normed_two, plane_three_last, plane_one_last, low_second]
    grads_low[2, 0] = jnp.concatenate([low_first, low_second], 1)
    normed = {(0, 0): normed_two, (0, 1): at.other_x(after(normed_two, *stage))}
    normed[2, 0] = at.across_z(after(normed_two, *stage), 2)
    normed[1, 0] = at.across_z(after(normed_two, *stage), 1)
    to_cores(2, (0,), 0, *stage)
    last = to_chips(1, [plane_one], *last, *stage)
    to_cores(1, (0,), 0, *stage)
    last = to_chips(3, [plane_three], *last)
    to_cores(3, (0,), 0, *stage)

    grads_low[2, 1] = at.other_x(after(grads_low[2, 0], normed[0, 1], *stage))

    stage = [*normed.values(), *last, grads_low[2, 1]]
    normed[3, 0] = at.across_z(after(normed[2, 0], *stage), 1)
    normed[2, 1] = at.other_x(after(normed[2, 0], *stage))
    grads_low[3, 0] = at.across_z(after(grads_low[2, 0], *stage), 1)
    for mask in (2, 1, 3):
        to_cores(mask, others, 0, *stage)
    last = to_chips(1, [plane_one_last], *stage) + to_chips(3, [plane_three_last], *stage)
    for mask in (1, 3):
        to_cores(mask, (0,), 1, *stage)

    stage = [normed[3, 0], normed[2, 1], grads_low[3, 0], *last]
    normed[3, 1] = at.other_x(after(normed[3, 0], *stage))
    normed[1, 1] = at.across_z(after(normed[0, 1], *stage), 1)
    for mask in (1, 3):
        to_cores(mask, others, 1, *stage)
    grads_low[3, 1] = at.other_x(after(grads_low[3, 0], normed[3, 1]))

    masks = (3, 2, 1, 0)
    normed_rows = [normed[mask, x] for mask in masks for x in range(2)]
    grad_rows = [grads_low[mask, x] for mask in masks for x in range(2)]
    hidden, silu, slope, *outs = forward(at, weights, normed_rows)
    def block_of(value, i):
        return value[i * rows_own : (i + 1) * rows_own]

    def out_block(mine, arrived, i):
        return block_of(mine, i).astype(jnp.float32) + arrived

    def of_chip(own, arrived, j):
        y = (at.y + j) % at.rows
        mine = lax.dynamic_index_in_dim(own, y, 0, keepdims=False)
        theirs = lax.dynamic_index_in_dim(arrived, y, 0, keepdims=False)
        return mine.astype(jnp.float32) + theirs

    def for_chips(own, arrived):
        return [of_chip(own, arrived, j).astype(jnp.bfloat16) for j in range(1, at.rows)]

    def send_chips(away, earlier):
        return [at.along_y(after(a, *earlier), j + 1) for j, a in enumerate(away)]

    def of_plane(terms, mask):
        own, arrived, chips = terms
        size = (1, 1) + own.shape[2:]
        at_plane = (at.y, at.z ^ mask, 0, 0)
        total = lax.dynamic_slice(own, at_plane, size)[0, 0].astype(jnp.float32)
        total = total + lax.dynamic_slice(arrived, at_plane, size)[0, 0]
        for part in chips:
            total = total + lax.dynamic_index_in_dim(part, at.z ^ mask, 0, keepdims=False)
        return total

    def send_planes(terms, wanted, earlier):
        sent = {}
        for mask in wanted:
            piece = of_plane(terms, mask).astype(jnp.bfloat16)
            sent[mask] = at.across_z(after(piece, *earlier), mask)
        return sent

    def all_columns(terms, pieces, *earlier):
        result = jnp.zeros((own_features, at.planes * quarter), jnp.float32)
        own = {0: of_plane(terms, 0)}
        for mask, piece in after({**own, **pieces}, *earlier).items():
            result = lax.dynamic_update_slice(
                result, piece.astype(jnp.float32), (0, (at.z ^ mask) * quarter)
            )
        return result

    out_first = at.other_x(outs[1])
    down_own, down_other = weight_grad(at, grad_rows, hidden, own_features)
    down_arrived = at.other_core(down_other)
    down_away = for_chips(down_own, down_arrived)
    grad_gate_in, grad_up_in, *back = backward(
        at, weights, grad_rows, after(silu, *down_away), slope
    )
    down_terms = (down_own, down_arrived, send_chips(down_away, ()))

    def sum_of(i, arrived):
        return back[2 * i].astype(jnp.float32) + arrived

    stage = [out_first, back[0], *down_terms[2]]
    three = at.other_x(after(back[1], *stage))
    one = at.across_z(after(back[5], *stage), 1)
    gate_own, gate_other = weight_grad(
        at, normed_rows, after(grad_gate_in, *stage), own_features
    )

    stage = [three, one, gate_own]
    to_two = at.across_z(after(sum_of(0, three).astype(jnp.bfloat16), *stage), 1)
    two = at.other_x(after(back[3], *stage))
    gate_arrived = at.other_core(after(gate_other, *stage))
    up_own, up_other = weight_grad(at, normed_rows, after(grad_up_in, *stage), own_features)

    stage = [to_two, two, gate_arrived, up_own]
    for_zero = (sum_of(1, two) + to_two).astype(jnp.bfloat16)
    middle = for_zero.shape[1] // 2
    to_zero_first = at.across_z(after(for_zero[:, :middle], *stage), 2)
    other_zero = (back[7].astype(jnp.float32) + one).astype(jnp.bfloat16)
    zero = at.other_x(after(other_zero, *stage))
    gate_away = for_chips(gate_own, gate_arrived)
    lower = at.planes // 2
    gate_lower = send_chips([away[:lower] for away in gate_away], stage)
    up_arrived = at.other_core(after(up_other, *stage))

    stage = [zero, to_zero_first, *gate_lower, up_arrived]
    to_zero_second = at.across_z(after(for_zero[:, middle:], *stage), 2)
    from_one = at.across_z(after(back[4], *stage), 1)
    gate_upper = send_chips([away[lower:] for away in gate_away], stage)

    to_zero = jnp.concatenate([to_zero_first, to_zero_second], 1)
    grad_normed_two = sum_of(3, zero) + from_one + to_zero
    hat_two = state * scale_two
    inner_two = grad_normed_two * gain_rows[1]
    grad_state = grad_mixed + scale_two * (
        inner_two - hat_two * jnp.mean(inner_two * hat_two, 1, keepdims=True)
    )
    gain_two = jnp.sum(grad_normed_two * hat_two, 0)
    grad_state_own = grad_state.astype(jnp.bfloat16)

    grad_state_other = at.other_x(grad_state_own)
    stage = [grad_state_own, *gate_upper]
    gate_chips = [jnp.concatenate(parts, 0) for parts in zip(gate_lower, gate_upper, strict=True)]
    gate_terms = (gate_own, gate_arrived, gate_chips)

    def both(mask):
        return jnp.stack(
            [of_plane(terms, mask).astype(jnp.bfloat16) for terms in (gate_terms, down_terms)]
        )

    down_pieces = send_planes(down_terms, (2,), stage)
    late = [*stage, grad_state_other, down_pieces[2]]
    gate_pieces = send_planes(gate_terms, (2,), late)
    pair_pieces = {mask: at.across_z(after(both(mask), *late), mask) for mask in (3, 1)}
    up_chips = send_chips(for_chips(up_own, up_arrived), stage)
    up_terms = (up_own, up_arrived, up_chips)

    out_second = at.other_x(after(outs[3], grad_state_other))
    shape = (at.chips, own_features, width_query + width_kv)
    back_own, back_other, qk_own, qk_other, vo_own, vo_other = attention_call(
        at,
        attention_back_kernel,
        width_kv,
        [
            grad_state_own,
            grad_state_other,
            normed_own,
            normed_other,
            *keys_of,
            after(query_key, *late),
            value,
            attended,
        ],
        projections,
        [
            ((rows_own, inputs.shape[1]), jnp.float32),
            ((rows_own, inputs.shape[1]), low),
            *[(shape, low)] * 4,
        ],
    )
    stage = [qk_other, out_second, *up_chips, gate_pieces[2], *pair_pieces.values()]
    for mask, piece in pair_pieces.items():
        gate_pieces[mask], down_pieces[mask] = piece[0], piece[1]
    out_blocks = [
        jnp.concatenate(
            [
                out_block(outs[2 * n], block_of(arrived, i), i)
                for n, arrived in enumerate((out_first, out_second))
            ],
            1,
        )
        for i in range(4)
    ]

    owns = {"qk": qk_own, "vo": vo_own}
    cores = {
        "qk": at.other_core(after(qk_other, *stage)),
        "vo": at.other_core(after(vo_other, *stage)),
    }

    def by_place(value):
        return value.reshape(at.planes, at.rows, own_features, -1)

    def for_chip(name, j):
        y = (at.y + j) % at.rows
        parts = [
            lax.dynamic_index_in_dim(by_place(value), y, 1, keepdims=False)
            for value in (owns[name], cores[name])
        ]
        return (parts[0].astype(jnp.float32) + parts[1]).astype(jnp.bfloat16)

    chips = {"qk": [], "vo": []}

    def to_chips_of(name, earlier):
        for j in others:
            chips[name].append(at.along_y(after(for_chip(name, j), *earlier), j))

    def for_plane(name, mask):
        z = at.z ^ mask
        total = 0.0
        for value in (owns[name], cores[name]):
            part = lax.dynamic_slice(by_place(value), (z, at.y, 0, 0), (1, 1) + by_place(value).shape[2:])
            total = total + part[0, 0].astype(jnp.float32)
        for part in chips[name]:
            total = total + lax.dynamic_index_in_dim(part, z, 0, keepdims=False)
        return total

    pairs, quarters = {}, {}

    def to_pair(name, earlier):
        both_planes = jnp.stack([for_plane(name, 1), for_plane(name, 3)]).astype(jnp.bfloat16)
        pairs[name] = at.across_z(after(both_planes, *earlier), 1)

    def to_quarter(name, earlier):
        far = (for_plane(name, 2) + pairs[name][1]).astype(jnp.bfloat16)
        quarters[name] = at.across_z(after(far, *earlier), 2)

    def total_of(name):
        return for_plane(name, 0) + pairs[name][0] + quarters[name]

    up_pieces = send_planes(up_terms, (2, 3), stage)
    out_two = at.across_z(after(out_blocks[0].astype(jnp.bfloat16), *stage), 1)
    to_chips_of("qk", ())

    out_one = at.across_z(after(out_blocks[2].astype(jnp.bfloat16), *stage), 1)

    stage = [*chips["qk"], *up_pieces.values(), out_two, out_one]
    normed_arrived = at.other_x(after(back_other, *stage))
    to_chips_of("vo", stage)
    to_pair("qk", stage)
    up_pieces.update(send_planes(up_terms, (1,), stage))
    out_zero = (out_blocks[1] + out_two).astype(jnp.bfloat16)
    out_zero = at.across_z(after(out_zero, *stage), 2)

    stage = [*chips["vo"], pairs["qk"], out_zero, normed_arrived, up_pieces[1]]
    to_pair("vo", stage)
    to_quarter("qk", stage)
    grad_normed_one = back_own + after(normed_arrived, *stage)
    hat_one = inputs * scale_one
    inner_one = grad_normed_one * gain_rows[0]
    grad_tokens = (
        grad_state
        + scale_one * (inner_one - hat_one * jnp.mean(inner_one * hat_one, 1, keepdims=True))
    ).astype(jnp.bfloat16)
    gain_one = jnp.sum(grad_normed_one * hat_one, 0)
    grad_gains = jnp.stack([gain_one, gain_two])
    grad_gains = grad_gains + at.other_x(grad_gains)
    bits = [1 << i for i in range(at.dp.bit_length() - 1)]
    for bit in bits:
        if bit < CORES * at.rows:
            grad_gains = grad_gains + at.move(grad_gains, lambda d: d ^ bit)

    stage = [pairs["vo"], quarters["qk"], grad_gains]
    to_quarter("vo", stage)
    for bit in bits:
        if bit >= CORES * at.rows:
            grad_gains = grad_gains + at.move(after(grad_gains, *stage), lambda d: d ^ bit)
    grad_gate = all_columns(gate_terms, gate_pieces, *stage)
    grad_up = all_columns(up_terms, up_pieces, *stage)
    grad_down = all_columns(down_terms, down_pieces, *stage)
    sum_qk, sum_vo = total_of("qk"), total_of("vo")
    grad_gate = all_columns(gate_terms, gate_pieces, *stage)
    grad_up = all_columns(up_terms, up_pieces, *stage)
    grad_down = all_columns(down_terms, down_pieces, *stage)
    ffn_out = out_blocks[3] + out_zero + out_one
    mixed = ((state + ffn_out) * in_use_own[:, None]).astype(jnp.bfloat16)
    return (
        mixed,
        grad_tokens,
        grad_gains,
        sum_qk[:, :width_query],
        sum_qk[:, width_query:],
        sum_vo[:, :width_kv],
        sum_vo[:, width_kv:],
        grad_gate,
        grad_up,
        grad_down,
    )


def solution(mesh):
    in_specs = (
        P(("dp", "tensor"), None),
        P("dp", None),
        P(),
        P("dp", "tensor"),
        P("dp", "tensor"),
        P("dp", "tensor"),
        P("dp", "tensor"),
        P("dp", "tensor"),
        P("dp", "tensor"),
        P("dp", "tensor"),
        P(("dp", "tensor"), None),
    )
    out_specs = (
        P(("dp", "tensor"), None),
        P(("dp", "tensor"), None),
        P(),
        P("dp", "tensor"),
        P("dp", "tensor"),
        P("dp", "tensor"),
        P("dp", "tensor"),
        P("dp", "tensor"),
        P("dp", "tensor"),
        P("dp", "tensor"),
    )
    return jax.shard_map(
        on_device, mesh=mesh, in_specs=in_specs, out_specs=out_specs, check_vma=False
    )
```

```python
import functools
import math

import jax
import jax.numpy as jnp
from jax import lax
from jax.experimental import pallas as pl
from jax.experimental.pallas import tpu as pltpu
from jax.sharding import PartitionSpec as P

HEAD_WIDTH = 64
EPSILON = 1e-05
MASKED = -1e30
CORES = 2
PLANES = 4


def after(value, *earlier):
    return lax.optimization_barrier((value, *earlier))[0]


def layout(lengths, row_count):
    finish = jnp.cumsum(lengths)
    starts = jnp.concatenate([finish - lengths, finish[-1:]])
    row_ids = jnp.arange(row_count, dtype=jnp.int32)
    segment = jnp.sum((row_ids[:, None] >= finish[None, :]).astype(jnp.int32), 1)
    chosen_slot = segment[:, None] == jnp.arange(starts.shape[0], dtype=jnp.int32)[None, :]
    first_row = jnp.sum(jnp.where(chosen_slot, starts[None, :], 0), 1)
    position = row_ids - first_row
    in_use = (segment < lengths.shape[0]).astype(jnp.float32)
    return (row_ids, segment, position, in_use)


def rope_tables(position, head_size):
    halfway = head_size // 2
    ladder = jnp.arange(halfway, dtype=jnp.float32)
    inverse = 1.0 / 500000.0 ** (ladder * 2.0 / head_size)
    wavelength = 2.0 * math.pi / inverse
    smooth = (8192.0 / wavelength - 1.0) / 3.0
    blended = (1.0 - smooth) * inverse / 32.0 + smooth * inverse
    scaled = jnp.where(
        wavelength > 8192.0, inverse / 32.0, jnp.where(wavelength < 2048.0, inverse, blended)
    )
    angles = position.astype(jnp.float32)[:, None] * scaled[None, :]
    cosine_lookup = jnp.cos(angles)
    sine_lookup = jnp.sin(angles)
    return (
        jnp.concatenate([cosine_lookup, cosine_lookup], 1),
        jnp.concatenate([sine_lookup, sine_lookup], 1),
    )


class Places:
    def __init__(self, dp):
        self.dp = dp
        self.planes = PLANES
        self.rows = dp // (PLANES * CORES)
        self.chips = dp // CORES
        index = lax.axis_index("dp")
        self.z = index // (self.rows * CORES)
        self.y = (index // CORES) % self.rows
        self.core = index % CORES
        self.x = lax.axis_index("tensor")

    def move(self, value, target):
        return lax.ppermute(value, "dp", [(d, target(d)) for d in range(self.dp)])

    def across_z(self, value, mask):
        stride = self.rows * CORES
        return self.move(value, lambda d: d ^ (mask * stride))

    def along_y(self, value, steps):
        def target(d):
            y = (d // CORES) % self.rows
            return d + ((y + steps) % self.rows - y) * CORES

        return self.move(value, target)

    def other_core(self, value):
        return self.move(value, lambda d: d ^ 1)

    def other_x(self, value):
        return lax.ppermute(value, "tensor", [(0, 1), (1, 0)])


def product(left_side, right_side, contract):
    return lax.dot_general(
        left_side, right_side, (contract, ((), ())), preferred_element_type=jnp.float32
    )


NN = ((1,), (0,))
NT = ((1,), (1,))
TN = ((0,), (0,))


class Held:
    def __init__(self, place, blocks, sources, which, held, sems):
        self.z, self.y, self.core, self.rows = (place[i] for i in range(4))
        self.blocks, self.sources, self.which = blocks, sources, which
        self.held, self.sems = held, sems
        for i in range(len(which)):
            for n in range(len(blocks)):
                self.copy(i, n).start()

    def copy(self, i, n):
        (mask, back, other), first, counts = self.blocks[n]
        source, within = first, self.which[i]
        for count in counts:
            if within < count:
                break
            source, within = source + 1, within - count
        size = self.sources[source].shape[1]
        chip = (self.z ^ mask) * self.rows + lax.rem(self.y + self.rows - back, self.rows)
        start = pl.multiple_of((chip * CORES + (self.core ^ other)) * size, size)
        return pltpu.make_async_copy(
            self.sources[source].at[within], self.held.at[i, pl.ds(start, size)], self.sems.at[i, n]
        )

    def wait(self, i):
        for n in range(len(self.blocks)):
            self.copy(i, n).wait()


def cost_of(flops, arrays, out_shapes):
    moved = [math.prod(array.shape) * array.dtype.itemsize for array in arrays]
    moved += [math.prod(shape) * jnp.dtype(kind).itemsize for shape, kind in out_shapes]
    return pl.CostEstimate(flops=flops, bytes_accessed=sum(moved), transcendentals=0)


def held_call(at, kernel, weights, which, arrays, out_shapes):
    blocks, sources = [], []
    for key, parts in weights.items():
        blocks.append((key, len(sources), [part.shape[0] for part in parts]))
        sources += parts
    _, size, quarter = sources[0].shape
    place = jnp.stack([at.z, at.y, at.core, jnp.int32(at.rows)]).astype(jnp.int32)
    vmem = pl.BlockSpec(memory_space=pltpu.VMEM)
    low = jnp.bfloat16

    def body(place, *refs):
        ins, refs = refs[: len(arrays)], refs[len(arrays) :]
        given, refs = refs[: len(sources)], refs[len(sources) :]
        outs, (held, sems) = refs[: len(out_shapes)], refs[len(out_shapes) :]
        kernel(Held(place, blocks, given, which, held, sems), ins, outs)

    return pl.pallas_call(
        body,
        in_specs=[pl.BlockSpec(memory_space=pltpu.SMEM)]
        + [vmem] * len(arrays)
        + [pl.BlockSpec(memory_space=pl.ANY)] * len(sources),
        out_specs=[vmem] * len(out_shapes),
        out_shape=[jax.ShapeDtypeStruct(shape, low) for shape in out_shapes],
        scratch_shapes=[
            pltpu.VMEM((len(which), len(blocks) * size, quarter), low),
            pltpu.SemaphoreType.DMA((len(which), len(blocks))),
        ],
        compiler_params=pltpu.CompilerParams(vmem_limit_bytes=56 * 2**20),
        cost_estimate=cost_of(
            6 * out_shapes[0][0] * size * len(blocks) * quarter,
            [*arrays, *sources],
            [(shape, low) for shape in out_shapes],
        ),
    )(place, *arrays, *sources)


def forward(at, weights, normed):
    rows_own, width = normed[0].shape
    quarter = next(iter(weights.values()))[0].shape[-1]
    count = len(normed) // 2
    half = width // 2

    def kernel(held, normed, outs):
        hidden_ref, silu_ref, slope_ref, *out_refs = outs
        held.wait(0)
        held.wait(1)

        def block(k, rows):
            here = pl.ds(pl.multiple_of(2 * k * rows_own, rows_own), 2 * rows_own)
            own = pl.ds(pl.multiple_of(k * rows_own, rows_own), rows_own)
            gate = product(rows, held.held[0], NN)
            up = product(rows, held.held[1], NN)
            sigmoid_gate = jax.nn.sigmoid(gate)
            silu_gate = gate * sigmoid_gate
            hidden = (silu_gate * up).astype(jnp.bfloat16)
            hidden_ref[here] = hidden
            silu_ref[here] = silu_gate.astype(jnp.bfloat16)
            slope = up * sigmoid_gate * (1.0 + gate * (1.0 - sigmoid_gate))
            slope_ref[here] = slope.astype(jnp.bfloat16)

            @pl.when(k == 0)
            def _():
                held.wait(2)

            out = product(hidden, held.held[2], NT).astype(jnp.bfloat16)
            for i in range(2):
                columns = slice(i * half, (i + 1) * half)
                out_refs[2 * i][own] = out[:rows_own, columns]
                out_refs[2 * i + 1][own] = out[rows_own:, columns]

        @pl.loop(0, count)
        def _(k):
            rows = jnp.concatenate([normed[0][...], normed[1][...]], 0)
            for i in range(1, count):
                other = jnp.concatenate([normed[2 * i][...], normed[2 * i + 1][...]], 0)
                rows = jnp.where(k == i, other, rows)
            block(k, rows)

    shapes = [(2 * count * rows_own, quarter)] * 3 + [(count * rows_own, half)] * 4
    return held_call(at, kernel, weights, (0, 1, 2), normed, shapes)


def backward(at, weights, grads, silu, slope):
    rows_own, width = grads[0].shape
    count = len(grads) // 2

    def kernel(held, ins, outs):
        *grads, silu, slope = ins
        gate_ref, up_ref, *back = outs
        for k in range(count):
            here = slice(2 * k * rows_own, 2 * (k + 1) * rows_own)
            rows = jnp.concatenate([grads[2 * k][...], grads[2 * k + 1][...]], 0)
            if k == 0:
                held.wait(0)
            grad_hidden = product(rows, held.held[0], NN)
            grad_gate = (grad_hidden * slope[here]).astype(jnp.bfloat16)
            grad_up = (grad_hidden * silu[here]).astype(jnp.bfloat16)
            gate_ref[here] = grad_gate
            up_ref[here] = grad_up
            if k == 0:
                held.wait(1)
            total = product(grad_gate, held.held[1], NT)
            if k == 0:
                held.wait(2)
            total = (total + product(grad_up, held.held[2], NT)).astype(jnp.bfloat16)
            back[2 * k][...] = total[:rows_own]
            back[2 * k + 1][...] = total[rows_own:]

    shapes = [silu.shape] * 2 + [(rows_own, width)] * (2 * count)
    return held_call(at, kernel, weights, (2, 0, 1), [*grads, silu, slope], shapes)


def weight_grad_kernel(place, *refs):
    core = place[0]
    *left, right, own_ref, other_ref = refs
    rows = jnp.concatenate([ref[...] for ref in left], 0)
    total = product(rows, right[...], TN).astype(jnp.bfloat16)
    chips, _, own_features, quarter = own_ref.shape
    total = total.reshape(chips, CORES, own_features, quarter)
    own_ref[:, 0] = jnp.where(core == 0, total[:, 0], total[:, 1])
    other_ref[:, 0] = jnp.where(core == 0, total[:, 1], total[:, 0])


def weight_grad(at, left, right, own_features):
    rows, width = left[0].shape
    quarter = right.shape[-1]
    place = jnp.stack([at.core]).astype(jnp.int32)
    shape = (at.rows, at.planes, own_features, quarter)
    block = (at.rows, 1, own_features, quarter)
    left_spec = pl.BlockSpec((rows, width // at.planes), lambda i, place: (0, i))
    return pl.pallas_call(
        weight_grad_kernel,
        grid_spec=pltpu.PrefetchScalarGridSpec(
            num_scalar_prefetch=1,
            grid=(at.planes,),
            in_specs=[left_spec] * len(left) + [pl.BlockSpec(right.shape, lambda i, place: (0, 0))],
            out_specs=[pl.BlockSpec(block, lambda i, place: (0, i, 0, 0))] * 2,
        ),
        out_shape=[jax.ShapeDtypeStruct(shape, jnp.bfloat16)] * 2,
        compiler_params=pltpu.CompilerParams(vmem_limit_bytes=56 * 2**20),
        cost_estimate=cost_of(
            2 * len(left) * rows * width * quarter,
            [*left, right],
            [(shape, right.dtype)] * 2,
        ),
    )(place, *left, right)


class Rotation:
    def __init__(self, cosine, sine):
        self.cosine, self.sine = cosine[...], sine[...]
        lanes = lax.broadcasted_iota(jnp.int32, self.cosine.shape, 1)
        self.first_half = lax.rem(lanes, HEAD_WIDTH) < HEAD_WIDTH // 2

    def turned(self, pair):
        quarter = HEAD_WIDTH // 2
        return pltpu.roll(pair, 2 * HEAD_WIDTH - quarter, 1), pltpu.roll(pair, quarter, 1)

    def forward(self, pair):
        ahead, behind = self.turned(pair)
        return pair * self.cosine + jnp.where(self.first_half, -ahead, behind) * self.sine

    def backward(self, pair):
        ahead, behind = self.turned(pair * self.sine)
        return pair * self.cosine + jnp.where(self.first_half, ahead, -behind)


class Whole:
    def __init__(self, place, keys, sources, held, sems):
        core, z, y, rows = (place[i] for i in range(1, 5))
        self.held = held
        self.copies = []
        for n, (mask, back, other) in enumerate(keys):
            chip = lax.rem(y + rows - back, rows)
            here = held.at[z ^ mask, chip, core ^ other]
            self.copies.append(pltpu.make_async_copy(sources[n], here, sems.at[n]))
        for copy in self.copies:
            copy.start()

    def wait(self):
        for copy in self.copies:
            copy.wait()

    def columns(self, at_columns):
        part = self.held[:, :, :, :, at_columns]
        return part.reshape(-1, part.shape[-1])


def by_x(x, own, other):
    first = jnp.where(x == 0, own[...], other[...])
    second = jnp.where(x == 0, other[...], own[...])
    return jnp.concatenate([first, second], 0)


def allowed_keys(segment, segment_row, per_group):
    rows = segment.shape[0]
    stacked = (per_group * rows, rows)
    row_ids = lax.rem(lax.broadcasted_iota(jnp.int32, stacked, 0), rows)
    columns = lax.broadcasted_iota(jnp.int32, stacked, 1)
    segments = jnp.concatenate([segment[...]] * per_group, 0)
    return (segments == segment_row[...]) & (columns <= row_ids)


def heads_of(values, group, per_group):
    start = group * per_group
    return jnp.concatenate(
        [
            values[:, (start + i) * HEAD_WIDTH : (start + i + 1) * HEAD_WIDTH]
            for i in range(per_group)
        ],
        0,
    )


def softmax_weights(query, key, allowed):
    scores = jnp.where(allowed, product(query, key, NT) * HEAD_WIDTH ** (-0.5), MASKED)
    exponent = jnp.exp(scores - jnp.max(scores, 1, keepdims=True))
    return exponent / jnp.sum(exponent, 1, keepdims=True)


def attention_kernel(width_kv, keys, place, *refs):
    normed_own, normed_other, segment, segment_row, cosine, sine = refs[:6]
    sources, refs = refs[6 : 6 + len(keys)], refs[6 + len(keys) :]
    query_key, value, attended, branch_own, branch_other, held, sems = refs
    x = place[0]
    low = jnp.bfloat16
    weights_of = Whole(place, keys, sources, held, sems)
    normed = by_x(x, normed_own, normed_other)
    rows_own = normed_own.shape[0]
    rotation = Rotation(cosine, sine)
    width_query = attended.shape[1]
    per_group = width_query // width_kv
    allowed = allowed_keys(segment, segment_row, per_group)
    to_value = slice(width_query + width_kv, width_query + 2 * width_kv)
    to_out = slice(width_query + 2 * width_kv, None)
    weights_of.wait()
    projected = product(normed, weights_of.columns(slice(0, width_query + width_kv)), NN)
    pairs = []
    for start in range(0, projected.shape[1], 2 * HEAD_WIDTH):
        pairs.append(rotation.forward(projected[:, start : start + 2 * HEAD_WIDTH]).astype(low))
    rotated = jnp.concatenate(pairs, 1)
    query_key[...] = rotated
    values = product(normed, weights_of.columns(to_value), NN).astype(low)
    value[...] = values
    heads = []
    for group in range(width_kv // HEAD_WIDTH):
        here = slice(group * HEAD_WIDTH, (group + 1) * HEAD_WIDTH)
        key = rotated[:, width_query:][:, here]
        weights = softmax_weights(heads_of(rotated, group, per_group), key, allowed).astype(low)
        out = product(weights, values[:, here], NN).astype(low)
        rows = rotated.shape[0]
        heads += [out[i * rows : (i + 1) * rows] for i in range(per_group)]
    all_heads = jnp.concatenate(heads, 1)
    attended[...] = all_heads
    branch = product(all_heads, weights_of.columns(to_out), NT)
    first, second = branch[:rows_own], branch[rows_own:]
    branch_own[...] = jnp.where(x == 0, first, second)
    branch_other[...] = jnp.where(x == 0, second, first).astype(low)


def attention_back_kernel(width_kv, keys, place, *refs):
    state_own, state_other, normed_own, normed_other, segment, segment_row, cosine, sine = refs[:8]
    query_key, value, attended = refs[8:11]
    sources, refs = refs[11 : 11 + len(keys)], refs[11 + len(keys) :]
    back_own, back_other, qk_own, qk_other, vo_own, vo_other, held, sems = refs
    x, core = place[0], place[1]
    low = jnp.bfloat16
    weights_of = Whole(place, keys, sources, held, sems)
    scaling = HEAD_WIDTH ** (-0.5)
    state = by_x(x, state_own, state_other)
    normed = by_x(x, normed_own, normed_other)
    rows_own, rows = state_own.shape[0], state.shape[0]
    rotation = Rotation(cosine, sine)
    width_query = attended.shape[1]
    per_group = width_query // width_kv
    allowed = allowed_keys(segment, segment_row, per_group)
    to_value = slice(width_query + width_kv, width_query + 2 * width_kv)
    to_out = slice(width_query + 2 * width_kv, None)
    weights_of.wait()
    grad_attended = product(state, weights_of.columns(to_out), NN).astype(low)

    grad_query, grad_key, grad_value = [], [], []
    for group in range(width_kv // HEAD_WIDTH):
        here = slice(group * HEAD_WIDTH, (group + 1) * HEAD_WIDTH)
        key = query_key[:, width_query:][:, here]
        query, grads = heads_of(query_key, group, per_group), heads_of(grad_attended, group, per_group)
        weights = softmax_weights(query, key, allowed)
        grad_probs = product(grads, value[:, here], NT)
        centered = grad_probs - jnp.sum(weights * grad_probs, 1, keepdims=True)
        grad_scores = (weights * centered).astype(low)
        grad_heads = product(grad_scores, key, NN) * scaling
        grad_query += [grad_heads[i * rows : (i + 1) * rows] for i in range(per_group)]
        grad_key.append(product(grad_scores, query, TN) * scaling)
        grad_value.append(product(weights.astype(low), grads, TN))

    grads = grad_query + grad_key
    grad_qk = jnp.concatenate(
        [
            rotation.backward(jnp.concatenate(grads[n : n + 2], 1)).astype(low)
            for n in range(0, len(grads), 2)
        ],
        1,
    )
    grad_v = jnp.concatenate(grad_value, 1).astype(low)

    own_features = qk_own.shape[1]
    block = max(256, CORES * own_features)
    count = block // (CORES * own_features)
    for start in range(0, normed.shape[1], block):
        features = slice(start, start + block)
        chip = slice(start // (CORES * own_features), start // (CORES * own_features) + count)
        left = normed[:, features]
        for total, own_ref, other_ref, at_columns in (
            (product(left, grad_qk, TN), qk_own, qk_other, slice(None)),
            (product(left, grad_v, TN), vo_own, vo_other, slice(0, width_kv)),
            (product(state[:, features], attended[...], TN), vo_own, vo_other, slice(width_kv, None)),
        ):
            total = total.astype(low).reshape(count, CORES, own_features, total.shape[-1])
            own_ref[chip, :, at_columns] = jnp.where(core == 0, total[:, 0], total[:, 1])
            other_ref[chip, :, at_columns] = jnp.where(core == 0, total[:, 1], total[:, 0])
    back = product(grad_qk, weights_of.columns(slice(0, width_query + width_kv)), NT)
    back = back + product(grad_v, weights_of.columns(to_value), NT)
    first, second = back[:rows_own], back[rows_own:]
    back_own[...] = jnp.where(x == 0, first, second)
    back_other[...] = jnp.where(x == 0, second, first).astype(low)


def attention_call(at, kernel, width_kv, arrays, weights, out_shapes):
    place = jnp.stack([at.x, at.core, at.z, at.y, jnp.int32(at.rows)]).astype(jnp.int32)
    vmem = pl.BlockSpec(memory_space=pltpu.VMEM)
    keys, sources = list(weights), list(weights.values())
    held = pltpu.VMEM((at.planes, at.rows, CORES) + sources[0].shape, sources[0].dtype)
    return pl.pallas_call(
        functools.partial(kernel, width_kv, keys),
        in_specs=[pl.BlockSpec(memory_space=pltpu.SMEM)]
        + [vmem] * len(arrays)
        + [pl.BlockSpec(memory_space=pl.ANY)] * len(sources),
        out_specs=[vmem] * len(out_shapes),
        out_shape=[jax.ShapeDtypeStruct(*shape) for shape in out_shapes],
        scratch_shapes=[held, pltpu.SemaphoreType.DMA((len(keys),))],
        compiler_params=pltpu.CompilerParams(vmem_limit_bytes=56 * 2**20),
        cost_estimate=cost_of(
            2 * len(arrays) * arrays[0].shape[0] * sources[0].size * len(sources) // 2,
            [*arrays, *sources],
            out_shapes,
        ),
    )(place, *arrays, *sources)


def side_by_side(*arrays):
    def kernel(*refs):
        start = 0
        for ref in refs[:-1]:
            refs[-1][:, start : start + ref.shape[1]] = ref[...]
            start += ref.shape[1]

    vmem = pl.BlockSpec(memory_space=pltpu.VMEM)
    shape = (arrays[0].shape[0], sum(array.shape[1] for array in arrays))
    return pl.pallas_call(
        kernel,
        in_specs=[vmem] * len(arrays),
        out_specs=vmem,
        out_shape=jax.ShapeDtypeStruct(shape, arrays[0].dtype),
        cost_estimate=cost_of(0, arrays, [(shape, arrays[0].dtype)]),
    )(*arrays)


def on_device(
    tokens,
    seq_lens,
    norm_gains,
    w_query,
    key_weight,
    value_weight,
    w_out,
    w_gate,
    w_up,
    w_down,
    cotangent,
):
    at = Places(lax.axis_size("dp"))
    rows_own = tokens.shape[0]
    row_count = rows_own * lax.axis_size("tensor")
    width_query = w_query.shape[1]
    width_kv = key_weight.shape[1]
    quarter = w_gate.shape[1] // at.planes
    own_features = w_gate.shape[0]

    row_ids, segment, position, in_use = layout(seq_lens[0], row_count)
    in_use_own = lax.dynamic_slice_in_dim(in_use, at.x * rows_own, rows_own, 0)
    gain_rows = norm_gains.astype(jnp.float32)
    inputs = tokens.astype(jnp.float32)
    scale_one = lax.rsqrt(jnp.mean(inputs * inputs, 1, keepdims=True) + EPSILON)
    normed_own = (inputs * scale_one * gain_rows[0]).astype(jnp.bfloat16)
    normed_other = at.other_x(normed_own)
    grad_mixed = cotangent.astype(jnp.float32) * in_use_own[:, None]
    grad_low_own = grad_mixed.astype(jnp.bfloat16)
    packed = side_by_side(w_query, key_weight, value_weight, w_out)
    others = range(1, at.rows)
    projections = {(0, 0, 0): packed}
    projections[2, 0, 0] = at.across_z(packed, 2)
    projections[1, 0, 0] = at.across_z(packed, 1)
    for j in others:
        projections[0, j, 0] = at.along_y(packed, j)

    stage = [*list(projections.values())[1:], normed_other]
    projections[3, 0, 0] = at.across_z(after(projections[2, 0, 0], *stage), 1)
    for j in others:
        projections[1, j, 0] = at.along_y(after(projections[1, 0, 0], *stage), j)
    grads_low = {(0, 0): grad_low_own, (0, 1): at.other_x(after(grad_low_own, *stage))}
    shares = {}
    for mask in range(at.planes):
        start = (at.z ^ mask) * quarter
        shares[mask] = jnp.stack(
            [lax.dynamic_slice_in_dim(w, start, quarter, 1) for w in (w_gate, w_up, w_down)]
        )
    plane_two = [at.across_z(after(shares[2][:1], *stage), 2)]
    second = [plane_two[0], *(projections[1, j, 0] for j in others)]
    for j in others:
        projections[2, j, 0] = at.along_y(after(projections[2, 0, 0], *second), j)
    plane_two.append(at.across_z(after(shares[2][1:2], *second), 2))
    for mask in (0, 1):
        for j in range(at.rows):
            key = (mask, j, 0)
            if key in projections:
                projections[mask, j, 1] = at.other_core(after(projections[key], *stage))

    middle = grad_low_own.shape[1] // 2
    stage = [projections[3, 0, 0], grads_low[0, 1], plane_two[1]]
    stage += [projections[2, j, 0] for j in others]
    plane_two.append(at.across_z(after(shares[2][2:], *stage), 2))
    grads_low[1, 0] = at.across_z(after(grad_low_own, *stage), 1)
    for j in others:
        projections[3, j, 0] = at.along_y(after(projections[3, 0, 0], *stage), j)
    for mask, j in ((1, 1), (2, 0), (2, 1), (3, 0)):
        for back in others if j else (0,):
            if (mask, back, 1) not in projections:
                block = after(projections[mask, back, 0], *stage)
                projections[mask, back, 1] = at.other_core(block)

    stage = [projections[3, j, 0] for j in others] + [plane_two[2], grads_low[1, 0]]
    plane_two = jnp.concatenate(plane_two, 0)
    low_first = at.across_z(after(grad_low_own[:, :middle], *stage), 2)
    for j in others:
        projections[3, j, 1] = at.other_core(projections[3, j, 0])
    tables = [jnp.concatenate([table, table], 1) for table in rope_tables(position, HEAD_WIDTH)]
    keys_of = [segment[:, None], segment[None, :], *tables]

    weights = {}

    def to_chips(mask, parts, *earlier):
        weights.setdefault((mask, 0, 0), []).extend(parts)
        for j in range(1, at.rows):
            sent = [at.along_y(after(part, *earlier), j) for part in parts]
            weights.setdefault((mask, j, 0), []).extend(sent)
            earlier = tuple(sent)
        return earlier

    plane_three = at.across_z(after(shares[3][:2], *stage), 3)
    plane_one = at.across_z(after(shares[1][:2], *stage), 1)
    grads_low[1, 1] = at.other_x(after(grads_low[1, 0], *stage))
    last = to_chips(0, [shares[0]], *stage)

    low = jnp.bfloat16
    query_key, value, attended, branch_own, branch_other = attention_call(
        at,
        attention_kernel,
        width_kv,
        [normed_own, normed_other, *keys_of],
        projections,
        [
            ((row_count, width_query + width_kv), low),
            ((row_count, width_kv), low),
            ((row_count, width_query), low),
            ((rows_own, inputs.shape[1]), jnp.float32),
            ((rows_own, inputs.shape[1]), low),
        ],
    )
    branch_other = after(
        branch_other, plane_one, plane_three, low_first, grads_low[1, 1], *last
    )
    branch = branch_other
    state = inputs + branch_own + at.other_x(branch_other)
    scale_two = lax.rsqrt(jnp.mean(state * state, 1, keepdims=True) + EPSILON)
    normed_two = (state * scale_two * gain_rows[1]).astype(jnp.bfloat16)

    plane_three_last = at.across_z(after(shares[3][2:], branch), 3)
    plane_one_last = at.across_z(after(shares[1][2:], branch), 1)
    low_second = at.across_z(after(grad_low_own[:, middle:], branch), 2)
    last = to_chips(2, [plane_two], *last, branch)

    def to_cores(mask, backs, part, *earlier):
        for back in backs:
            block = after(weights[mask, back, 0][part], *earlier)
            weights.setdefault((mask, back, 1), []).append(at.other_core(block))

    to_cores(0, range(at.rows), 0, branch)
    stage = [normed_two, plane_three_last, plane_one_last, low_second]
    grads_low[2, 0] = jnp.concatenate([low_first, low_second], 1)
    normed = {(0, 0): normed_two, (0, 1): at.other_x(after(normed_two, *stage))}
    normed[2, 0] = at.across_z(after(normed_two, *stage), 2)
    normed[1, 0] = at.across_z(after(normed_two, *stage), 1)
    to_cores(2, (0,), 0, *stage)
    last = to_chips(1, [plane_one], *last, *stage)
    to_cores(1, (0,), 0, *stage)
    last = to_chips(3, [plane_three], *last)
    to_cores(3, (0,), 0, *stage)

    grads_low[2, 1] = at.other_x(after(grads_low[2, 0], normed[0, 1], *stage))

    stage = [*normed.values(), *last, grads_low[2, 1]]
    normed[3, 0] = at.across_z(after(normed[2, 0], *stage), 1)
    normed[2, 1] = at.other_x(after(normed[2, 0], *stage))
    grads_low[3, 0] = at.across_z(after(grads_low[2, 0], *stage), 1)
    for mask in (2, 1, 3):
        to_cores(mask, others, 0, *stage)
    last = to_chips(1, [plane_one_last], *stage) + to_chips(3, [plane_three_last], *stage)
    for mask in (1, 3):
        to_cores(mask, (0,), 1, *stage)

    stage = [normed[3, 0], normed[2, 1], grads_low[3, 0], *last]
    normed[3, 1] = at.other_x(after(normed[3, 0], *stage))
    normed[1, 1] = at.across_z(after(normed[0, 1], *stage), 1)
    for mask in (1, 3):
        to_cores(mask, others, 1, *stage)
    grads_low[3, 1] = at.other_x(after(grads_low[3, 0], normed[3, 1]))

    masks = (3, 2, 1, 0)
    normed_rows = [normed[mask, x] for mask in masks for x in range(2)]
    grad_rows = [grads_low[mask, x] for mask in masks for x in range(2)]
    hidden, silu, slope, *outs = forward(at, weights, normed_rows)
    def block_of(value, i):
        return value[i * rows_own : (i + 1) * rows_own]

    def out_block(mine, arrived, i):
        return block_of(mine, i).astype(jnp.float32) + arrived

    def of_chip(own, arrived, j):
        y = (at.y + j) % at.rows
        mine = lax.dynamic_index_in_dim(own, y, 0, keepdims=False)
        theirs = lax.dynamic_index_in_dim(arrived, y, 0, keepdims=False)
        return mine.astype(jnp.float32) + theirs

    def for_chips(own, arrived):
        return [of_chip(own, arrived, j).astype(jnp.bfloat16) for j in range(1, at.rows)]

    def send_chips(away, earlier):
        return [at.along_y(after(a, *earlier), j + 1) for j, a in enumerate(away)]

    def of_plane(terms, mask):
        own, arrived, chips = terms
        size = (1, 1) + own.shape[2:]
        at_plane = (at.y, at.z ^ mask, 0, 0)
        total = lax.dynamic_slice(own, at_plane, size)[0, 0].astype(jnp.float32)
        total = total + lax.dynamic_slice(arrived, at_plane, size)[0, 0]
        for part in chips:
            total = total + lax.dynamic_index_in_dim(part, at.z ^ mask, 0, keepdims=False)
        return total

    def send_planes(terms, wanted, earlier):
        sent = {}
        for mask in wanted:
            piece = of_plane(terms, mask).astype(jnp.bfloat16)
            sent[mask] = at.across_z(after(piece, *earlier), mask)
        return sent

    def all_columns(terms, pieces, *earlier):
        result = jnp.zeros((own_features, at.planes * quarter), jnp.float32)
        own = {0: of_plane(terms, 0)}
        for mask, piece in after({**own, **pieces}, *earlier).items():
            result = lax.dynamic_update_slice(
                result, piece.astype(jnp.float32), (0, (at.z ^ mask) * quarter)
            )
        return result

    out_first = at.other_x(outs[1])
    down_own, down_other = weight_grad(at, grad_rows, hidden, own_features)
    down_arrived = at.other_core(down_other)
    down_away = for_chips(down_own, down_arrived)
    grad_gate_in, grad_up_in, *back = backward(
        at, weights, grad_rows, after(silu, *down_away), slope
    )
    down_terms = (down_own, down_arrived, send_chips(down_away, ()))

    def sum_of(i, arrived):
        return back[2 * i].astype(jnp.float32) + arrived

    stage = [out_first, back[0], *down_terms[2]]
    three = at.other_x(after(back[1], *stage))
    one = at.across_z(after(back[5], *stage), 1)
    gate_own, gate_other = weight_grad(
        at, normed_rows, after(grad_gate_in, *stage), own_features
    )

    stage = [three, one, gate_own]
    to_two = at.across_z(after(sum_of(0, three).astype(jnp.bfloat16), *stage), 1)
    two = at.other_x(after(back[3], *stage))
    gate_arrived = at.other_core(after(gate_other, *stage))
    up_own, up_other = weight_grad(at, normed_rows, after(grad_up_in, *stage), own_features)

    stage = [to_two, two, gate_arrived, up_own]
    for_zero = (sum_of(1, two) + to_two).astype(jnp.bfloat16)
    middle = for_zero.shape[1] // 2
    to_zero_first = at.across_z(after(for_zero[:, :middle], *stage), 2)
    other_zero = (back[7].astype(jnp.float32) + one).astype(jnp.bfloat16)
    zero = at.other_x(after(other_zero, *stage))
    gate_away = for_chips(gate_own, gate_arrived)
    lower = at.planes // 2
    gate_lower = send_chips([away[:lower] for away in gate_away], stage)
    up_arrived = at.other_core(after(up_other, *stage))

    stage = [zero, to_zero_first, *gate_lower, up_arrived]
    to_zero_second = at.across_z(after(for_zero[:, middle:], *stage), 2)
    from_one = at.across_z(after(back[4], *stage), 1)
    gate_upper = send_chips([away[lower:] for away in gate_away], stage)

    to_zero = jnp.concatenate([to_zero_first, to_zero_second], 1)
    grad_normed_two = sum_of(3, zero) + from_one + to_zero
    hat_two = state * scale_two
    inner_two = grad_normed_two * gain_rows[1]
    grad_state = grad_mixed + scale_two * (
        inner_two - hat_two * jnp.mean(inner_two * hat_two, 1, keepdims=True)
    )
    gain_two = jnp.sum(grad_normed_two * hat_two, 0)
    grad_state_own = grad_state.astype(jnp.bfloat16)

    grad_state_other = at.other_x(grad_state_own)
    stage = [grad_state_own, *gate_upper]
    gate_chips = [jnp.concatenate(parts, 0) for parts in zip(gate_lower, gate_upper, strict=True)]
    gate_terms = (gate_own, gate_arrived, gate_chips)

    def both(mask, *pair):
        return jnp.stack([of_plane(terms, mask).astype(jnp.bfloat16) for terms in pair])

    down_pieces = send_planes(down_terms, (2,), stage)
    first_one = out_block(outs[0], block_of(out_first, 2), 2).astype(jnp.bfloat16)
    first_one = at.across_z(after(first_one, *stage), 1)
    late = [*stage, grad_state_other, down_pieces[2], first_one]
    gate_pieces = send_planes(gate_terms, (2, 3), late)
    gate_down = at.across_z(after(both(1, gate_terms, down_terms), *late), 1)
    up_chips = send_chips(for_chips(up_own, up_arrived), stage)
    up_terms = (up_own, up_arrived, up_chips)

    out_second = at.other_x(after(outs[3], grad_state_other))
    shape = (at.chips, own_features, width_query + width_kv)
    back_own, back_other, qk_own, qk_other, vo_own, vo_other = attention_call(
        at,
        attention_back_kernel,
        width_kv,
        [
            grad_state_own,
            grad_state_other,
            normed_own,
            normed_other,
            *keys_of,
            after(query_key, *late),
            value,
            attended,
        ],
        projections,
        [
            ((rows_own, inputs.shape[1]), jnp.float32),
            ((rows_own, inputs.shape[1]), low),
            *[(shape, low)] * 4,
        ],
    )
    stage = [qk_other, out_second, *up_chips, *gate_pieces.values(), gate_down]
    gate_pieces[1], down_pieces[1] = gate_down[0], gate_down[1]
    out_blocks = [
        jnp.concatenate(
            [
                out_block(outs[2 * n], block_of(arrived, i), i)
                for n, arrived in enumerate((out_first, out_second))
            ],
            1,
        )
        for i in range(4)
    ]

    owns = {"qk": qk_own, "vo": vo_own}
    cores = {
        "qk": at.other_core(after(qk_other, *stage)),
        "vo": at.other_core(after(vo_other, *stage)),
    }

    def by_place(value):
        return value.reshape(at.planes, at.rows, own_features, -1)

    def for_chip(name, j):
        y = (at.y + j) % at.rows
        parts = [
            lax.dynamic_index_in_dim(by_place(value), y, 1, keepdims=False)
            for value in (owns[name], cores[name])
        ]
        return (parts[0].astype(jnp.float32) + parts[1]).astype(jnp.bfloat16)

    chips = {"qk": [], "vo": []}

    def to_chips_of(name, earlier):
        for j in others:
            chips[name].append(at.along_y(after(for_chip(name, j), *earlier), j))

    def for_plane(name, mask):
        z = at.z ^ mask
        total = 0.0
        for value in (owns[name], cores[name]):
            part = lax.dynamic_slice(by_place(value), (z, at.y, 0, 0), (1, 1) + by_place(value).shape[2:])
            total = total + part[0, 0].astype(jnp.float32)
        for part in chips[name]:
            total = total + lax.dynamic_index_in_dim(part, z, 0, keepdims=False)
        return total

    pairs, quarters = {}, {}

    def to_pair(name, earlier):
        both_planes = jnp.stack([for_plane(name, 1), for_plane(name, 3)]).astype(jnp.bfloat16)
        pairs[name] = at.across_z(after(both_planes, *earlier), 1)

    def to_quarter(name, earlier):
        far = (for_plane(name, 2) + pairs[name][1]).astype(jnp.bfloat16)
        quarters[name] = at.across_z(after(far, *earlier), 2)

    def total_of(name):
        return for_plane(name, 0) + pairs[name][0] + quarters[name]

    up_pieces = send_planes(up_terms, (2,), stage)
    up_down = at.across_z(after(both(3, up_terms, down_terms), *stage), 3)
    up_pieces[3], down_pieces[3] = up_down[0], up_down[1]
    out_two = at.across_z(after(out_blocks[0].astype(jnp.bfloat16), *stage), 1)
    to_chips_of("qk", ())

    middle = out_blocks[2].shape[1] // 2
    second_one = at.across_z(after(out_blocks[2][:, middle:].astype(jnp.bfloat16), *stage), 1)
    out_one = jnp.concatenate([first_one, second_one], 1)

    stage = [*chips["qk"], up_pieces[2], up_down, out_two, second_one]
    normed_arrived = at.other_x(after(back_other, *stage))
    to_chips_of("vo", stage)
    to_pair("qk", stage)
    up_pieces.update(send_planes(up_terms, (1,), stage))
    out_zero = (out_blocks[1] + out_two).astype(jnp.bfloat16)
    out_zero = at.across_z(after(out_zero, *stage), 2)

    stage = [*chips["vo"], pairs["qk"], out_zero, normed_arrived, up_pieces[1]]
    to_pair("vo", stage)
    to_quarter("qk", stage)
    grad_normed_one = back_own + after(normed_arrived, *stage)
    hat_one = inputs * scale_one
    inner_one = grad_normed_one * gain_rows[0]
    grad_tokens = (
        grad_state
        + scale_one * (inner_one - hat_one * jnp.mean(inner_one * hat_one, 1, keepdims=True))
    ).astype(jnp.bfloat16)
    gain_one = jnp.sum(grad_normed_one * hat_one, 0)
    grad_gains = jnp.stack([gain_one, gain_two])
    grad_gains = grad_gains + at.other_x(grad_gains)
    bits = [1 << i for i in range(at.dp.bit_length() - 1)]
    for bit in bits:
        if bit < CORES * at.rows:
            grad_gains = grad_gains + at.move(grad_gains, lambda d: d ^ bit)

    stage = [pairs["vo"], quarters["qk"], grad_gains]
    to_quarter("vo", stage)
    for bit in bits:
        if bit >= CORES * at.rows:
            grad_gains = grad_gains + at.move(after(grad_gains, *stage), lambda d: d ^ bit)
    grad_gate = all_columns(gate_terms, gate_pieces, *stage)
    grad_up = all_columns(up_terms, up_pieces, *stage)
    grad_down = all_columns(down_terms, down_pieces, *stage)
    sum_qk, sum_vo = total_of("qk"), total_of("vo")
    grad_gate = all_columns(gate_terms, gate_pieces, *stage)
    grad_up = all_columns(up_terms, up_pieces, *stage)
    grad_down = all_columns(down_terms, down_pieces, *stage)
    ffn_out = out_blocks[3] + out_zero + out_one
    mixed = ((state + ffn_out) * in_use_own[:, None]).astype(jnp.bfloat16)
    return (
        mixed,
        grad_tokens,
        grad_gains,
        sum_qk[:, :width_query],
        sum_qk[:, width_query:],
        sum_vo[:, :width_kv],
        sum_vo[:, width_kv:],
        grad_gate,
        grad_up,
        grad_down,
    )


def solution(mesh):
    in_specs = (
        P(("dp", "tensor"), None),
        P("dp", None),
        P(),
        P("dp", "tensor"),
        P("dp", "tensor"),
        P("dp", "tensor"),
        P("dp", "tensor"),
        P("dp", "tensor"),
        P("dp", "tensor"),
        P("dp", "tensor"),
        P(("dp", "tensor"), None),
    )
    out_specs = (
        P(("dp", "tensor"), None),
        P(("dp", "tensor"), None),
        P(),
        P("dp", "tensor"),
        P("dp", "tensor"),
        P("dp", "tensor"),
        P("dp", "tensor"),
        P("dp", "tensor"),
        P("dp", "tensor"),
        P("dp", "tensor"),
    )
    return jax.shard_map(
        on_device, mesh=mesh, in_specs=in_specs, out_specs=out_specs, check_vma=False
    )
```

```python
import functools
import math

import jax
import jax.numpy as jnp
from jax import lax
from jax.experimental import pallas as pl
from jax.experimental.pallas import tpu as pltpu
from jax.sharding import PartitionSpec as P

HEAD_WIDTH = 64
EPSILON = 1e-05
MASKED = -1e30
CORES = 2
PLANES = 4


def after(value, *earlier):
    return lax.optimization_barrier((value, *earlier))[0]


def layout(lengths, row_count):
    finish = jnp.cumsum(lengths)
    starts = jnp.concatenate([finish - lengths, finish[-1:]])
    row_ids = jnp.arange(row_count, dtype=jnp.int32)
    segment = jnp.sum((row_ids[:, None] >= finish[None, :]).astype(jnp.int32), 1)
    chosen_slot = segment[:, None] == jnp.arange(starts.shape[0], dtype=jnp.int32)[None, :]
    first_row = jnp.sum(jnp.where(chosen_slot, starts[None, :], 0), 1)
    position = row_ids - first_row
    in_use = (segment < lengths.shape[0]).astype(jnp.float32)
    return (row_ids, segment, position, in_use)


def rope_tables(position, head_size):
    halfway = head_size // 2
    ladder = jnp.arange(halfway, dtype=jnp.float32)
    inverse = 1.0 / 500000.0 ** (ladder * 2.0 / head_size)
    wavelength = 2.0 * math.pi / inverse
    smooth = (8192.0 / wavelength - 1.0) / 3.0
    blended = (1.0 - smooth) * inverse / 32.0 + smooth * inverse
    scaled = jnp.where(
        wavelength > 8192.0, inverse / 32.0, jnp.where(wavelength < 2048.0, inverse, blended)
    )
    angles = position.astype(jnp.float32)[:, None] * scaled[None, :]
    cosine_lookup = jnp.cos(angles)
    sine_lookup = jnp.sin(angles)
    return (
        jnp.concatenate([cosine_lookup, cosine_lookup], 1),
        jnp.concatenate([sine_lookup, sine_lookup], 1),
    )


class Places:
    def __init__(self, dp):
        self.dp = dp
        self.planes = PLANES
        self.rows = dp // (PLANES * CORES)
        self.chips = dp // CORES
        index = lax.axis_index("dp")
        self.z = index // (self.rows * CORES)
        self.y = (index // CORES) % self.rows
        self.core = index % CORES
        self.x = lax.axis_index("tensor")

    def move(self, value, target):
        return lax.ppermute(value, "dp", [(d, target(d)) for d in range(self.dp)])

    def across_z(self, value, mask):
        stride = self.rows * CORES
        return self.move(value, lambda d: d ^ (mask * stride))

    def along_y(self, value, steps):
        def target(d):
            y = (d // CORES) % self.rows
            return d + ((y + steps) % self.rows - y) * CORES

        return self.move(value, target)

    def other_core(self, value):
        return self.move(value, lambda d: d ^ 1)

    def other_x(self, value):
        return lax.ppermute(value, "tensor", [(0, 1), (1, 0)])


def product(left_side, right_side, contract):
    return lax.dot_general(
        left_side, right_side, (contract, ((), ())), preferred_element_type=jnp.float32
    )


NN = ((1,), (0,))
NT = ((1,), (1,))
TN = ((0,), (0,))


class Held:
    def __init__(self, place, blocks, sources, which, held, sems):
        self.z, self.y, self.core, self.rows = (place[i] for i in range(4))
        self.blocks, self.sources, self.which = blocks, sources, which
        self.held, self.sems = held, sems
        for i in range(len(which)):
            for n in range(len(blocks)):
                self.copy(i, n).start()

    def copy(self, i, n):
        (mask, back, other), first, counts = self.blocks[n]
        source, within = first, self.which[i]
        for count in counts:
            if within < count:
                break
            source, within = source + 1, within - count
        size = self.sources[source].shape[1]
        chip = (self.z ^ mask) * self.rows + lax.rem(self.y + self.rows - back, self.rows)
        start = pl.multiple_of((chip * CORES + (self.core ^ other)) * size, size)
        return pltpu.make_async_copy(
            self.sources[source].at[within], self.held.at[i, pl.ds(start, size)], self.sems.at[i, n]
        )

    def wait(self, i):
        for n in range(len(self.blocks)):
            self.copy(i, n).wait()


def cost_of(flops, arrays, out_shapes):
    moved = [math.prod(array.shape) * array.dtype.itemsize for array in arrays]
    moved += [math.prod(shape) * jnp.dtype(kind).itemsize for shape, kind in out_shapes]
    return pl.CostEstimate(flops=flops, bytes_accessed=sum(moved), transcendentals=0)


def held_call(at, kernel, weights, which, arrays, out_shapes):
    blocks, sources = [], []
    for key, parts in weights.items():
        blocks.append((key, len(sources), [part.shape[0] for part in parts]))
        sources += parts
    _, size, quarter = sources[0].shape
    place = jnp.stack([at.z, at.y, at.core, jnp.int32(at.rows)]).astype(jnp.int32)
    vmem = pl.BlockSpec(memory_space=pltpu.VMEM)
    low = jnp.bfloat16

    def body(place, *refs):
        ins, refs = refs[: len(arrays)], refs[len(arrays) :]
        given, refs = refs[: len(sources)], refs[len(sources) :]
        outs, (held, sems) = refs[: len(out_shapes)], refs[len(out_shapes) :]
        kernel(Held(place, blocks, given, which, held, sems), ins, outs)

    return pl.pallas_call(
        body,
        in_specs=[pl.BlockSpec(memory_space=pltpu.SMEM)]
        + [vmem] * len(arrays)
        + [pl.BlockSpec(memory_space=pl.ANY)] * len(sources),
        out_specs=[vmem] * len(out_shapes),
        out_shape=[jax.ShapeDtypeStruct(shape, low) for shape in out_shapes],
        scratch_shapes=[
            pltpu.VMEM((len(which), len(blocks) * size, quarter), low),
            pltpu.SemaphoreType.DMA((len(which), len(blocks))),
        ],
        compiler_params=pltpu.CompilerParams(vmem_limit_bytes=56 * 2**20),
        cost_estimate=cost_of(
            6 * out_shapes[0][0] * size * len(blocks) * quarter,
            [*arrays, *sources],
            [(shape, low) for shape in out_shapes],
        ),
    )(place, *arrays, *sources)


def forward(at, weights, normed):
    rows_own, width = normed[0].shape
    quarter = next(iter(weights.values()))[0].shape[-1]
    count = len(normed) // 2
    half = width // 2

    def kernel(held, normed, outs):
        hidden_ref, silu_ref, slope_ref, *out_refs = outs
        held.wait(0)
        held.wait(1)

        def block(k, rows):
            here = pl.ds(pl.multiple_of(2 * k * rows_own, rows_own), 2 * rows_own)
            own = pl.ds(pl.multiple_of(k * rows_own, rows_own), rows_own)
            gate = product(rows, held.held[0], NN)
            up = product(rows, held.held[1], NN)
            sigmoid_gate = jax.nn.sigmoid(gate)
            silu_gate = gate * sigmoid_gate
            hidden = (silu_gate * up).astype(jnp.bfloat16)
            hidden_ref[here] = hidden
            silu_ref[here] = silu_gate.astype(jnp.bfloat16)
            slope = up * sigmoid_gate * (1.0 + gate * (1.0 - sigmoid_gate))
            slope_ref[here] = slope.astype(jnp.bfloat16)

            @pl.when(k == 0)
            def _():
                held.wait(2)

            out = product(hidden, held.held[2], NT).astype(jnp.bfloat16)
            for i in range(2):
                columns = slice(i * half, (i + 1) * half)
                out_refs[2 * i][own] = out[:rows_own, columns]
                out_refs[2 * i + 1][own] = out[rows_own:, columns]

        @pl.loop(0, count)
        def _(k):
            rows = jnp.concatenate([normed[0][...], normed[1][...]], 0)
            for i in range(1, count):
                other = jnp.concatenate([normed[2 * i][...], normed[2 * i + 1][...]], 0)
                rows = jnp.where(k == i, other, rows)
            block(k, rows)

    shapes = [(2 * count * rows_own, quarter)] * 3 + [(count * rows_own, half)] * 4
    return held_call(at, kernel, weights, (0, 1, 2), normed, shapes)


def backward(at, weights, grads, silu, slope):
    rows_own, width = grads[0].shape
    count = len(grads) // 2

    def kernel(held, ins, outs):
        *grads, silu, slope = ins
        gate_ref, up_ref, *back = outs
        for k in range(count):
            here = slice(2 * k * rows_own, 2 * (k + 1) * rows_own)
            rows = jnp.concatenate([grads[2 * k][...], grads[2 * k + 1][...]], 0)
            if k == 0:
                held.wait(0)
            grad_hidden = product(rows, held.held[0], NN)
            grad_gate = (grad_hidden * slope[here]).astype(jnp.bfloat16)
            grad_up = (grad_hidden * silu[here]).astype(jnp.bfloat16)
            gate_ref[here] = grad_gate
            up_ref[here] = grad_up
            if k == 0:
                held.wait(1)
            total = product(grad_gate, held.held[1], NT)
            if k == 0:
                held.wait(2)
            total = (total + product(grad_up, held.held[2], NT)).astype(jnp.bfloat16)
            back[2 * k][...] = total[:rows_own]
            back[2 * k + 1][...] = total[rows_own:]

    shapes = [silu.shape] * 2 + [(rows_own, width)] * (2 * count)
    return held_call(at, kernel, weights, (2, 0, 1), [*grads, silu, slope], shapes)


def weight_grad_kernel(place, *refs):
    core = place[0]
    *left, right, own_ref, other_ref = refs
    rows = jnp.concatenate([ref[...] for ref in left], 0)
    total = product(rows, right[...], TN).astype(jnp.bfloat16)
    chips, _, own_features, quarter = own_ref.shape
    total = total.reshape(chips, CORES, own_features, quarter)
    own_ref[:, 0] = jnp.where(core == 0, total[:, 0], total[:, 1])
    other_ref[:, 0] = jnp.where(core == 0, total[:, 1], total[:, 0])


def weight_grad(at, left, right, own_features):
    rows, width = left[0].shape
    quarter = right.shape[-1]
    place = jnp.stack([at.core]).astype(jnp.int32)
    shape = (at.rows, at.planes, own_features, quarter)
    block = (at.rows, 1, own_features, quarter)
    left_spec = pl.BlockSpec((rows, width // at.planes), lambda i, place: (0, i))
    return pl.pallas_call(
        weight_grad_kernel,
        grid_spec=pltpu.PrefetchScalarGridSpec(
            num_scalar_prefetch=1,
            grid=(at.planes,),
            in_specs=[left_spec] * len(left) + [pl.BlockSpec(right.shape, lambda i, place: (0, 0))],
            out_specs=[pl.BlockSpec(block, lambda i, place: (0, i, 0, 0))] * 2,
        ),
        out_shape=[jax.ShapeDtypeStruct(shape, jnp.bfloat16)] * 2,
        compiler_params=pltpu.CompilerParams(vmem_limit_bytes=56 * 2**20),
        cost_estimate=cost_of(
            2 * len(left) * rows * width * quarter,
            [*left, right],
            [(shape, right.dtype)] * 2,
        ),
    )(place, *left, right)


class Rotation:
    def __init__(self, cosine, sine):
        self.cosine, self.sine = cosine[...], sine[...]
        lanes = lax.broadcasted_iota(jnp.int32, self.cosine.shape, 1)
        self.first_half = lax.rem(lanes, HEAD_WIDTH) < HEAD_WIDTH // 2

    def turned(self, pair):
        quarter = HEAD_WIDTH // 2
        return pltpu.roll(pair, 2 * HEAD_WIDTH - quarter, 1), pltpu.roll(pair, quarter, 1)

    def forward(self, pair):
        ahead, behind = self.turned(pair)
        return pair * self.cosine + jnp.where(self.first_half, -ahead, behind) * self.sine

    def backward(self, pair):
        ahead, behind = self.turned(pair * self.sine)
        return pair * self.cosine + jnp.where(self.first_half, ahead, -behind)


class Whole:
    def __init__(self, place, keys, sources, held, sems):
        core, z, y, rows = (place[i] for i in range(1, 5))
        self.held = held
        self.copies = []
        for n, (mask, back, other) in enumerate(keys):
            chip = lax.rem(y + rows - back, rows)
            here = held.at[z ^ mask, chip, core ^ other]
            self.copies.append(pltpu.make_async_copy(sources[n], here, sems.at[n]))
        for copy in self.copies:
            copy.start()

    def wait(self):
        for copy in self.copies:
            copy.wait()

    def columns(self, at_columns):
        part = self.held[:, :, :, :, at_columns]
        return part.reshape(-1, part.shape[-1])


def by_x(x, own, other):
    first = jnp.where(x == 0, own[...], other[...])
    second = jnp.where(x == 0, other[...], own[...])
    return jnp.concatenate([first, second], 0)


def allowed_keys(segment, segment_row, per_group):
    rows = segment.shape[0]
    stacked = (per_group * rows, rows)
    row_ids = lax.rem(lax.broadcasted_iota(jnp.int32, stacked, 0), rows)
    columns = lax.broadcasted_iota(jnp.int32, stacked, 1)
    segments = jnp.concatenate([segment[...]] * per_group, 0)
    return (segments == segment_row[...]) & (columns <= row_ids)


def heads_of(values, group, per_group):
    start = group * per_group
    return jnp.concatenate(
        [
            values[:, (start + i) * HEAD_WIDTH : (start + i + 1) * HEAD_WIDTH]
            for i in range(per_group)
        ],
        0,
    )


def softmax_weights(query, key, allowed):
    scores = jnp.where(allowed, product(query, key, NT) * HEAD_WIDTH ** (-0.5), MASKED)
    exponent = jnp.exp(scores - jnp.max(scores, 1, keepdims=True))
    return exponent / jnp.sum(exponent, 1, keepdims=True)


def attention_kernel(width_kv, keys, place, *refs):
    normed_own, normed_other, segment, segment_row, cosine, sine = refs[:6]
    sources, refs = refs[6 : 6 + len(keys)], refs[6 + len(keys) :]
    query_key, value, attended, branch_own, branch_other, held, sems = refs
    x = place[0]
    low = jnp.bfloat16
    weights_of = Whole(place, keys, sources, held, sems)
    normed = by_x(x, normed_own, normed_other)
    rows_own = normed_own.shape[0]
    rotation = Rotation(cosine, sine)
    width_query = attended.shape[1]
    per_group = width_query // width_kv
    allowed = allowed_keys(segment, segment_row, per_group)
    to_value = slice(width_query + width_kv, width_query + 2 * width_kv)
    to_out = slice(width_query + 2 * width_kv, None)
    weights_of.wait()
    projected = product(normed, weights_of.columns(slice(0, width_query + width_kv)), NN)
    pairs = []
    for start in range(0, projected.shape[1], 2 * HEAD_WIDTH):
        pairs.append(rotation.forward(projected[:, start : start + 2 * HEAD_WIDTH]).astype(low))
    rotated = jnp.concatenate(pairs, 1)
    query_key[...] = rotated
    values = product(normed, weights_of.columns(to_value), NN).astype(low)
    value[...] = values
    heads = []
    for group in range(width_kv // HEAD_WIDTH):
        here = slice(group * HEAD_WIDTH, (group + 1) * HEAD_WIDTH)
        key = rotated[:, width_query:][:, here]
        weights = softmax_weights(heads_of(rotated, group, per_group), key, allowed).astype(low)
        out = product(weights, values[:, here], NN).astype(low)
        rows = rotated.shape[0]
        heads += [out[i * rows : (i + 1) * rows] for i in range(per_group)]
    all_heads = jnp.concatenate(heads, 1)
    attended[...] = all_heads
    branch = product(all_heads, weights_of.columns(to_out), NT)
    first, second = branch[:rows_own], branch[rows_own:]
    branch_own[...] = jnp.where(x == 0, first, second)
    branch_other[...] = jnp.where(x == 0, second, first).astype(low)


def attention_back_kernel(width_kv, keys, place, *refs):
    state_own, state_other, normed_own, normed_other, segment, segment_row, cosine, sine = refs[:8]
    query_key, value, attended = refs[8:11]
    sources, refs = refs[11 : 11 + len(keys)], refs[11 + len(keys) :]
    back_own, back_other, qk_own, qk_other, vo_own, vo_other, held, sems = refs
    x, core = place[0], place[1]
    low = jnp.bfloat16
    weights_of = Whole(place, keys, sources, held, sems)
    scaling = HEAD_WIDTH ** (-0.5)
    state = by_x(x, state_own, state_other)
    normed = by_x(x, normed_own, normed_other)
    rows_own, rows = state_own.shape[0], state.shape[0]
    rotation = Rotation(cosine, sine)
    width_query = attended.shape[1]
    per_group = width_query // width_kv
    allowed = allowed_keys(segment, segment_row, per_group)
    to_value = slice(width_query + width_kv, width_query + 2 * width_kv)
    to_out = slice(width_query + 2 * width_kv, None)
    weights_of.wait()
    grad_attended = product(state, weights_of.columns(to_out), NN).astype(low)

    grad_query, grad_key, grad_value = [], [], []
    for group in range(width_kv // HEAD_WIDTH):
        here = slice(group * HEAD_WIDTH, (group + 1) * HEAD_WIDTH)
        key = query_key[:, width_query:][:, here]
        query, grads = heads_of(query_key, group, per_group), heads_of(grad_attended, group, per_group)
        weights = softmax_weights(query, key, allowed)
        grad_probs = product(grads, value[:, here], NT)
        centered = grad_probs - jnp.sum(weights * grad_probs, 1, keepdims=True)
        grad_scores = (weights * centered).astype(low)
        grad_heads = product(grad_scores, key, NN) * scaling
        grad_query += [grad_heads[i * rows : (i + 1) * rows] for i in range(per_group)]
        grad_key.append(product(grad_scores, query, TN) * scaling)
        grad_value.append(product(weights.astype(low), grads, TN))

    grads = grad_query + grad_key
    grad_qk = jnp.concatenate(
        [
            rotation.backward(jnp.concatenate(grads[n : n + 2], 1)).astype(low)
            for n in range(0, len(grads), 2)
        ],
        1,
    )
    grad_v = jnp.concatenate(grad_value, 1).astype(low)

    own_features = qk_own.shape[1]
    block = max(256, CORES * own_features)
    count = block // (CORES * own_features)
    for start in range(0, normed.shape[1], block):
        features = slice(start, start + block)
        chip = slice(start // (CORES * own_features), start // (CORES * own_features) + count)
        left = normed[:, features]
        for total, own_ref, other_ref, at_columns in (
            (product(left, grad_qk, TN), qk_own, qk_other, slice(None)),
            (product(left, grad_v, TN), vo_own, vo_other, slice(0, width_kv)),
            (product(state[:, features], attended[...], TN), vo_own, vo_other, slice(width_kv, None)),
        ):
            total = total.astype(low).reshape(count, CORES, own_features, total.shape[-1])
            own_ref[chip, :, at_columns] = jnp.where(core == 0, total[:, 0], total[:, 1])
            other_ref[chip, :, at_columns] = jnp.where(core == 0, total[:, 1], total[:, 0])
    back = product(grad_qk, weights_of.columns(slice(0, width_query + width_kv)), NT)
    back = back + product(grad_v, weights_of.columns(to_value), NT)
    first, second = back[:rows_own], back[rows_own:]
    back_own[...] = jnp.where(x == 0, first, second)
    back_other[...] = jnp.where(x == 0, second, first).astype(low)


def attention_call(at, kernel, width_kv, arrays, weights, out_shapes):
    place = jnp.stack([at.x, at.core, at.z, at.y, jnp.int32(at.rows)]).astype(jnp.int32)
    vmem = pl.BlockSpec(memory_space=pltpu.VMEM)
    keys, sources = list(weights), list(weights.values())
    held = pltpu.VMEM((at.planes, at.rows, CORES) + sources[0].shape, sources[0].dtype)
    return pl.pallas_call(
        functools.partial(kernel, width_kv, keys),
        in_specs=[pl.BlockSpec(memory_space=pltpu.SMEM)]
        + [vmem] * len(arrays)
        + [pl.BlockSpec(memory_space=pl.ANY)] * len(sources),
        out_specs=[vmem] * len(out_shapes),
        out_shape=[jax.ShapeDtypeStruct(*shape) for shape in out_shapes],
        scratch_shapes=[held, pltpu.SemaphoreType.DMA((len(keys),))],
        compiler_params=pltpu.CompilerParams(vmem_limit_bytes=56 * 2**20),
        cost_estimate=cost_of(
            2 * len(arrays) * arrays[0].shape[0] * sources[0].size * len(sources) // 2,
            [*arrays, *sources],
            out_shapes,
        ),
    )(place, *arrays, *sources)


def side_by_side(*arrays):
    def kernel(*refs):
        start = 0
        for ref in refs[:-1]:
            refs[-1][:, start : start + ref.shape[1]] = ref[...]
            start += ref.shape[1]

    vmem = pl.BlockSpec(memory_space=pltpu.VMEM)
    shape = (arrays[0].shape[0], sum(array.shape[1] for array in arrays))
    return pl.pallas_call(
        kernel,
        in_specs=[vmem] * len(arrays),
        out_specs=vmem,
        out_shape=jax.ShapeDtypeStruct(shape, arrays[0].dtype),
        cost_estimate=cost_of(0, arrays, [(shape, arrays[0].dtype)]),
    )(*arrays)


def on_device(
    tokens,
    seq_lens,
    norm_gains,
    w_query,
    key_weight,
    value_weight,
    w_out,
    w_gate,
    w_up,
    w_down,
    cotangent,
):
    at = Places(lax.axis_size("dp"))
    rows_own = tokens.shape[0]
    row_count = rows_own * lax.axis_size("tensor")
    width_query = w_query.shape[1]
    width_kv = key_weight.shape[1]
    quarter = w_gate.shape[1] // at.planes
    own_features = w_gate.shape[0]

    row_ids, segment, position, in_use = layout(seq_lens[0], row_count)
    in_use_own = lax.dynamic_slice_in_dim(in_use, at.x * rows_own, rows_own, 0)
    gain_rows = norm_gains.astype(jnp.float32)
    inputs = tokens.astype(jnp.float32)
    scale_one = lax.rsqrt(jnp.mean(inputs * inputs, 1, keepdims=True) + EPSILON)
    normed_own = (inputs * scale_one * gain_rows[0]).astype(jnp.bfloat16)
    normed_other = at.other_x(normed_own)
    grad_mixed = cotangent.astype(jnp.float32) * in_use_own[:, None]
    grad_low_own = grad_mixed.astype(jnp.bfloat16)
    packed = side_by_side(w_query, key_weight, value_weight, w_out)
    others = range(1, at.rows)
    projections = {(0, 0, 0): packed}
    projections[2, 0, 0] = at.across_z(packed, 2)
    projections[1, 0, 0] = at.across_z(packed, 1)
    for j in others:
        projections[0, j, 0] = at.along_y(packed, j)

    stage = [*list(projections.values())[1:], normed_other]
    projections[3, 0, 0] = at.across_z(after(projections[2, 0, 0], *stage), 1)
    for j in others:
        projections[1, j, 0] = at.along_y(after(projections[1, 0, 0], *stage), j)
    grads_low = {(0, 0): grad_low_own, (0, 1): at.other_x(after(grad_low_own, *stage))}
    shares = {}
    for mask in range(at.planes):
        start = (at.z ^ mask) * quarter
        shares[mask] = jnp.stack(
            [lax.dynamic_slice_in_dim(w, start, quarter, 1) for w in (w_gate, w_up, w_down)]
        )
    plane_two = [at.across_z(after(shares[2][:1], *stage), 2)]
    second = [plane_two[0], *(projections[1, j, 0] for j in others)]
    for j in others:
        projections[2, j, 0] = at.along_y(after(projections[2, 0, 0], *second), j)
    plane_two.append(at.across_z(after(shares[2][1:2], *second), 2))
    for mask in (0, 1):
        for j in range(at.rows):
            key = (mask, j, 0)
            if key in projections:
                projections[mask, j, 1] = at.other_core(after(projections[key], *stage))

    middle = grad_low_own.shape[1] // 2
    stage = [projections[3, 0, 0], grads_low[0, 1], plane_two[1]]
    stage += [projections[2, j, 0] for j in others]
    plane_two.append(at.across_z(after(shares[2][2:], *stage), 2))
    grads_low[1, 0] = at.across_z(after(grad_low_own, *stage), 1)
    for j in others:
        projections[3, j, 0] = at.along_y(after(projections[3, 0, 0], *stage), j)
    for mask, j in ((1, 1), (2, 0), (2, 1), (3, 0)):
        for back in others if j else (0,):
            if (mask, back, 1) not in projections:
                block = after(projections[mask, back, 0], *stage)
                projections[mask, back, 1] = at.other_core(block)

    stage = [projections[3, j, 0] for j in others] + [plane_two[2], grads_low[1, 0]]
    plane_two = jnp.concatenate(plane_two, 0)
    low_first = at.across_z(after(grad_low_own[:, :middle], *stage), 2)
    for j in others:
        projections[3, j, 1] = at.other_core(projections[3, j, 0])
    tables = [jnp.concatenate([table, table], 1) for table in rope_tables(position, HEAD_WIDTH)]
    keys_of = [segment[:, None], segment[None, :], *tables]

    weights = {}

    def to_chips(mask, parts, *earlier):
        weights.setdefault((mask, 0, 0), []).extend(parts)
        for j in range(1, at.rows):
            sent = [at.along_y(after(part, *earlier), j) for part in parts]
            weights.setdefault((mask, j, 0), []).extend(sent)
            earlier = tuple(sent)
        return earlier

    plane_three = at.across_z(after(shares[3][:2], *stage), 3)
    plane_one = at.across_z(after(shares[1][:2], *stage), 1)
    grads_low[1, 1] = at.other_x(after(grads_low[1, 0], *stage))
    last = to_chips(0, [shares[0]], *stage)

    low = jnp.bfloat16
    query_key, value, attended, branch_own, branch_other = attention_call(
        at,
        attention_kernel,
        width_kv,
        [normed_own, normed_other, *keys_of],
        projections,
        [
            ((row_count, width_query + width_kv), low),
            ((row_count, width_kv), low),
            ((row_count, width_query), low),
            ((rows_own, inputs.shape[1]), jnp.float32),
            ((rows_own, inputs.shape[1]), low),
        ],
    )
    branch_other = after(
        branch_other, plane_one, plane_three, low_first, grads_low[1, 1], *last
    )
    branch = branch_other
    state = inputs + branch_own + at.other_x(branch_other)
    scale_two = lax.rsqrt(jnp.mean(state * state, 1, keepdims=True) + EPSILON)
    normed_two = (state * scale_two * gain_rows[1]).astype(jnp.bfloat16)

    plane_three_last = at.across_z(after(shares[3][2:], branch), 3)
    plane_one_last = at.across_z(after(shares[1][2:], branch), 1)
    low_second = at.across_z(after(grad_low_own[:, middle:], branch), 2)
    last = to_chips(2, [plane_two], *last, branch)

    def to_cores(mask, backs, part, *earlier):
        for back in backs:
            block = after(weights[mask, back, 0][part], *earlier)
            weights.setdefault((mask, back, 1), []).append(at.other_core(block))

    to_cores(0, range(at.rows), 0, branch)
    stage = [normed_two, plane_three_last, plane_one_last, low_second]
    grads_low[2, 0] = jnp.concatenate([low_first, low_second], 1)
    normed = {(0, 0): normed_two, (0, 1): at.other_x(after(normed_two, *stage))}
    normed[2, 0] = at.across_z(after(normed_two, *stage), 2)
    normed[1, 0] = at.across_z(after(normed_two, *stage), 1)
    to_cores(2, (0,), 0, *stage)
    last = to_chips(1, [plane_one], *last, *stage)
    to_cores(1, (0,), 0, *stage)
    last = to_chips(3, [plane_three], *last)
    to_cores(3, (0,), 0, *stage)

    grads_low[2, 1] = at.other_x(after(grads_low[2, 0], normed[0, 1], *stage))

    stage = [*normed.values(), *last, grads_low[2, 1]]
    normed[3, 0] = at.across_z(after(normed[2, 0], *stage), 1)
    normed[2, 1] = at.other_x(after(normed[2, 0], *stage))
    grads_low[3, 0] = at.across_z(after(grads_low[2, 0], *stage), 1)
    for mask in (2, 1, 3):
        to_cores(mask, others, 0, *stage)
    last = to_chips(1, [plane_one_last], *stage) + to_chips(3, [plane_three_last], *stage)
    for mask in (1, 3):
        to_cores(mask, (0,), 1, *stage)

    stage = [normed[3, 0], normed[2, 1], grads_low[3, 0], *last]
    normed[3, 1] = at.other_x(after(normed[3, 0], *stage))
    normed[1, 1] = at.across_z(after(normed[0, 1], *stage), 1)
    for mask in (1, 3):
        to_cores(mask, others, 1, *stage)
    grads_low[3, 1] = at.other_x(after(grads_low[3, 0], normed[3, 1]))

    masks = (3, 2, 1, 0)
    normed_rows = [normed[mask, x] for mask in masks for x in range(2)]
    grad_rows = [grads_low[mask, x] for mask in masks for x in range(2)]
    hidden, silu, slope, *outs = forward(at, weights, normed_rows)
    def block_of(value, i):
        return value[i * rows_own : (i + 1) * rows_own]

    def out_block(mine, arrived, i):
        return block_of(mine, i).astype(jnp.float32) + arrived

    def of_chip(own, arrived, j):
        y = (at.y + j) % at.rows
        mine = lax.dynamic_index_in_dim(own, y, 0, keepdims=False)
        theirs = lax.dynamic_index_in_dim(arrived, y, 0, keepdims=False)
        return mine.astype(jnp.float32) + theirs

    def for_chips(own, arrived):
        return [of_chip(own, arrived, j).astype(jnp.bfloat16) for j in range(1, at.rows)]

    def send_chips(away, earlier):
        return [at.along_y(after(a, *earlier), j + 1) for j, a in enumerate(away)]

    def of_plane(terms, mask):
        own, arrived, chips = terms
        size = (1, 1) + own.shape[2:]
        at_plane = (at.y, at.z ^ mask, 0, 0)
        total = lax.dynamic_slice(own, at_plane, size)[0, 0].astype(jnp.float32)
        total = total + lax.dynamic_slice(arrived, at_plane, size)[0, 0]
        for part in chips:
            total = total + lax.dynamic_index_in_dim(part, at.z ^ mask, 0, keepdims=False)
        return total

    def send_planes(terms, wanted, earlier):
        sent = {}
        for mask in wanted:
            piece = of_plane(terms, mask).astype(jnp.bfloat16)
            sent[mask] = at.across_z(after(piece, *earlier), mask)
        return sent

    def all_columns(terms, pieces, *earlier):
        result = jnp.zeros((own_features, at.planes * quarter), jnp.float32)
        own = {0: of_plane(terms, 0)}
        for mask, piece in after({**own, **pieces}, *earlier).items():
            result = lax.dynamic_update_slice(
                result, piece.astype(jnp.float32), (0, (at.z ^ mask) * quarter)
            )
        return result

    out_first = at.other_x(outs[1])
    down_own, down_other = weight_grad(at, grad_rows, hidden, own_features)
    down_arrived = at.other_core(down_other)
    down_away = for_chips(down_own, down_arrived)
    grad_gate_in, grad_up_in, *back = backward(
        at, weights, grad_rows, after(silu, *down_away), slope
    )
    down_terms = (down_own, down_arrived, send_chips(down_away, ()))

    def sum_of(i, arrived):
        return back[2 * i].astype(jnp.float32) + arrived

    stage = [out_first, back[0], *down_terms[2]]
    three = at.other_x(after(back[1], *stage))
    one = at.across_z(after(back[5], *stage), 1)
    gate_own, gate_other = weight_grad(
        at, normed_rows, after(grad_gate_in, *stage), own_features
    )

    stage = [three, one, gate_own]
    to_two = at.across_z(after(sum_of(0, three).astype(jnp.bfloat16), *stage), 1)
    two = at.other_x(after(back[3], *stage))
    gate_arrived = at.other_core(after(gate_other, *stage))
    up_own, up_other = weight_grad(at, normed_rows, after(grad_up_in, *stage), own_features)

    stage = [to_two, two, gate_arrived, up_own]
    for_zero = (sum_of(1, two) + to_two).astype(jnp.bfloat16)
    to_zero = at.across_z(after(for_zero, *stage), 2)
    other_zero = (back[7].astype(jnp.float32) + one).astype(jnp.bfloat16)
    zero = at.other_x(after(other_zero, *stage))
    from_one = at.across_z(after(back[4], *stage), 1)
    gate_chips = send_chips(for_chips(gate_own, gate_arrived), stage)
    up_arrived = at.other_core(after(up_other, *stage))

    grad_normed_two = sum_of(3, zero) + from_one + to_zero
    hat_two = state * scale_two
    inner_two = grad_normed_two * gain_rows[1]
    grad_state = grad_mixed + scale_two * (
        inner_two - hat_two * jnp.mean(inner_two * hat_two, 1, keepdims=True)
    )
    gain_two = jnp.sum(grad_normed_two * hat_two, 0)
    grad_state_own = grad_state.astype(jnp.bfloat16)

    grad_state_other = at.other_x(grad_state_own)
    stage = [grad_state_own, *gate_chips]
    gate_terms = (gate_own, gate_arrived, gate_chips)

    def both(mask, *pair):
        return jnp.stack([of_plane(terms, mask).astype(jnp.bfloat16) for terms in pair])

    down_pieces = send_planes(down_terms, (2,), stage)
    first_one = out_block(outs[0], block_of(out_first, 2), 2).astype(jnp.bfloat16)
    first_one = at.across_z(after(first_one, *stage), 1)
    late = [*stage, grad_state_other, down_pieces[2], first_one]
    gate_pieces = send_planes(gate_terms, (2, 3), late)
    gate_down = at.across_z(after(both(1, gate_terms, down_terms), *late), 1)
    up_chips = send_chips(for_chips(up_own, up_arrived), stage)
    up_terms = (up_own, up_arrived, up_chips)

    out_second = at.other_x(after(outs[3], grad_state_other))
    shape = (at.chips, own_features, width_query + width_kv)
    back_own, back_other, qk_own, qk_other, vo_own, vo_other = attention_call(
        at,
        attention_back_kernel,
        width_kv,
        [
            grad_state_own,
            grad_state_other,
            normed_own,
            normed_other,
            *keys_of,
            after(query_key, *late),
            value,
            attended,
        ],
        projections,
        [
            ((rows_own, inputs.shape[1]), jnp.float32),
            ((rows_own, inputs.shape[1]), low),
            *[(shape, low)] * 4,
        ],
    )
    stage = [qk_other, out_second, *up_chips, *gate_pieces.values(), gate_down]
    gate_pieces[1], down_pieces[1] = gate_down[0], gate_down[1]
    out_blocks = [
        jnp.concatenate(
            [
                out_block(outs[2 * n], block_of(arrived, i), i)
                for n, arrived in enumerate((out_first, out_second))
            ],
            1,
        )
        for i in range(4)
    ]

    owns = {"qk": qk_own, "vo": vo_own}
    cores = {
        "qk": at.other_core(after(qk_other, *stage)),
        "vo": at.other_core(after(vo_other, *stage)),
    }

    def by_place(value):
        return value.reshape(at.planes, at.rows, own_features, -1)

    def for_chip(name, j):
        y = (at.y + j) % at.rows
        parts = [
            lax.dynamic_index_in_dim(by_place(value), y, 1, keepdims=False)
            for value in (owns[name], cores[name])
        ]
        return (parts[0].astype(jnp.float32) + parts[1]).astype(jnp.bfloat16)

    chips = {"qk": [], "vo": []}

    def to_chips_of(name, earlier):
        for j in others:
            chips[name].append(at.along_y(after(for_chip(name, j), *earlier), j))

    def for_plane(name, mask):
        z = at.z ^ mask
        total = 0.0
        for value in (owns[name], cores[name]):
            part = lax.dynamic_slice(by_place(value), (z, at.y, 0, 0), (1, 1) + by_place(value).shape[2:])
            total = total + part[0, 0].astype(jnp.float32)
        for part in chips[name]:
            total = total + lax.dynamic_index_in_dim(part, z, 0, keepdims=False)
        return total

    pairs, quarters = {}, {}

    def to_pair(name, earlier):
        both_planes = jnp.stack([for_plane(name, 1), for_plane(name, 3)]).astype(jnp.bfloat16)
        pairs[name] = at.across_z(after(both_planes, *earlier), 1)

    def to_quarter(name, earlier):
        far = (for_plane(name, 2) + pairs[name][1]).astype(jnp.bfloat16)
        quarters[name] = at.across_z(after(far, *earlier), 2)

    def total_of(name):
        return for_plane(name, 0) + pairs[name][0] + quarters[name]

    up_pieces = send_planes(up_terms, (2,), stage)
    up_down = at.across_z(after(both(3, up_terms, down_terms), *stage), 3)
    up_pieces[3], down_pieces[3] = up_down[0], up_down[1]
    out_two = at.across_z(after(out_blocks[0].astype(jnp.bfloat16), *stage), 1)
    to_chips_of("qk", ())

    middle = out_blocks[2].shape[1] // 2
    second_one = at.across_z(after(out_blocks[2][:, middle:].astype(jnp.bfloat16), *stage), 1)
    out_one = jnp.concatenate([first_one, second_one], 1)

    stage = [*chips["qk"], up_pieces[2], up_down, out_two, second_one]
    normed_arrived = at.other_x(after(back_other, *stage))
    to_chips_of("vo", stage)
    to_pair("qk", stage)
    up_pieces.update(send_planes(up_terms, (1,), stage))
    out_zero = (out_blocks[1] + out_two).astype(jnp.bfloat16)
    out_zero = at.across_z(after(out_zero, *stage), 2)

    stage = [*chips["vo"], pairs["qk"], out_zero, normed_arrived, up_pieces[1]]
    to_pair("vo", stage)
    to_quarter("qk", stage)
    grad_normed_one = back_own + after(normed_arrived, *stage)
    hat_one = inputs * scale_one
    inner_one = grad_normed_one * gain_rows[0]
    grad_tokens = (
        grad_state
        + scale_one * (inner_one - hat_one * jnp.mean(inner_one * hat_one, 1, keepdims=True))
    ).astype(jnp.bfloat16)
    gain_one = jnp.sum(grad_normed_one * hat_one, 0)
    grad_gains = jnp.stack([gain_one, gain_two])
    grad_gains = grad_gains + at.other_x(grad_gains)
    bits = [1 << i for i in range(at.dp.bit_length() - 1)]
    for bit in bits:
        if bit < CORES * at.rows:
            grad_gains = grad_gains + at.move(grad_gains, lambda d: d ^ bit)

    stage = [pairs["vo"], quarters["qk"], grad_gains]
    to_quarter("vo", stage)
    for bit in bits:
        if bit >= CORES * at.rows:
            grad_gains = grad_gains + at.move(after(grad_gains, *stage), lambda d: d ^ bit)
    grad_gate = all_columns(gate_terms, gate_pieces, *stage)
    grad_up = all_columns(up_terms, up_pieces, *stage)
    grad_down = all_columns(down_terms, down_pieces, *stage)
    sum_qk, sum_vo = total_of("qk"), total_of("vo")
    grad_gate = all_columns(gate_terms, gate_pieces, *stage)
    grad_up = all_columns(up_terms, up_pieces, *stage)
    grad_down = all_columns(down_terms, down_pieces, *stage)
    ffn_out = out_blocks[3] + out_zero + out_one
    mixed = ((state + ffn_out) * in_use_own[:, None]).astype(jnp.bfloat16)
    return (
        mixed,
        grad_tokens,
        grad_gains,
        sum_qk[:, :width_query],
        sum_qk[:, width_query:],
        sum_vo[:, :width_kv],
        sum_vo[:, width_kv:],
        grad_gate,
        grad_up,
        grad_down,
    )


def solution(mesh):
    in_specs = (
        P(("dp", "tensor"), None),
        P("dp", None),
        P(),
        P("dp", "tensor"),
        P("dp", "tensor"),
        P("dp", "tensor"),
        P("dp", "tensor"),
        P("dp", "tensor"),
        P("dp", "tensor"),
        P("dp", "tensor"),
        P(("dp", "tensor"), None),
    )
    out_specs = (
        P(("dp", "tensor"), None),
        P(("dp", "tensor"), None),
        P(),
        P("dp", "tensor"),
        P("dp", "tensor"),
        P("dp", "tensor"),
        P("dp", "tensor"),
        P("dp", "tensor"),
        P("dp", "tensor"),
        P("dp", "tensor"),
    )
    return jax.shard_map(
        on_device, mesh=mesh, in_specs=in_specs, out_specs=out_specs, check_vma=False
    )
```

```python
import functools
import math

import jax
import jax.numpy as jnp
from jax import lax
from jax.experimental import pallas as pl
from jax.experimental.pallas import tpu as pltpu
from jax.sharding import PartitionSpec as P

HEAD_WIDTH = 64
EPSILON = 1e-05
MASKED = -1e30
CORES = 2
PLANES = 4


def after(value, *earlier):
    return lax.optimization_barrier((value, *earlier))[0]


def layout(lengths, row_count):
    finish = jnp.cumsum(lengths)
    starts = jnp.concatenate([finish - lengths, finish[-1:]])
    row_ids = jnp.arange(row_count, dtype=jnp.int32)
    segment = jnp.sum((row_ids[:, None] >= finish[None, :]).astype(jnp.int32), 1)
    chosen_slot = segment[:, None] == jnp.arange(starts.shape[0], dtype=jnp.int32)[None, :]
    first_row = jnp.sum(jnp.where(chosen_slot, starts[None, :], 0), 1)
    position = row_ids - first_row
    in_use = (segment < lengths.shape[0]).astype(jnp.float32)
    return (row_ids, segment, position, in_use)


def rope_tables(position, head_size):
    halfway = head_size // 2
    ladder = jnp.arange(halfway, dtype=jnp.float32)
    inverse = 1.0 / 500000.0 ** (ladder * 2.0 / head_size)
    wavelength = 2.0 * math.pi / inverse
    smooth = (8192.0 / wavelength - 1.0) / 3.0
    blended = (1.0 - smooth) * inverse / 32.0 + smooth * inverse
    scaled = jnp.where(
        wavelength > 8192.0, inverse / 32.0, jnp.where(wavelength < 2048.0, inverse, blended)
    )
    angles = position.astype(jnp.float32)[:, None] * scaled[None, :]
    cosine_lookup = jnp.cos(angles)
    sine_lookup = jnp.sin(angles)
    return (
        jnp.concatenate([cosine_lookup, cosine_lookup], 1),
        jnp.concatenate([sine_lookup, sine_lookup], 1),
    )


class Places:
    def __init__(self, dp):
        self.dp = dp
        self.planes = PLANES
        self.rows = dp // (PLANES * CORES)
        self.chips = dp // CORES
        index = lax.axis_index("dp")
        self.z = index // (self.rows * CORES)
        self.y = (index // CORES) % self.rows
        self.core = index % CORES
        self.x = lax.axis_index("tensor")

    def move(self, value, target):
        return lax.ppermute(value, "dp", [(d, target(d)) for d in range(self.dp)])

    def across_z(self, value, mask):
        stride = self.rows * CORES
        return self.move(value, lambda d: d ^ (mask * stride))

    def along_y(self, value, steps):
        def target(d):
            y = (d // CORES) % self.rows
            return d + ((y + steps) % self.rows - y) * CORES

        return self.move(value, target)

    def other_core(self, value):
        return self.move(value, lambda d: d ^ 1)

    def other_x(self, value):
        return lax.ppermute(value, "tensor", [(0, 1), (1, 0)])


def product(left_side, right_side, contract):
    return lax.dot_general(
        left_side, right_side, (contract, ((), ())), preferred_element_type=jnp.float32
    )


NN = ((1,), (0,))
NT = ((1,), (1,))
TN = ((0,), (0,))


class Held:
    def __init__(self, place, blocks, sources, which, held, sems):
        self.z, self.y, self.core, self.rows = (place[i] for i in range(4))
        self.blocks, self.sources, self.which = blocks, sources, which
        self.held, self.sems = held, sems
        for i in range(len(which)):
            for n in range(len(blocks)):
                self.copy(i, n).start()

    def copy(self, i, n):
        (mask, back, other), first, counts = self.blocks[n]
        source, within = first, self.which[i]
        for count in counts:
            if within < count:
                break
            source, within = source + 1, within - count
        size = self.sources[source].shape[1]
        chip = (self.z ^ mask) * self.rows + lax.rem(self.y + self.rows - back, self.rows)
        start = pl.multiple_of((chip * CORES + (self.core ^ other)) * size, size)
        return pltpu.make_async_copy(
            self.sources[source].at[within], self.held.at[i, pl.ds(start, size)], self.sems.at[i, n]
        )

    def wait(self, i):
        for n in range(len(self.blocks)):
            self.copy(i, n).wait()


def cost_of(flops, arrays, out_shapes):
    moved = [math.prod(array.shape) * array.dtype.itemsize for array in arrays]
    moved += [math.prod(shape) * jnp.dtype(kind).itemsize for shape, kind in out_shapes]
    return pl.CostEstimate(flops=flops, bytes_accessed=sum(moved), transcendentals=0)


def held_call(at, kernel, weights, which, arrays, out_shapes):
    blocks, sources = [], []
    for key, parts in weights.items():
        blocks.append((key, len(sources), [part.shape[0] for part in parts]))
        sources += parts
    _, size, quarter = sources[0].shape
    place = jnp.stack([at.z, at.y, at.core, jnp.int32(at.rows)]).astype(jnp.int32)
    vmem = pl.BlockSpec(memory_space=pltpu.VMEM)
    low = jnp.bfloat16

    def body(place, *refs):
        ins, refs = refs[: len(arrays)], refs[len(arrays) :]
        given, refs = refs[: len(sources)], refs[len(sources) :]
        outs, (held, sems) = refs[: len(out_shapes)], refs[len(out_shapes) :]
        kernel(Held(place, blocks, given, which, held, sems), ins, outs)

    return pl.pallas_call(
        body,
        in_specs=[pl.BlockSpec(memory_space=pltpu.SMEM)]
        + [vmem] * len(arrays)
        + [pl.BlockSpec(memory_space=pl.ANY)] * len(sources),
        out_specs=[vmem] * len(out_shapes),
        out_shape=[jax.ShapeDtypeStruct(shape, low) for shape in out_shapes],
        scratch_shapes=[
            pltpu.VMEM((len(which), len(blocks) * size, quarter), low),
            pltpu.SemaphoreType.DMA((len(which), len(blocks))),
        ],
        compiler_params=pltpu.CompilerParams(vmem_limit_bytes=56 * 2**20),
        cost_estimate=cost_of(
            6 * out_shapes[0][0] * size * len(blocks) * quarter,
            [*arrays, *sources],
            [(shape, low) for shape in out_shapes],
        ),
    )(place, *arrays, *sources)


def forward(at, weights, normed):
    rows_own, width = normed[0].shape
    quarter = next(iter(weights.values()))[0].shape[-1]
    count = len(normed) // 2
    half = width // 2

    def kernel(held, normed, outs):
        hidden_ref, silu_ref, slope_ref, *out_refs = outs
        held.wait(0)
        held.wait(1)

        def block(k, rows):
            here = pl.ds(pl.multiple_of(2 * k * rows_own, rows_own), 2 * rows_own)
            own = pl.ds(pl.multiple_of(k * rows_own, rows_own), rows_own)
            gate = product(rows, held.held[0], NN)
            up = product(rows, held.held[1], NN)
            sigmoid_gate = jax.nn.sigmoid(gate)
            silu_gate = gate * sigmoid_gate
            hidden = (silu_gate * up).astype(jnp.bfloat16)
            hidden_ref[here] = hidden
            silu_ref[here] = silu_gate.astype(jnp.bfloat16)
            slope = up * sigmoid_gate * (1.0 + gate * (1.0 - sigmoid_gate))
            slope_ref[here] = slope.astype(jnp.bfloat16)

            @pl.when(k == 0)
            def _():
                held.wait(2)

            out = product(hidden, held.held[2], NT).astype(jnp.bfloat16)
            for i in range(2):
                columns = slice(i * half, (i + 1) * half)
                out_refs[2 * i][own] = out[:rows_own, columns]
                out_refs[2 * i + 1][own] = out[rows_own:, columns]

        @pl.loop(0, count)
        def _(k):
            rows = jnp.concatenate([normed[0][...], normed[1][...]], 0)
            for i in range(1, count):
                other = jnp.concatenate([normed[2 * i][...], normed[2 * i + 1][...]], 0)
                rows = jnp.where(k == i, other, rows)
            block(k, rows)

    shapes = [(2 * count * rows_own, quarter)] * 3 + [(count * rows_own, half)] * 4
    return held_call(at, kernel, weights, (0, 1, 2), normed, shapes)


def backward(at, weights, grads, silu, slope):
    rows_own, width = grads[0].shape
    count = len(grads) // 2

    def kernel(held, ins, outs):
        *grads, silu, slope = ins
        gate_ref, up_ref, *back = outs
        for k in range(count):
            here = slice(2 * k * rows_own, 2 * (k + 1) * rows_own)
            rows = jnp.concatenate([grads[2 * k][...], grads[2 * k + 1][...]], 0)
            if k == 0:
                held.wait(0)
            grad_hidden = product(rows, held.held[0], NN)
            grad_gate = (grad_hidden * slope[here]).astype(jnp.bfloat16)
            grad_up = (grad_hidden * silu[here]).astype(jnp.bfloat16)
            gate_ref[here] = grad_gate
            up_ref[here] = grad_up
            if k == 0:
                held.wait(1)
            total = product(grad_gate, held.held[1], NT)
            if k == 0:
                held.wait(2)
            total = (total + product(grad_up, held.held[2], NT)).astype(jnp.bfloat16)
            back[2 * k][...] = total[:rows_own]
            back[2 * k + 1][...] = total[rows_own:]

    shapes = [silu.shape] * 2 + [(rows_own, width)] * (2 * count)
    return held_call(at, kernel, weights, (2, 0, 1), [*grads, silu, slope], shapes)


def weight_grad_kernel(place, *refs):
    core = place[0]
    *left, right, own_ref, other_ref = refs
    rows = jnp.concatenate([ref[...] for ref in left], 0)
    total = product(rows, right[...], TN).astype(jnp.bfloat16)
    chips, _, own_features, quarter = own_ref.shape
    total = total.reshape(chips, CORES, own_features, quarter)
    own_ref[:, 0] = jnp.where(core == 0, total[:, 0], total[:, 1])
    other_ref[:, 0] = jnp.where(core == 0, total[:, 1], total[:, 0])


def weight_grad(at, left, right, own_features):
    rows, width = left[0].shape
    quarter = right.shape[-1]
    place = jnp.stack([at.core]).astype(jnp.int32)
    shape = (at.rows, at.planes, own_features, quarter)
    block = (at.rows, 1, own_features, quarter)
    left_spec = pl.BlockSpec((rows, width // at.planes), lambda i, place: (0, i))
    return pl.pallas_call(
        weight_grad_kernel,
        grid_spec=pltpu.PrefetchScalarGridSpec(
            num_scalar_prefetch=1,
            grid=(at.planes,),
            in_specs=[left_spec] * len(left) + [pl.BlockSpec(right.shape, lambda i, place: (0, 0))],
            out_specs=[pl.BlockSpec(block, lambda i, place: (0, i, 0, 0))] * 2,
        ),
        out_shape=[jax.ShapeDtypeStruct(shape, jnp.bfloat16)] * 2,
        compiler_params=pltpu.CompilerParams(vmem_limit_bytes=56 * 2**20),
        cost_estimate=cost_of(
            2 * len(left) * rows * width * quarter,
            [*left, right],
            [(shape, right.dtype)] * 2,
        ),
    )(place, *left, right)


class Rotation:
    def __init__(self, cosine, sine):
        self.cosine, self.sine = cosine[...], sine[...]
        lanes = lax.broadcasted_iota(jnp.int32, self.cosine.shape, 1)
        self.first_half = lax.rem(lanes, HEAD_WIDTH) < HEAD_WIDTH // 2

    def turned(self, pair):
        quarter = HEAD_WIDTH // 2
        return pltpu.roll(pair, 2 * HEAD_WIDTH - quarter, 1), pltpu.roll(pair, quarter, 1)

    def forward(self, pair):
        ahead, behind = self.turned(pair)
        return pair * self.cosine + jnp.where(self.first_half, -ahead, behind) * self.sine

    def backward(self, pair):
        ahead, behind = self.turned(pair * self.sine)
        return pair * self.cosine + jnp.where(self.first_half, ahead, -behind)


class Whole:
    def __init__(self, place, keys, sources, held, sems):
        core, z, y, rows = (place[i] for i in range(1, 5))
        self.held = held
        self.copies = []
        for n, (mask, back, other) in enumerate(keys):
            chip = lax.rem(y + rows - back, rows)
            here = held.at[z ^ mask, chip, core ^ other]
            self.copies.append(pltpu.make_async_copy(sources[n], here, sems.at[n]))
        for copy in self.copies:
            copy.start()

    def wait(self):
        for copy in self.copies:
            copy.wait()

    def columns(self, at_columns):
        part = self.held[:, :, :, :, at_columns]
        return part.reshape(-1, part.shape[-1])


def by_x(x, own, other):
    first = jnp.where(x == 0, own[...], other[...])
    second = jnp.where(x == 0, other[...], own[...])
    return jnp.concatenate([first, second], 0)


def allowed_keys(segment, segment_row, per_group):
    rows = segment.shape[0]
    stacked = (per_group * rows, rows)
    row_ids = lax.rem(lax.broadcasted_iota(jnp.int32, stacked, 0), rows)
    columns = lax.broadcasted_iota(jnp.int32, stacked, 1)
    segments = jnp.concatenate([segment[...]] * per_group, 0)
    return (segments == segment_row[...]) & (columns <= row_ids)


def heads_of(values, group, per_group):
    start = group * per_group
    return jnp.concatenate(
        [
            values[:, (start + i) * HEAD_WIDTH : (start + i + 1) * HEAD_WIDTH]
            for i in range(per_group)
        ],
        0,
    )


def softmax_weights(query, key, allowed):
    scores = jnp.where(allowed, product(query, key, NT) * HEAD_WIDTH ** (-0.5), MASKED)
    exponent = jnp.exp(scores - jnp.max(scores, 1, keepdims=True))
    return exponent / jnp.sum(exponent, 1, keepdims=True)


def attention_kernel(width_kv, keys, place, *refs):
    normed_own, normed_other, segment, segment_row, cosine, sine = refs[:6]
    sources, refs = refs[6 : 6 + len(keys)], refs[6 + len(keys) :]
    query_key, value, attended, branch_own, branch_other, held, sems = refs
    x = place[0]
    low = jnp.bfloat16
    weights_of = Whole(place, keys, sources, held, sems)
    normed = by_x(x, normed_own, normed_other)
    rows_own = normed_own.shape[0]
    rotation = Rotation(cosine, sine)
    width_query = attended.shape[1]
    per_group = width_query // width_kv
    allowed = allowed_keys(segment, segment_row, per_group)
    to_value = slice(width_query + width_kv, width_query + 2 * width_kv)
    to_out = slice(width_query + 2 * width_kv, None)
    weights_of.wait()
    projected = product(normed, weights_of.columns(slice(0, width_query + width_kv)), NN)
    pairs = []
    for start in range(0, projected.shape[1], 2 * HEAD_WIDTH):
        pairs.append(rotation.forward(projected[:, start : start + 2 * HEAD_WIDTH]).astype(low))
    rotated = jnp.concatenate(pairs, 1)
    query_key[...] = rotated
    values = product(normed, weights_of.columns(to_value), NN).astype(low)
    value[...] = values
    heads = []
    for group in range(width_kv // HEAD_WIDTH):
        here = slice(group * HEAD_WIDTH, (group + 1) * HEAD_WIDTH)
        key = rotated[:, width_query:][:, here]
        weights = softmax_weights(heads_of(rotated, group, per_group), key, allowed).astype(low)
        out = product(weights, values[:, here], NN).astype(low)
        rows = rotated.shape[0]
        heads += [out[i * rows : (i + 1) * rows] for i in range(per_group)]
    all_heads = jnp.concatenate(heads, 1)
    attended[...] = all_heads
    branch = product(all_heads, weights_of.columns(to_out), NT)
    first, second = branch[:rows_own], branch[rows_own:]
    branch_own[...] = jnp.where(x == 0, first, second)
    branch_other[...] = jnp.where(x == 0, second, first).astype(low)


def attention_back_kernel(width_kv, keys, place, *refs):
    state_own, state_other, normed_own, normed_other, segment, segment_row, cosine, sine = refs[:8]
    query_key, value, attended = refs[8:11]
    sources, refs = refs[11 : 11 + len(keys)], refs[11 + len(keys) :]
    back_own, back_other, qk_own, qk_other, vo_own, vo_other, held, sems = refs
    x, core = place[0], place[1]
    low = jnp.bfloat16
    weights_of = Whole(place, keys, sources, held, sems)
    scaling = HEAD_WIDTH ** (-0.5)
    state = by_x(x, state_own, state_other)
    normed = by_x(x, normed_own, normed_other)
    rows_own, rows = state_own.shape[0], state.shape[0]
    rotation = Rotation(cosine, sine)
    width_query = attended.shape[1]
    per_group = width_query // width_kv
    allowed = allowed_keys(segment, segment_row, per_group)
    to_value = slice(width_query + width_kv, width_query + 2 * width_kv)
    to_out = slice(width_query + 2 * width_kv, None)
    weights_of.wait()
    grad_attended = product(state, weights_of.columns(to_out), NN).astype(low)

    grad_query, grad_key, grad_value = [], [], []
    for group in range(width_kv // HEAD_WIDTH):
        here = slice(group * HEAD_WIDTH, (group + 1) * HEAD_WIDTH)
        key = query_key[:, width_query:][:, here]
        query, grads = heads_of(query_key, group, per_group), heads_of(grad_attended, group, per_group)
        weights = softmax_weights(query, key, allowed)
        grad_probs = product(grads, value[:, here], NT)
        centered = grad_probs - jnp.sum(weights * grad_probs, 1, keepdims=True)
        grad_scores = (weights * centered).astype(low)
        grad_heads = product(grad_scores, key, NN) * scaling
        grad_query += [grad_heads[i * rows : (i + 1) * rows] for i in range(per_group)]
        grad_key.append(product(grad_scores, query, TN) * scaling)
        grad_value.append(product(weights.astype(low), grads, TN))

    grads = grad_query + grad_key
    grad_qk = jnp.concatenate(
        [
            rotation.backward(jnp.concatenate(grads[n : n + 2], 1)).astype(low)
            for n in range(0, len(grads), 2)
        ],
        1,
    )
    grad_v = jnp.concatenate(grad_value, 1).astype(low)

    own_features = qk_own.shape[1]
    block = max(256, CORES * own_features)
    count = block // (CORES * own_features)
    for start in range(0, normed.shape[1], block):
        features = slice(start, start + block)
        chip = slice(start // (CORES * own_features), start // (CORES * own_features) + count)
        left = normed[:, features]
        for total, own_ref, other_ref, at_columns in (
            (product(left, grad_qk, TN), qk_own, qk_other, slice(None)),
            (product(left, grad_v, TN), vo_own, vo_other, slice(0, width_kv)),
            (product(state[:, features], attended[...], TN), vo_own, vo_other, slice(width_kv, None)),
        ):
            total = total.astype(low).reshape(count, CORES, own_features, total.shape[-1])
            own_ref[chip, :, at_columns] = jnp.where(core == 0, total[:, 0], total[:, 1])
            other_ref[chip, :, at_columns] = jnp.where(core == 0, total[:, 1], total[:, 0])
    back = product(grad_qk, weights_of.columns(slice(0, width_query + width_kv)), NT)
    back = back + product(grad_v, weights_of.columns(to_value), NT)
    first, second = back[:rows_own], back[rows_own:]
    back_own[...] = jnp.where(x == 0, first, second)
    back_other[...] = jnp.where(x == 0, second, first).astype(low)


def attention_call(at, kernel, width_kv, arrays, weights, out_shapes):
    place = jnp.stack([at.x, at.core, at.z, at.y, jnp.int32(at.rows)]).astype(jnp.int32)
    vmem = pl.BlockSpec(memory_space=pltpu.VMEM)
    keys, sources = list(weights), list(weights.values())
    held = pltpu.VMEM((at.planes, at.rows, CORES) + sources[0].shape, sources[0].dtype)
    return pl.pallas_call(
        functools.partial(kernel, width_kv, keys),
        in_specs=[pl.BlockSpec(memory_space=pltpu.SMEM)]
        + [vmem] * len(arrays)
        + [pl.BlockSpec(memory_space=pl.ANY)] * len(sources),
        out_specs=[vmem] * len(out_shapes),
        out_shape=[jax.ShapeDtypeStruct(*shape) for shape in out_shapes],
        scratch_shapes=[held, pltpu.SemaphoreType.DMA((len(keys),))],
        compiler_params=pltpu.CompilerParams(vmem_limit_bytes=56 * 2**20),
        cost_estimate=cost_of(
            2 * len(arrays) * arrays[0].shape[0] * sources[0].size * len(sources) // 2,
            [*arrays, *sources],
            out_shapes,
        ),
    )(place, *arrays, *sources)


def side_by_side(*arrays):
    def kernel(*refs):
        start = 0
        for ref in refs[:-1]:
            refs[-1][:, start : start + ref.shape[1]] = ref[...]
            start += ref.shape[1]

    vmem = pl.BlockSpec(memory_space=pltpu.VMEM)
    shape = (arrays[0].shape[0], sum(array.shape[1] for array in arrays))
    return pl.pallas_call(
        kernel,
        in_specs=[vmem] * len(arrays),
        out_specs=vmem,
        out_shape=jax.ShapeDtypeStruct(shape, arrays[0].dtype),
        cost_estimate=cost_of(0, arrays, [(shape, arrays[0].dtype)]),
    )(*arrays)


def on_device(
    tokens,
    seq_lens,
    norm_gains,
    w_query,
    key_weight,
    value_weight,
    w_out,
    w_gate,
    w_up,
    w_down,
    cotangent,
):
    at = Places(lax.axis_size("dp"))
    rows_own = tokens.shape[0]
    row_count = rows_own * lax.axis_size("tensor")
    width_query = w_query.shape[1]
    width_kv = key_weight.shape[1]
    quarter = w_gate.shape[1] // at.planes
    own_features = w_gate.shape[0]

    row_ids, segment, position, in_use = layout(seq_lens[0], row_count)
    in_use_own = lax.dynamic_slice_in_dim(in_use, at.x * rows_own, rows_own, 0)
    gain_rows = norm_gains.astype(jnp.float32)
    inputs = tokens.astype(jnp.float32)
    scale_one = lax.rsqrt(jnp.mean(inputs * inputs, 1, keepdims=True) + EPSILON)
    normed_own = (inputs * scale_one * gain_rows[0]).astype(jnp.bfloat16)
    normed_other = at.other_x(normed_own)
    grad_mixed = cotangent.astype(jnp.float32) * in_use_own[:, None]
    grad_low_own = grad_mixed.astype(jnp.bfloat16)
    packed = side_by_side(w_query, key_weight, value_weight, w_out)
    others = range(1, at.rows)
    projections = {(0, 0, 0): packed}
    projections[2, 0, 0] = at.across_z(packed, 2)
    projections[1, 0, 0] = at.across_z(packed, 1)
    for j in others:
        projections[0, j, 0] = at.along_y(packed, j)

    stage = [*list(projections.values())[1:], normed_other]
    projections[3, 0, 0] = at.across_z(after(projections[2, 0, 0], *stage), 1)
    for j in others:
        projections[1, j, 0] = at.along_y(after(projections[1, 0, 0], *stage), j)
    grads_low = {(0, 0): grad_low_own, (0, 1): at.other_x(after(grad_low_own, *stage))}
    shares = {}
    for mask in range(at.planes):
        start = (at.z ^ mask) * quarter
        shares[mask] = jnp.stack(
            [lax.dynamic_slice_in_dim(w, start, quarter, 1) for w in (w_gate, w_up, w_down)]
        )
    plane_two = [at.across_z(after(shares[2][:1], *stage), 2)]
    second = [plane_two[0], *(projections[1, j, 0] for j in others)]
    for j in others:
        projections[2, j, 0] = at.along_y(after(projections[2, 0, 0], *second), j)
    plane_two.append(at.across_z(after(shares[2][1:2], *second), 2))
    for mask in (0, 1):
        for j in range(at.rows):
            key = (mask, j, 0)
            if key in projections:
                projections[mask, j, 1] = at.other_core(after(projections[key], *stage))

    middle = grad_low_own.shape[1] // 2
    stage = [projections[3, 0, 0], grads_low[0, 1], plane_two[1]]
    stage += [projections[2, j, 0] for j in others]
    plane_two.append(at.across_z(after(shares[2][2:], *stage), 2))
    grads_low[1, 0] = at.across_z(after(grad_low_own, *stage), 1)
    for j in others:
        projections[3, j, 0] = at.along_y(after(projections[3, 0, 0], *stage), j)
    for mask, j in ((1, 1), (2, 0), (2, 1), (3, 0)):
        for back in others if j else (0,):
            if (mask, back, 1) not in projections:
                block = after(projections[mask, back, 0], *stage)
                projections[mask, back, 1] = at.other_core(block)

    stage = [projections[3, j, 0] for j in others] + [plane_two[2], grads_low[1, 0]]
    plane_two = jnp.concatenate(plane_two, 0)
    low_first = at.across_z(after(grad_low_own[:, :middle], *stage), 2)
    for j in others:
        projections[3, j, 1] = at.other_core(projections[3, j, 0])
    tables = [jnp.concatenate([table, table], 1) for table in rope_tables(position, HEAD_WIDTH)]
    keys_of = [segment[:, None], segment[None, :], *tables]

    weights = {}

    def to_chips(mask, parts, *earlier):
        weights.setdefault((mask, 0, 0), []).extend(parts)
        for j in range(1, at.rows):
            sent = [at.along_y(after(part, *earlier), j) for part in parts]
            weights.setdefault((mask, j, 0), []).extend(sent)
            earlier = tuple(sent)
        return earlier

    plane_three = at.across_z(after(shares[3][:2], *stage), 3)
    plane_one = at.across_z(after(shares[1][:2], *stage), 1)
    grads_low[1, 1] = at.other_x(after(grads_low[1, 0], *stage))
    last = to_chips(0, [shares[0]], *stage)

    low = jnp.bfloat16
    query_key, value, attended, branch_own, branch_other = attention_call(
        at,
        attention_kernel,
        width_kv,
        [normed_own, normed_other, *keys_of],
        projections,
        [
            ((row_count, width_query + width_kv), low),
            ((row_count, width_kv), low),
            ((row_count, width_query), low),
            ((rows_own, inputs.shape[1]), jnp.float32),
            ((rows_own, inputs.shape[1]), low),
        ],
    )
    branch_other = after(
        branch_other, plane_one, plane_three, low_first, grads_low[1, 1], *last
    )
    branch = branch_other
    state = inputs + branch_own + at.other_x(branch_other)
    scale_two = lax.rsqrt(jnp.mean(state * state, 1, keepdims=True) + EPSILON)
    normed_two = (state * scale_two * gain_rows[1]).astype(jnp.bfloat16)

    plane_three_last = at.across_z(after(shares[3][2:], branch), 3)
    plane_one_last = at.across_z(after(shares[1][2:], branch), 1)
    low_second = at.across_z(after(grad_low_own[:, middle:], branch), 2)
    last = to_chips(2, [plane_two], *last, branch)

    def to_cores(mask, backs, part, *earlier):
        for back in backs:
            block = after(weights[mask, back, 0][part], *earlier)
            weights.setdefault((mask, back, 1), []).append(at.other_core(block))

    to_cores(0, range(at.rows), 0, branch)
    stage = [normed_two, plane_three_last, plane_one_last, low_second]
    grads_low[2, 0] = jnp.concatenate([low_first, low_second], 1)
    normed = {(0, 0): normed_two, (0, 1): at.other_x(after(normed_two, *stage))}
    normed[2, 0] = at.across_z(after(normed_two, *stage), 2)
    normed[1, 0] = at.across_z(after(normed_two, *stage), 1)
    to_cores(2, (0,), 0, *stage)
    last = to_chips(1, [plane_one], *last, *stage)
    to_cores(1, (0,), 0, *stage)
    last = to_chips(3, [plane_three], *last)
    to_cores(3, (0,), 0, *stage)

    grads_low[2, 1] = at.other_x(after(grads_low[2, 0], normed[0, 1], *stage))

    stage = [*normed.values(), *last, grads_low[2, 1]]
    normed[3, 0] = at.across_z(after(normed[2, 0], *stage), 1)
    normed[2, 1] = at.other_x(after(normed[2, 0], *stage))
    for mask in (2, 1, 3):
        to_cores(mask, others, 0, *stage)
    last = to_chips(1, [plane_one_last], *stage) + to_chips(3, [plane_three_last], *stage)
    for mask in (1, 3):
        to_cores(mask, (0,), 1, *stage)

    stage = [normed[3, 0], normed[2, 1], *last]
    grads_low[3, 0] = at.across_z(after(grads_low[2, 0], *stage), 1)
    normed[3, 1] = at.other_x(after(normed[3, 0], *stage))
    normed[1, 1] = at.across_z(after(normed[0, 1], *stage), 1)
    for mask in (1, 3):
        to_cores(mask, others, 1, *stage)
    grads_low[3, 1] = at.other_x(after(grads_low[3, 0], normed[3, 1]))

    masks = (3, 2, 1, 0)
    normed_rows = [normed[mask, x] for mask in masks for x in range(2)]
    grad_rows = [grads_low[mask, x] for mask in masks for x in range(2)]
    hidden, silu, slope, *outs = forward(at, weights, normed_rows)
    def block_of(value, i):
        return value[i * rows_own : (i + 1) * rows_own]

    def out_block(mine, arrived, i):
        return block_of(mine, i).astype(jnp.float32) + arrived

    def of_chip(own, arrived, j):
        y = (at.y + j) % at.rows
        mine = lax.dynamic_index_in_dim(own, y, 0, keepdims=False)
        theirs = lax.dynamic_index_in_dim(arrived, y, 0, keepdims=False)
        return mine.astype(jnp.float32) + theirs

    def for_chips(own, arrived):
        return [of_chip(own, arrived, j).astype(jnp.bfloat16) for j in range(1, at.rows)]

    def send_chips(away, earlier):
        return [at.along_y(after(a, *earlier), j + 1) for j, a in enumerate(away)]

    def of_plane(terms, mask):
        own, arrived, chips = terms
        size = (1, 1) + own.shape[2:]
        at_plane = (at.y, at.z ^ mask, 0, 0)
        total = lax.dynamic_slice(own, at_plane, size)[0, 0].astype(jnp.float32)
        total = total + lax.dynamic_slice(arrived, at_plane, size)[0, 0]
        for part in chips:
            total = total + lax.dynamic_index_in_dim(part, at.z ^ mask, 0, keepdims=False)
        return total

    def send_planes(terms, wanted, earlier):
        sent = {}
        for mask in wanted:
            piece = of_plane(terms, mask).astype(jnp.bfloat16)
            sent[mask] = at.across_z(after(piece, *earlier), mask)
        return sent

    def all_columns(terms, pieces, *earlier):
        result = jnp.zeros((own_features, at.planes * quarter), jnp.float32)
        own = {0: of_plane(terms, 0)}
        for mask, piece in after({**own, **pieces}, *earlier).items():
            result = lax.dynamic_update_slice(
                result, piece.astype(jnp.float32), (0, (at.z ^ mask) * quarter)
            )
        return result

    out_first = at.other_x(outs[1])
    down_own, down_other = weight_grad(at, grad_rows, hidden, own_features)
    down_arrived = at.other_core(down_other)
    down_away = for_chips(down_own, down_arrived)
    grad_gate_in, grad_up_in, *back = backward(
        at, weights, grad_rows, after(silu, *down_away), slope
    )
    down_terms = (down_own, down_arrived, send_chips(down_away, ()))

    def sum_of(i, arrived):
        return back[2 * i].astype(jnp.float32) + arrived

    stage = [out_first, back[0], *down_terms[2]]
    three = at.other_x(after(back[1], *stage))
    one = at.across_z(after(back[5], *stage), 1)
    gate_own, gate_other = weight_grad(
        at, normed_rows, after(grad_gate_in, *stage), own_features
    )

    stage = [three, one, gate_own]
    to_two = at.across_z(after(sum_of(0, three).astype(jnp.bfloat16), *stage), 1)
    two = at.other_x(after(back[3], *stage))
    gate_arrived = at.other_core(after(gate_other, *stage))
    up_own, up_other = weight_grad(at, normed_rows, after(grad_up_in, *stage), own_features)

    stage = [to_two, two, gate_arrived, up_own]
    for_zero = (sum_of(1, two) + to_two).astype(jnp.bfloat16)
    to_zero = at.across_z(after(for_zero, *stage), 2)
    other_zero = (back[7].astype(jnp.float32) + one).astype(jnp.bfloat16)
    zero = at.other_x(after(other_zero, *stage))
    from_one = at.across_z(after(back[4], *stage), 1)
    gate_chips = send_chips(for_chips(gate_own, gate_arrived), stage)
    up_arrived = at.other_core(after(up_other, *stage))

    grad_normed_two = sum_of(3, zero) + from_one + to_zero
    hat_two = state * scale_two
    inner_two = grad_normed_two * gain_rows[1]
    grad_state = grad_mixed + scale_two * (
        inner_two - hat_two * jnp.mean(inner_two * hat_two, 1, keepdims=True)
    )
    gain_two = jnp.sum(grad_normed_two * hat_two, 0)
    grad_state_own = grad_state.astype(jnp.bfloat16)

    grad_state_other = at.other_x(grad_state_own)
    stage = [grad_state_own, *gate_chips]
    gate_terms = (gate_own, gate_arrived, gate_chips)

    def both(mask, *pair):
        return jnp.stack([of_plane(terms, mask).astype(jnp.bfloat16) for terms in pair])

    down_pieces = send_planes(down_terms, (2,), stage)
    first_one = out_block(outs[0], block_of(out_first, 2), 2).astype(jnp.bfloat16)
    first_one = at.across_z(after(first_one, *stage), 1)
    late = [*stage, grad_state_other, down_pieces[2], first_one]
    gate_pieces = send_planes(gate_terms, (2, 3), late)
    gate_down = at.across_z(after(both(1, gate_terms, down_terms), *late), 1)
    up_chips = send_chips(for_chips(up_own, up_arrived), stage)
    up_terms = (up_own, up_arrived, up_chips)

    out_second = at.other_x(after(outs[3], grad_state_other))
    shape = (at.chips, own_features, width_query + width_kv)
    back_own, back_other, qk_own, qk_other, vo_own, vo_other = attention_call(
        at,
        attention_back_kernel,
        width_kv,
        [
            grad_state_own,
            grad_state_other,
            normed_own,
            normed_other,
            *keys_of,
            after(query_key, *late),
            value,
            attended,
        ],
        projections,
        [
            ((rows_own, inputs.shape[1]), jnp.float32),
            ((rows_own, inputs.shape[1]), low),
            *[(shape, low)] * 4,
        ],
    )
    stage = [qk_other, out_second, *up_chips, *gate_pieces.values(), gate_down]
    gate_pieces[1], down_pieces[1] = gate_down[0], gate_down[1]
    out_blocks = [
        jnp.concatenate(
            [
                out_block(outs[2 * n], block_of(arrived, i), i)
                for n, arrived in enumerate((out_first, out_second))
            ],
            1,
        )
        for i in range(4)
    ]

    owns = {"qk": qk_own, "vo": vo_own}
    cores = {
        "qk": at.other_core(after(qk_other, *stage)),
        "vo": at.other_core(after(vo_other, *stage)),
    }

    def by_place(value):
        return value.reshape(at.planes, at.rows, own_features, -1)

    def for_chip(name, j):
        y = (at.y + j) % at.rows
        parts = [
            lax.dynamic_index_in_dim(by_place(value), y, 1, keepdims=False)
            for value in (owns[name], cores[name])
        ]
        return (parts[0].astype(jnp.float32) + parts[1]).astype(jnp.bfloat16)

    chips = {"qk": [], "vo": []}

    def to_chips_of(name, earlier):
        for j in others:
            chips[name].append(at.along_y(after(for_chip(name, j), *earlier), j))

    def for_plane(name, mask):
        z = at.z ^ mask
        total = 0.0
        for value in (owns[name], cores[name]):
            part = lax.dynamic_slice(by_place(value), (z, at.y, 0, 0), (1, 1) + by_place(value).shape[2:])
            total = total + part[0, 0].astype(jnp.float32)
        for part in chips[name]:
            total = total + lax.dynamic_index_in_dim(part, z, 0, keepdims=False)
        return total

    pairs, quarters = {}, {}

    def to_pair(name, earlier):
        both_planes = jnp.stack([for_plane(name, 1), for_plane(name, 3)]).astype(jnp.bfloat16)
        pairs[name] = at.across_z(after(both_planes, *earlier), 1)

    def to_quarter(name, earlier):
        far = (for_plane(name, 2) + pairs[name][1]).astype(jnp.bfloat16)
        quarters[name] = at.across_z(after(far, *earlier), 2)

    def total_of(name):
        return for_plane(name, 0) + pairs[name][0] + quarters[name]

    up_pieces = send_planes(up_terms, (2,), stage)
    up_down = at.across_z(after(both(3, up_terms, down_terms), *stage), 3)
    up_pieces[3], down_pieces[3] = up_down[0], up_down[1]
    out_two = at.across_z(after(out_blocks[0].astype(jnp.bfloat16), *stage), 1)
    to_chips_of("qk", ())

    middle = out_blocks[2].shape[1] // 2
    second_one = at.across_z(after(out_blocks[2][:, middle:].astype(jnp.bfloat16), *stage), 1)
    out_one = jnp.concatenate([first_one, second_one], 1)

    stage = [*chips["qk"], up_pieces[2], up_down, out_two, second_one]
    normed_arrived = at.other_x(after(back_other, *stage))
    to_chips_of("vo", stage)
    to_pair("qk", stage)
    up_pieces.update(send_planes(up_terms, (1,), stage))
    out_zero = (out_blocks[1] + out_two).astype(jnp.bfloat16)
    out_zero = at.across_z(after(out_zero, *stage), 2)

    stage = [*chips["vo"], pairs["qk"], out_zero, normed_arrived, up_pieces[1]]
    to_pair("vo", stage)
    to_quarter("qk", stage)
    grad_normed_one = back_own + after(normed_arrived, *stage)
    hat_one = inputs * scale_one
    inner_one = grad_normed_one * gain_rows[0]
    grad_tokens = (
        grad_state
        + scale_one * (inner_one - hat_one * jnp.mean(inner_one * hat_one, 1, keepdims=True))
    ).astype(jnp.bfloat16)
    gain_one = jnp.sum(grad_normed_one * hat_one, 0)
    grad_gains = jnp.stack([gain_one, gain_two])
    grad_gains = grad_gains + at.other_x(grad_gains)
    bits = [1 << i for i in range(at.dp.bit_length() - 1)]
    for bit in bits:
        if bit < CORES * at.rows:
            grad_gains = grad_gains + at.move(grad_gains, lambda d: d ^ bit)

    stage = [pairs["vo"], quarters["qk"], grad_gains]
    to_quarter("vo", stage)
    for bit in bits:
        if bit >= CORES * at.rows:
            grad_gains = grad_gains + at.move(after(grad_gains, *stage), lambda d: d ^ bit)
    grad_gate = all_columns(gate_terms, gate_pieces, *stage)
    grad_up = all_columns(up_terms, up_pieces, *stage)
    grad_down = all_columns(down_terms, down_pieces, *stage)
    sum_qk, sum_vo = total_of("qk"), total_of("vo")
    grad_gate = all_columns(gate_terms, gate_pieces, *stage)
    grad_up = all_columns(up_terms, up_pieces, *stage)
    grad_down = all_columns(down_terms, down_pieces, *stage)
    ffn_out = out_blocks[3] + out_zero + out_one
    mixed = ((state + ffn_out) * in_use_own[:, None]).astype(jnp.bfloat16)
    return (
        mixed,
        grad_tokens,
        grad_gains,
        sum_qk[:, :width_query],
        sum_qk[:, width_query:],
        sum_vo[:, :width_kv],
        sum_vo[:, width_kv:],
        grad_gate,
        grad_up,
        grad_down,
    )


def solution(mesh):
    in_specs = (
        P(("dp", "tensor"), None),
        P("dp", None),
        P(),
        P("dp", "tensor"),
        P("dp", "tensor"),
        P("dp", "tensor"),
        P("dp", "tensor"),
        P("dp", "tensor"),
        P("dp", "tensor"),
        P("dp", "tensor"),
        P(("dp", "tensor"), None),
    )
    out_specs = (
        P(("dp", "tensor"), None),
        P(("dp", "tensor"), None),
        P(),
        P("dp", "tensor"),
        P("dp", "tensor"),
        P("dp", "tensor"),
        P("dp", "tensor"),
        P("dp", "tensor"),
        P("dp", "tensor"),
        P("dp", "tensor"),
    )
    return jax.shard_map(
        on_device, mesh=mesh, in_specs=in_specs, out_specs=out_specs, check_vma=False
    )
```
